32 devices in a mesh: section: 4 (over y, x), seq: 8 (over z, core).
Axes of the slice: x: 2, y: 2, z: 4, core: 2. Of those that a mesh axis runs over, the one named last changes fastest.
Arguments:
- grad_out: bfloat16 [4, 1024, 8192], P('section', 'seq'), may hold values from -7.5 to 7.5
- queries: bfloat16 [4, 1024, 8192], P('section', 'seq'), may hold values from -2.5 to 2.5
- mem_out: bfloat16 [4, 1024, 8192], P('section', 'seq'), may hold values from -6 to 6
- row_total: bfloat16 [4, 1024, 64], P('section', 'seq'), may hold values from 8192 to 32768
- gate_logit: float32 [4, 64], P('section'), may hold values from -2 to 2
- mem_keys: bfloat16 [4, 8192, 1024], P('section', 'seq'), may hold values from -3.5 to 3.5
- mem_values: bfloat16 [4, 8192, 1024], P('section', 'seq'), may hold values from -7.5 to 7.5
- retrieved: int32 [4, 8, 8, 32], P('section'), may hold values from 0 to 63, all different within a row
Outputs:
- onward: bfloat16 [4, 1024, 8192], P('section', 'seq')
The draws below stay inside these ranges and needn't reach their ends.
Inputs may be any that keep to these rules, and one draw needn't show every extreme that they name: `retrieved`: 32 different memory blocks for each section, key head and query block; every memory block is named somewhere, some far more often than others.
All inputs are finite; a program needn't handle non-finite values.
Results may differ from the reference program's by a relative error of at most 0.0054.
Values may be sent and summed in bfloat16 or wider, within the bound.
No kernel may reach another device: no remote copies, remote signals or barrier semaphores. Data moves between devices by JAX's collectives and lax.ppermute only.
A program may use at most 128 MiB of HBM per device.

```python
import math
import jax
import jax.numpy as jnp
from jax import lax

HEADS = 64
KV_HEADS = 8
HEAD_DIM = 128
TOPK = 32
BLOCK = 128
SECTIONS = 4
TOKENS = 1024
MEM = 8192
QBLOCKS = 8
MBLOCKS = 64
WIDTH = 8192
KV_WIDTH = 1024


def steps_of(rng, shape, split, smallest, largest):
    def one(axis_at, parts):
        steps = jax.random.uniform(jax.random.fold_in(jax.random.fold_in(rng, 6), axis_at), (parts,), jnp.float32, smallest / len(split), largest / len(split))
        return jnp.repeat(jnp.exp(steps), shape[axis_at] // parts).reshape((-1,) + (1,) * (len(shape) - axis_at - 1))

    loudness = one(*split[0])
    for cut in split[1:]:
        loudness = loudness * one(*cut)
    return loudness


def different_ones(stream_key, rows, number_of, top, lift):
    order = jax.random.permutation(jax.random.fold_in(stream_key, 1), number_of)
    boost = order
    for power in range(3):
        boost = boost * boost // number_of
    boost = boost * lift // number_of
    lots = jax.random.randint(jax.random.fold_in(stream_key, 2), (rows, number_of), 0, 4096) + boost
    sure = jax.random.permutation(jax.random.fold_in(stream_key, 3), rows)[jnp.arange(number_of) % rows]
    lots = jnp.where(jnp.arange(rows)[:, None] == sure[None, :], 1 << 14, lots)
    priority = lots * number_of + jnp.arange(number_of)
    return lax.top_k(priority.astype(jnp.int32), top)[1].astype(jnp.int32)


def scatter_about(own_key, dims, scale, reach, shards=(), dtype=jnp.bfloat16):
    values = scale * jax.random.normal(own_key, dims, jnp.float32)
    if shards:
        values = values * steps_of(own_key, dims, shards, -0.22, 0.18)
    return jnp.clip(values, -reach, reach).astype(dtype)


def setup_inputs(seed: int = 0) -> dict:
    keys = jax.random.split(jax.random.key(seed), 9)
    return {
        "grad_out": scatter_about(keys[0], (SECTIONS, TOKENS, WIDTH), 3.0, 7.5, ((0, 4), (1, 8))),
        "queries": scatter_about(keys[1], (SECTIONS, TOKENS, WIDTH), 1.0, 2.5, ((0, 4), (1, 8))),
        "mem_out": scatter_about(keys[2], (SECTIONS, TOKENS, WIDTH), 1.0, 6.0, ((0, 4), (1, 8))),
        "row_total": jnp.clip(jnp.exp(math.log(32768.0) - 1.3862944 * jax.random.uniform(keys[3], (SECTIONS, TOKENS, HEADS), jnp.float32) ** steps_of(keys[3], (SECTIONS, TOKENS, HEADS), ((0, 4), (1, 8)), -0.2, 0.2)), 8192.0, 32768.0).astype(jnp.bfloat16),
        "gate_logit": jnp.clip(jax.random.uniform(keys[4], (SECTIONS, HEADS), jnp.float32, -2.0, 2.0) * steps_of(keys[4], (SECTIONS, HEADS), ((0, 4),), -0.4, 0.0), -2.0, 2.0),
        "mem_keys": scatter_about(keys[5], (SECTIONS, MEM, KV_WIDTH), 1.4, 3.5, ((0, 4), (1, 8))),
        "mem_values": scatter_about(keys[6], (SECTIONS, MEM, KV_WIDTH), 3.0, 7.5, ((0, 4), (1, 8))),
        "retrieved": different_ones(keys[7], SECTIONS * KV_HEADS * QBLOCKS, MBLOCKS, TOPK, 8192).reshape((SECTIONS, KV_HEADS, QBLOCKS, TOPK)),
    }


def reference(grad_out, queries, mem_out, row_total, gate_logit, mem_keys, mem_values, retrieved):
    group_size = HEADS // KV_HEADS
    score_scale = HEAD_DIM ** -0.5

    def one_section(pieces):
        grad_section, query_section, out_section, sum_section, logit_section, keys_section, values_section, chosen = pieces
        gate_values = jax.nn.sigmoid(logit_section.astype(jnp.float32))
        grad_mem = (gate_values[None, :, None] * grad_section.reshape(TOKENS, HEADS, HEAD_DIM).astype(jnp.float32)).astype(jnp.bfloat16)
        row_delta = jnp.sum(grad_mem.astype(jnp.float32) * out_section.reshape(TOKENS, HEADS, HEAD_DIM).astype(jnp.float32), axis=-1)
        key_blocks = keys_section.reshape(MBLOCKS, BLOCK, KV_HEADS, HEAD_DIM).transpose(2, 0, 1, 3)
        value_blocks = values_section.reshape(MBLOCKS, BLOCK, KV_HEADS, HEAD_DIM).transpose(2, 0, 1, 3)

        def one_block(items):
            query_tile, grad_tile, delta_tile, sum_tile, picks = items
            tile_keys = jax.vmap(lambda table, rows_of: table[rows_of].reshape(TOPK * BLOCK, HEAD_DIM))(key_blocks, picks)
            tile_values = jax.vmap(lambda table, rows_of: table[rows_of].reshape(TOPK * BLOCK, HEAD_DIM))(value_blocks, picks)
            query_four = query_tile.reshape(BLOCK, KV_HEADS, group_size, HEAD_DIM).astype(jnp.float32)
            grad_four = grad_tile.reshape(BLOCK, KV_HEADS, group_size, HEAD_DIM).astype(jnp.float32)
            scores = jnp.einsum("qkgd,kjd->qkgj", query_four, tile_keys.astype(jnp.float32)) * score_scale
            probs = jnp.exp(scores - jnp.log(sum_tile.reshape(BLOCK, KV_HEADS, group_size).astype(jnp.float32))[..., None])
            grad_probs = jnp.einsum("qkgd,kjd->qkgj", grad_four, tile_values.astype(jnp.float32))
            grad_scores = (probs * (grad_probs - delta_tile.reshape(BLOCK, KV_HEADS, group_size)[..., None]) * score_scale).astype(jnp.bfloat16)
            result = jnp.einsum("qkgj,kjd->qkgd", grad_scores.astype(jnp.float32), tile_keys.astype(jnp.float32))
            return result.astype(jnp.bfloat16).reshape(BLOCK, WIDTH)

        blocks_in = (
            query_section.reshape(QBLOCKS, BLOCK, HEADS, HEAD_DIM),
            grad_mem.reshape(QBLOCKS, BLOCK, HEADS, HEAD_DIM),
            row_delta.reshape(QBLOCKS, BLOCK, HEADS),
            sum_section.reshape(QBLOCKS, BLOCK, HEADS),
            chosen.transpose(1, 0, 2),
        )
        return lax.map(one_block, blocks_in).reshape(TOKENS, WIDTH)

    grads = lax.map(one_section, (grad_out, queries, mem_out, row_total, gate_logit, mem_keys, mem_values, retrieved))
    return jnp.roll(grads, -1, axis=0)
```

```python
import functools
import math

import jax
import jax.numpy as jnp
from jax import lax
from jax.experimental import pallas as pl
from jax.experimental.pallas import tpu as pltpu
from jax.sharding import PartitionSpec as P

BLOCK = 128
PARTS = 3
VMEM_LIMIT = 48 * 1024 * 1024

NT = (((1,), (1,)), ((), ()))
NN = (((1,), (0,)), ((), ()))


def split_parts(value):
    terms = []
    for _ in range(PARTS):
        term = value.astype(jnp.bfloat16)
        terms.append(term)
        value = value - term.astype(jnp.float32)
    return terms


def prepare_kernel(heads, dim, gate_ref, grad_ref, query_ref, out_ref, log_ref, packed_ref):
    rows = grad_ref.shape[0]
    first = pl.program_id(0) * heads
    deltas = []
    for h in range(heads):
        columns = slice(h * dim, (h + 1) * dim)
        gated = (gate_ref[first + h] * grad_ref[:, columns].astype(jnp.float32)).astype(jnp.bfloat16)
        packed_ref[0, h * rows:(h + 1) * rows, :] = query_ref[:, columns]
        packed_ref[0, (heads + h) * rows:(heads + h + 1) * rows, :] = gated
        product = gated.astype(jnp.float32) * out_ref[:, columns].astype(jnp.float32)
        deltas.append(jnp.sum(product.T, axis=0, keepdims=True))
    stats = jnp.concatenate(deltas + [log_ref[...]], axis=0)
    base = 2 * heads * rows
    for part, term in enumerate(split_parts(stats)):
        packed_ref[0, base + part * 2 * heads:base + (part + 1) * 2 * heads, :] = term


def prepare(grad_out, queries, mem_out, logs, gates, kv_heads, dim):
    rows, width = grad_out.shape
    heads = width // dim // kv_heads
    span = 2 * heads * rows + PARTS * 2 * heads
    wide = pl.BlockSpec((rows, heads * dim), lambda k, _: (0, k))
    return pl.pallas_call(
        functools.partial(prepare_kernel, heads, dim),
        out_shape=jax.ShapeDtypeStruct((kv_heads, span, dim), jnp.bfloat16),
        grid_spec=pltpu.PrefetchScalarGridSpec(
            num_scalar_prefetch=1,
            grid=(kv_heads,),
            in_specs=[wide, wide, wide, pl.BlockSpec((heads, rows), lambda k, _: (k, 0))],
            out_specs=pl.BlockSpec((1, span, dim), lambda k, _: (k, 0, 0)),
        ),
        compiler_params=pltpu.CompilerParams(vmem_limit_bytes=VMEM_LIMIT),
        cost_estimate=pl.CostEstimate(flops=rows * width * 4, bytes_accessed=rows * width * 12, transcendentals=0),
    )(gates, grad_out, queries, mem_out, logs)


def attend_kernel(heads, rows, dim, scale, fresh, last, places, *refs):
    count = len(places)
    picks_ref, starts_ref = refs[:2]
    packed_ref = refs[2]
    memory_refs = refs[3:3 + count]
    rest = refs[3 + count:]
    acc_in = None if fresh else rest[0]
    out_ref = rest[0] if fresh else rest[1]
    turned, total = rest[-2:]
    tile = pl.program_id(0)
    blocks = memory_refs[0].shape[1] // BLOCK
    pair = 2 * rows

    @pl.when(tile == 0)
    def _():
        for at, memory in enumerate(memory_refs):
            for block in range(blocks):
                turned[at, block] = memory[0, block * BLOCK:(block + 1) * BLOCK, :].T

    if fresh:
        total[...] = jnp.zeros_like(total)
    else:
        total[...] = acc_in[0]

    base = 2 * heads * rows
    stats = sum(
        packed_ref[0, base + part * 2 * heads:base + (part + 1) * 2 * heads, :].astype(jnp.float32)
        for part in range(PARTS)
    )
    exponent = scale * math.log2(math.e)

    for at, (place, memory) in enumerate(zip(places, memory_refs)):
        low = starts_ref[tile, place]
        high = starts_ref[tile, place + 1]

        def step(turn, carry):
            here = low + 2 * turn
            second = here + 1 < high
            one = picks_ref[tile, here]
            two = picks_ref[tile, jnp.where(second, here + 1, here)]
            row_one = pl.ds(pl.multiple_of(one * BLOCK, BLOCK), BLOCK)
            row_two = pl.ds(pl.multiple_of(two * BLOCK, BLOCK), BLOCK)
            keys = jnp.concatenate([memory[0, row_one, :], memory[0, row_two, :]], axis=0)
            values = jnp.concatenate([memory[1, row_one, :], memory[1, row_two, :]], axis=0)
            later = turned[at, two]
            later = jnp.where(second, later, jnp.zeros_like(later))
            across = jnp.concatenate([turned[at, one], later], axis=1)
            for p in range(heads // 2):
                span = slice(p * pair, (p + 1) * pair)
                grads = slice(heads * rows + p * pair, heads * rows + (p + 1) * pair)
                scores = lax.dot_general(keys, packed_ref[0, span, :], NT, preferred_element_type=jnp.float32)
                grad_probs = lax.dot_general(values, packed_ref[0, grads, :], NT, preferred_element_type=jnp.float32)
                log_row = jnp.concatenate([stats[heads + 2 * p:heads + 2 * p + 1], stats[heads + 2 * p + 1:heads + 2 * p + 2]], axis=1)
                delta_row = jnp.concatenate([stats[2 * p:2 * p + 1], stats[2 * p + 1:2 * p + 2]], axis=1)
                probs = jnp.exp2(scores * exponent - log_row)
                grad_scores = (probs * (grad_probs - delta_row)).astype(jnp.bfloat16)
                total[:, span] += lax.dot_general(across, grad_scores, NN, preferred_element_type=jnp.float32)
            return carry

        lax.fori_loop(0, (high - low + 1) // 2, step, 0)

    if last:
        for h in range(heads):
            out_ref[0, :, h * dim:(h + 1) * dim] = total[:, h * rows:(h + 1) * rows].T.astype(jnp.bfloat16)
    else:
        out_ref[0] = total[...]


def attend(packed, memories, places, acc, picks, starts, heads, rows, dim, scale, last):
    tiles, span, _ = packed.shape
    fresh = acc is None
    count = len(places)
    blocks = memories[0].shape[1] // BLOCK
    width = heads * rows
    acc_spec = pl.BlockSpec((1, dim, width), lambda t, *_: (t, 0, 0))
    if last:
        out_shape = jax.ShapeDtypeStruct((tiles, rows, heads * dim), jnp.bfloat16)
        out_spec = pl.BlockSpec((1, rows, heads * dim), lambda t, *_: (t, 0, 0))
    else:
        out_shape = jax.ShapeDtypeStruct((tiles, dim, width), jnp.float32)
        out_spec = acc_spec
    flops = tiles * count * (blocks // 2) * BLOCK * width * dim * 6
    return pl.pallas_call(
        functools.partial(attend_kernel, heads, rows, dim, scale, fresh, last, places),
        out_shape=out_shape,
        grid_spec=pltpu.PrefetchScalarGridSpec(
            num_scalar_prefetch=2,
            grid=(tiles,),
            in_specs=[pl.BlockSpec((1, span, dim), lambda t, *_: (t, 0, 0))]
            + [pl.BlockSpec(m.shape, lambda t, *_: (0, 0, 0)) for m in memories]
            + ([] if fresh else [acc_spec]),
            out_specs=out_spec,
            scratch_shapes=[
                pltpu.VMEM((count, blocks, dim, BLOCK), jnp.bfloat16),
                pltpu.VMEM((dim, width), jnp.float32),
            ],
        ),
        compiler_params=pltpu.CompilerParams(vmem_limit_bytes=VMEM_LIMIT),
        cost_estimate=pl.CostEstimate(
            flops=flops * 2, bytes_accessed=tiles * span * dim * 2 + tiles * width * dim * 8, transcendentals=0
        ),
    )(picks, starts, packed, *memories, *([] if fresh else [acc]))


def shards(grad_out, queries, mem_out, row_total, gate_logit, mem_keys, mem_values, retrieved):
    seq = lax.axis_size("seq")
    sections = lax.axis_size("section")
    position = lax.axis_index("seq")
    rows, width = grad_out.shape[1:]
    head_count = gate_logit.shape[1]
    dim = width // head_count
    kv_heads = mem_keys.shape[2] // dim
    heads = head_count // kv_heads
    mem_dev = mem_keys.shape[1]
    blocks = mem_dev // BLOCK
    group = min(kv_heads, seq // 2)
    own = kv_heads // group
    at = position % group
    scale = dim ** (-0.5)

    def swapped(value, step):
        return lax.ppermute(value, "seq", [(p, p ^ step) for p in range(seq)])

    memory = jnp.stack([mem_keys[0], mem_values[0]]).reshape(2, mem_dev, kv_heads, dim).transpose(2, 0, 1, 3)

    logs = jnp.log2(row_total[0].T.astype(jnp.float32)) - math.log2(scale)
    gates = jax.nn.sigmoid(gate_logit[0])
    packed = prepare(grad_out[0], queries[0], mem_out[0], logs, gates, kv_heads, dim)
    packed = packed.reshape(group, own, *packed.shape[1:])

    tile_of = (position // group) * group + jnp.arange(group)
    mine = lax.dynamic_slice_in_dim(retrieved[0], at * own, own, 0)
    mine = lax.dynamic_slice_in_dim(mine, (position // group) * group, group, 1)
    distance = ((mine // blocks) ^ position) * blocks + mine % blocks
    rank = jnp.sum(distance[..., None, :] < distance[..., :, None], axis=-1)
    order = jnp.arange(distance.shape[-1])
    ordered = jnp.sum(jnp.where(rank[..., :, None] == order, distance[..., :, None], 0), axis=-2)
    picks = (ordered % blocks).astype(jnp.int32)
    starts = jnp.sum(distance[..., None, :] < (jnp.arange(seq + 1) * blocks)[:, None], axis=-1).astype(jnp.int32)

    stages = [tuple(range(group))]
    half = group + (seq - group) // 2
    stages.append(tuple(range(group, half)))
    stages.append(tuple(range(half, seq)))

    groups = [list(range(g * group, (g + 1) * group)) for g in range(seq // group)]
    out = jnp.zeros((rows, width), jnp.bfloat16)
    for i in range(own):
        sends = [
            lax.dynamic_index_in_dim(memory, (at ^ x) * own + i, 0, keepdims=False) for x in range(group)
        ]
        arrived = {0: sends[0]}
        for step in range(group, seq):
            arrived[step] = swapped(sends[step % group], step)
        mixed = lax.all_to_all(
            packed[:, i], "seq", split_axis=0, concat_axis=0, axis_index_groups=groups, tiled=True
        )
        for step in range(1, group):
            arrived[step] = swapped(sends[step], step)
        acc = None
        for number, places in enumerate(stages):
            acc = attend(
                mixed, [arrived[p] for p in places], places, acc, picks[i], starts[i],
                heads, rows, dim, scale, number == len(stages) - 1,
            )
        for x in range(group):
            piece = lax.dynamic_index_in_dim(acc, at ^ x, 0, keepdims=False)
            pairs = [
                (s * seq + p, ((s - 1) % sections) * seq + (p ^ x)) for s in range(sections) for p in range(seq)
            ]
            piece = lax.ppermute(piece, ("section", "seq"), pairs)
            out = lax.dynamic_update_slice_in_dim(out, piece, ((at ^ x) * own + i) * heads * dim, 1)
    return out[None]


def solution(mesh):
    return jax.shard_map(
        shards,
        mesh=mesh,
        in_specs=(
            P("section", "seq", None),
            P("section", "seq", None),
            P("section", "seq", None),
            P("section", "seq", None),
            P("section", None),
            P("section", "seq", None),
            P("section", "seq", None),
            P("section", None, None, None),
        ),
        out_specs=P("section", "seq", None),
        check_vma=False,
    )
```

```python
import functools
import math

import jax
import jax.numpy as jnp
from jax import lax
from jax.experimental import pallas as pl
from jax.experimental.pallas import tpu as pltpu
from jax.sharding import PartitionSpec as P

BLOCK = 128
PARTS = 3
STAT_ROWS = 16
VMEM_LIMIT = 48 * 1024 * 1024


def split_parts(value):
    terms = []
    for _ in range(PARTS):
        term = value.astype(jnp.bfloat16)
        terms.append(term)
        value = value - term.astype(jnp.float32)
    return terms


def pack_kernel(own, group, index, at_ref, keys_ref, values_ref, *refs):
    outs, sems = refs[:group], refs[group]
    dim = outs[0].shape[2]
    copies = []
    for x, out in enumerate(outs):
        column = pl.multiple_of(((at_ref[0] ^ x) * own + index) * dim, dim)
        for half, source in enumerate((keys_ref, values_ref)):
            copy = pltpu.make_async_copy(source.at[:, pl.ds(column, dim)], out.at[half], sems.at[2 * x + half])
            copy.start()
            copies.append(copy)
    for copy in copies:
        copy.wait()


def pack(mem_keys, mem_values, at, own, group, index, dim):
    mem_dev = mem_keys.shape[0]
    shape = jax.ShapeDtypeStruct((2, mem_dev, dim), mem_keys.dtype)
    anywhere = pl.BlockSpec(memory_space=pl.ANY)
    return pl.pallas_call(
        functools.partial(pack_kernel, own, group, index),
        out_shape=[shape] * group,
        grid_spec=pltpu.PrefetchScalarGridSpec(
            num_scalar_prefetch=1,
            in_specs=[anywhere, anywhere],
            out_specs=[anywhere] * group,
            scratch_shapes=[pltpu.SemaphoreType.DMA((2 * group,))],
        ),
        compiler_params=pltpu.CompilerParams(vmem_limit_bytes=VMEM_LIMIT),
        cost_estimate=pl.CostEstimate(flops=0, bytes_accessed=8 * group * mem_dev * dim, transcendentals=0),
    )(at[None], mem_keys, mem_values)


def prepare_kernel(heads, dim, own, index, gate_ref, grad_ref, query_ref, out_ref, log_ref, packed_ref):
    rows = grad_ref.shape[0]
    first = (pl.program_id(0) * own + index) * heads
    for h in range(heads):
        columns = slice(h * dim, (h + 1) * dim)
        place = slice(h * rows, (h + 1) * rows)
        packed_ref[0, :dim, place] = query_ref[:, columns].T
        gated = (gate_ref[first + h] * grad_ref[:, columns].T.astype(jnp.float32)).astype(jnp.bfloat16)
        packed_ref[0, dim:2 * dim, place] = gated
        product = gated.astype(jnp.float32) * out_ref[:, columns].T.astype(jnp.float32)
        delta = jnp.sum(product, axis=0, keepdims=True)
        terms = split_parts(delta) + split_parts(log_ref[h:h + 1, :])
        terms = [term.astype(jnp.float32) for term in terms]
        filler = jnp.zeros((STAT_ROWS - len(terms), rows), jnp.float32)
        packed_ref[0, 2 * dim:, place] = jnp.concatenate(terms + [filler], axis=0).astype(jnp.bfloat16)


def prepare(grad_out, queries, mem_out, logs, gates, kv_heads, dim, own, index):
    rows, width = grad_out.shape
    heads = width // dim // kv_heads
    group = kv_heads // own
    span = 2 * dim + STAT_ROWS
    wide = pl.BlockSpec((rows, heads * dim), lambda k, _: (0, k * own + index))
    return pl.pallas_call(
        functools.partial(prepare_kernel, heads, dim, own, index),
        out_shape=jax.ShapeDtypeStruct((group, span, heads * rows), jnp.bfloat16),
        grid_spec=pltpu.PrefetchScalarGridSpec(
            num_scalar_prefetch=1,
            grid=(group,),
            in_specs=[wide, wide, wide, pl.BlockSpec((heads, rows), lambda k, _: (k * own + index, 0))],
            out_specs=pl.BlockSpec((1, span, heads * rows), lambda k, _: (k, 0, 0)),
        ),
        compiler_params=pltpu.CompilerParams(vmem_limit_bytes=VMEM_LIMIT),
        cost_estimate=pl.CostEstimate(flops=rows * width * 4, bytes_accessed=rows * width * 12 // own, transcendentals=0),
    )(gates, grad_out, queries, mem_out, logs)


def attend_kernel(heads, rows, dim, scale, fresh, last, places, picks_ref, starts_ref, packed_ref, *refs):
    count = len(places)
    memory_refs = refs[:count]
    rest = refs[count:]
    acc_in = None if fresh else rest[0]
    out_ref = rest[0] if fresh else rest[1]
    keys_ref, values_ref, turned, total = rest[-4:]
    tile = pl.program_id(0)
    mem_dev = memory_refs[0].shape[1]
    blocks = mem_dev // BLOCK
    pair = 2 * rows

    @pl.when(tile == 0)
    def _():
        for at, memory in enumerate(memory_refs):
            here = slice(at * mem_dev, (at + 1) * mem_dev)
            keys_ref[here, :] = memory[0]
            values_ref[here, :] = memory[1]
            for block in range(blocks):
                turned[at * blocks + block] = memory[0, block * BLOCK:(block + 1) * BLOCK, :].T

    if fresh:
        total[...] = jnp.zeros_like(total)
    else:
        total[...] = acc_in[0]

    stats = packed_ref[0, 2 * dim:, :].astype(jnp.float32)
    delta_row = jnp.sum(stats[:PARTS], axis=0, keepdims=True)
    log_row = jnp.sum(stats[PARTS:2 * PARTS], axis=0, keepdims=True)

    low = starts_ref[tile, places[0]]
    high = starts_ref[tile, places[-1] + 1]
    offset = places[0] * blocks

    def add(here, number, checked):
        sides = []
        for two in range(0, number, 2):
            keys, values, across = [], [], []
            for j in (two, two + 1):
                valid = here + j < high
                block = picks_ref[tile, jnp.where(valid, here + j, here) if checked else here + j] - offset
                row = pl.ds(pl.multiple_of(block * BLOCK, BLOCK), BLOCK)
                keys.append(keys_ref[row, :])
                values.append(values_ref[row, :])
                side = turned[block]
                across.append(jnp.where(valid, side, jnp.zeros_like(side)) if checked and j else side)
            sides.append(
                (jnp.concatenate(keys, axis=0), jnp.concatenate(values, axis=0), jnp.concatenate(across, axis=1))
            )
        for p in range(heads // 2):
            span = slice(p * pair, (p + 1) * pair)
            query = packed_ref[0, :dim, span]
            grad = packed_ref[0, dim:2 * dim, span]
            gained = None
            for keys, values, across in sides:
                scores = jnp.dot(keys, query, preferred_element_type=jnp.float32)
                grad_probs = jnp.dot(values, grad, preferred_element_type=jnp.float32)
                probs = jnp.exp(scores * scale - log_row[:, span])
                grad_scores = (probs * (grad_probs - delta_row[:, span])).astype(jnp.bfloat16)
                part = jnp.dot(across, grad_scores, preferred_element_type=jnp.float32)
                gained = part if gained is None else gained + part
            total[:, span] += gained

    fours = (high - low) // 4

    def four(turn, carry):
        add(low + 4 * turn, 4, False)
        return carry

    def two(turn, carry):
        add(low + 4 * fours + 2 * turn, 2, True)
        return carry

    lax.fori_loop(0, fours, four, 0)
    lax.fori_loop(0, (high - low - 4 * fours + 1) // 2, two, 0)

    if last:
        for h in range(heads):
            out_ref[0, :, h * dim:(h + 1) * dim] = total[:, h * rows:(h + 1) * rows].T.astype(jnp.bfloat16)
    else:
        out_ref[0] = total[...]


def attend(packed, memories, places, acc, picks, starts, heads, rows, dim, scale, last):
    tiles, span, _ = packed.shape
    fresh = acc is None
    count = len(places)
    mem_dev = memories[0].shape[1]
    blocks = mem_dev // BLOCK
    width = heads * rows
    acc_spec = pl.BlockSpec((1, dim, width), lambda t, *_: (t, 0, 0))
    if last:
        out_shape = jax.ShapeDtypeStruct((tiles, rows, heads * dim), jnp.bfloat16)
        out_spec = pl.BlockSpec((1, rows, heads * dim), lambda t, *_: (t, 0, 0))
    else:
        out_shape = jax.ShapeDtypeStruct((tiles, dim, width), jnp.float32)
        out_spec = acc_spec
    flops = tiles * count * (blocks // 2) * BLOCK * width * dim * 6
    return pl.pallas_call(
        functools.partial(attend_kernel, heads, rows, dim, scale, fresh, last, places),
        out_shape=out_shape,
        grid_spec=pltpu.PrefetchScalarGridSpec(
            num_scalar_prefetch=2,
            grid=(tiles,),
            in_specs=[pl.BlockSpec((1, span, width), lambda t, *_: (t, 0, 0))]
            + [pl.BlockSpec(m.shape, lambda t, *_: (0, 0, 0)) for m in memories]
            + ([] if fresh else [acc_spec]),
            out_specs=out_spec,
            scratch_shapes=[
                pltpu.VMEM((count * mem_dev, dim), jnp.bfloat16),
                pltpu.VMEM((count * mem_dev, dim), jnp.bfloat16),
                pltpu.VMEM((count * blocks, dim, BLOCK), jnp.bfloat16),
                pltpu.VMEM((dim, width), jnp.float32),
            ],
        ),
        compiler_params=pltpu.CompilerParams(vmem_limit_bytes=VMEM_LIMIT),
        cost_estimate=pl.CostEstimate(
            flops=flops * 2, bytes_accessed=tiles * span * width * 2 + tiles * width * dim * 8, transcendentals=0
        ),
    )(picks, starts, packed, *memories, *([] if fresh else [acc]))


def shards(grad_out, queries, mem_out, row_total, gate_logit, mem_keys, mem_values, retrieved):
    seq = lax.axis_size("seq")
    sections = lax.axis_size("section")
    position = lax.axis_index("seq")
    rows, width = grad_out.shape[1:]
    head_count = gate_logit.shape[1]
    dim = width // head_count
    kv_heads = mem_keys.shape[2] // dim
    heads = head_count // kv_heads
    mem_dev = mem_keys.shape[1]
    blocks = mem_dev // BLOCK
    group = min(kv_heads, seq // 2)
    own = kv_heads // group
    at = position % group
    scale = dim ** (-0.5)

    def swapped(value, step):
        return lax.ppermute(value, "seq", [(p, p ^ step) for p in range(seq)])

    logs = jnp.log(row_total[0].T.astype(jnp.float32)) - math.log(scale)
    gates = jax.nn.sigmoid(gate_logit[0])

    mine = lax.dynamic_slice_in_dim(retrieved[0], at * own, own, 0)
    mine = lax.dynamic_slice_in_dim(mine, (position // group) * group, group, 1)
    distance = ((mine // blocks) ^ position) * blocks + mine % blocks
    rank = jnp.sum(distance[..., None, :] < distance[..., :, None], axis=-1)
    order = jnp.arange(distance.shape[-1])
    ordered = jnp.sum(jnp.where(rank[..., :, None] == order, distance[..., :, None], 0), axis=-2)
    picks = ordered.astype(jnp.int32)
    starts = jnp.sum(distance[..., None, :] < (jnp.arange(seq + 1) * blocks)[:, None], axis=-1).astype(jnp.int32)

    stages = [tuple(range(group))]
    half = group + (seq - group) // 2
    stages.append(tuple(range(group, half)))
    stages.append(tuple(range(half, seq)))

    groups = [list(range(g * group, (g + 1) * group)) for g in range(seq // group)]
    out = jnp.zeros((rows, width), jnp.bfloat16)
    for i in range(own):
        sends = pack(mem_keys[0], mem_values[0], at, own, group, i, dim)
        arrived = {0: sends[0]}
        for step in range(group, seq):
            arrived[step] = swapped(sends[step % group], step)
        packed = prepare(grad_out[0], queries[0], mem_out[0], logs, gates, kv_heads, dim, own, i)
        mixed = lax.all_to_all(
            packed, "seq", split_axis=0, concat_axis=0, axis_index_groups=groups, tiled=True
        )
        for step in range(1, group):
            arrived[step] = swapped(sends[step], step)
        acc = None
        for number, places in enumerate(stages):
            acc = attend(
                mixed, [arrived[p] for p in places], places, acc, picks[i], starts[i],
                heads, rows, dim, scale, number == len(stages) - 1,
            )
        for x in range(group):
            piece = lax.dynamic_index_in_dim(acc, at ^ x, 0, keepdims=False)
            pairs = [
                (s * seq + p, ((s - 1) % sections) * seq + (p ^ x)) for s in range(sections) for p in range(seq)
            ]
            piece = lax.ppermute(piece, ("section", "seq"), pairs)
            out = lax.dynamic_update_slice_in_dim(out, piece, ((at ^ x) * own + i) * heads * dim, 1)
    return out[None]


def solution(mesh):
    return jax.shard_map(
        shards,
        mesh=mesh,
        in_specs=(
            P("section", "seq", None),
            P("section", "seq", None),
            P("section", "seq", None),
            P("section", "seq", None),
            P("section", None),
            P("section", "seq", None),
            P("section", "seq", None),
            P("section", None, None, None),
        ),
        out_specs=P("section", "seq", None),
        check_vma=False,
    )
```

```python
import functools
import math

import jax
import jax.numpy as jnp
from jax import lax
from jax.experimental import pallas as pl
from jax.experimental.pallas import tpu as pltpu
from jax.sharding import PartitionSpec as P

BLOCK = 128
PARTS = 3
STAT_ROWS = 16
STEP = 4
VMEM_LIMIT = 48 * 1024 * 1024


def split_parts(value):
    terms = []
    for _ in range(PARTS):
        term = value.astype(jnp.bfloat16)
        terms.append(term.astype(jnp.float32))
        value = value - terms[-1]
    return terms


def pack_kernel(own, group, at_ref, keys_ref, values_ref, *outs):
    rows = keys_ref.shape[0]
    dim = outs[0].shape[2]
    for x in range(group):
        for index in range(own):
            column = pl.multiple_of(((at_ref[0] ^ x) * own + index) * dim, dim)
            out = outs[index * group + x]
            out[0, :rows, :] = keys_ref[:, pl.ds(column, dim)]
            out[0, rows:, :] = values_ref[:, pl.ds(column, dim)]


def pack(mem_keys, mem_values, at, own, group, dim):
    mem_dev, width = mem_keys.shape
    shape = jax.ShapeDtypeStruct((1, 2 * mem_dev, dim), mem_keys.dtype)
    whole = pl.BlockSpec((mem_dev, width), lambda i, _: (0, 0))
    return pl.pallas_call(
        functools.partial(pack_kernel, own, group),
        out_shape=[shape] * (own * group),
        grid_spec=pltpu.PrefetchScalarGridSpec(
            num_scalar_prefetch=1,
            grid=(1,),
            in_specs=[whole, whole],
            out_specs=[pl.BlockSpec((1, 2 * mem_dev, dim), lambda i, _: (0, 0, 0))] * (own * group),
        ),
        compiler_params=pltpu.CompilerParams(vmem_limit_bytes=VMEM_LIMIT),
        cost_estimate=pl.CostEstimate(flops=0, bytes_accessed=8 * mem_dev * width, transcendentals=0),
    )(at[None], mem_keys, mem_values)


def prepare_kernel(heads, dim, own, index, gate_ref, grad_ref, query_ref, out_ref, log_ref, keys_ref, values_ref, mixed_ref):
    rows = grad_ref.shape[0]
    mem_dev = keys_ref.shape[0]
    head = pl.program_id(0) * own + index
    column = pl.ds(pl.multiple_of(head * dim, dim), dim)
    mixed_ref[0, :mem_dev, :] = keys_ref[:, column]
    mixed_ref[0, mem_dev:2 * mem_dev, :] = values_ref[:, column]
    base = 2 * mem_dev
    for h in range(heads):
        columns = slice(h * dim, (h + 1) * dim)
        mixed_ref[0, base + h * dim:base + (h + 1) * dim, :] = query_ref[:, columns].T
        gated = (gate_ref[head * heads + h] * grad_ref[:, columns].T.astype(jnp.float32)).astype(jnp.bfloat16)
        mixed_ref[0, base + (heads + h) * dim:base + (heads + h + 1) * dim, :] = gated
        product = gated.astype(jnp.float32) * out_ref[:, columns].T.astype(jnp.float32)
        delta = jnp.sum(product, axis=0, keepdims=True)
        terms = split_parts(delta) + split_parts(log_ref[h:h + 1, :])
        filler = jnp.zeros((STAT_ROWS - len(terms), rows), jnp.float32)
        start = base + 2 * heads * dim + h * STAT_ROWS
        mixed_ref[0, start:start + STAT_ROWS, :] = jnp.concatenate(terms + [filler], axis=0).astype(jnp.bfloat16)


def prepare(grad_out, queries, mem_out, logs, gates, mem_keys, mem_values, kv_heads, dim, own, index):
    rows, width = grad_out.shape
    mem_dev, kv_width = mem_keys.shape
    heads = width // dim // kv_heads
    group = kv_heads // own
    span = 2 * mem_dev + heads * (2 * dim + STAT_ROWS)
    wide = pl.BlockSpec((rows, heads * dim), lambda k, _: (0, k * own + index))
    whole = pl.BlockSpec((mem_dev, kv_width), lambda k, _: (0, 0))
    return pl.pallas_call(
        functools.partial(prepare_kernel, heads, dim, own, index),
        out_shape=jax.ShapeDtypeStruct((group, span, rows), jnp.bfloat16),
        grid_spec=pltpu.PrefetchScalarGridSpec(
            num_scalar_prefetch=1,
            grid=(group,),
            in_specs=[
                wide, wide, wide, pl.BlockSpec((heads, rows), lambda k, _: (k * own + index, 0)), whole, whole,
            ],
            out_specs=pl.BlockSpec((1, span, rows), lambda k, _: (k, 0, 0)),
        ),
        compiler_params=pltpu.CompilerParams(vmem_limit_bytes=VMEM_LIMIT),
        cost_estimate=pl.CostEstimate(flops=rows * width * 4, bytes_accessed=rows * width * 12 // own, transcendentals=0),
    )(gates, grad_out, queries, mem_out, logs, mem_keys, mem_values)


def attend_kernel(heads, dim, rows, mem_dev, scale, fresh, last, places, only_ref, picks_ref, starts_ref, *refs):
    count = places[1] - places[0]
    query_ref, stat_ref = refs[:2]
    if fresh:
        memory_refs, acc_in = refs[2:-5], None
    else:
        memory_refs, acc_in = refs[2:-6], refs[-6]
    out_ref, keys_ref, values_ref, turned, total = refs[-5:]
    step = pl.program_id(0)
    tile = only_ref[0] + step
    blocks = mem_dev // BLOCK
    pair = 2 * rows

    @pl.when(step == 0)
    def _():
        at = 0
        for memory in memory_refs:
            for piece in range(memory.shape[0]):
                here = slice(at * mem_dev, (at + 1) * mem_dev)
                keys_ref[here, :] = memory[piece, :mem_dev, :]
                values_ref[here, :] = memory[piece, mem_dev:, :]
                for block in range(blocks):
                    turned[at * blocks + block] = memory[piece, block * BLOCK:(block + 1) * BLOCK, :].T
                at += 1

    if fresh:
        total[...] = jnp.zeros_like(total)
    else:
        total[...] = acc_in[0]

    deltas, logs = [], []
    for h in range(heads):
        stats = stat_ref[0, h * STAT_ROWS:(h + 1) * STAT_ROWS, :].astype(jnp.float32)
        deltas.append(jnp.sum(stats[:PARTS], axis=0, keepdims=True))
        logs.append(jnp.sum(stats[PARTS:2 * PARTS], axis=0, keepdims=True))

    def wide(ref, first):
        return jnp.concatenate([ref[0, first * dim:(first + 1) * dim, :], ref[0, (first + 1) * dim:(first + 2) * dim, :]], axis=1)

    low = starts_ref[tile, places[0]]
    high = starts_ref[tile, places[1]]
    offset = places[0] * blocks
    exponent = scale * math.log2(math.e)

    def add(here, number, checked):
        keys, values, across = [], [], []
        for j in range(number):
            valid = here + j < high
            block = picks_ref[tile, jnp.where(valid, here + j, here) if checked else here + j] - offset
            row = pl.ds(pl.multiple_of(block * BLOCK, BLOCK), BLOCK)
            keys.append(keys_ref[row, :])
            values.append(values_ref[row, :])
            side = turned[block]
            across.append(jnp.where(valid, side, jnp.zeros_like(side)) if checked and j else side)
        keys = jnp.concatenate(keys, axis=0)
        values = jnp.concatenate(values, axis=0)
        across = jnp.concatenate(across, axis=1)
        for p in range(heads // 2):
            span = slice(p * pair, (p + 1) * pair)
            log_row = jnp.concatenate(logs[2 * p:2 * p + 2], axis=1)
            delta_row = jnp.concatenate(deltas[2 * p:2 * p + 2], axis=1)
            scores = jnp.dot(keys, wide(query_ref, 2 * p), preferred_element_type=jnp.float32)
            grad_probs = jnp.dot(values, wide(query_ref, heads + 2 * p), preferred_element_type=jnp.float32)
            probs = jnp.exp2(scores * exponent - log_row)
            grad_scores = (probs * (grad_probs - delta_row)).astype(jnp.bfloat16)
            total[:, span] += jnp.dot(across, grad_scores, preferred_element_type=jnp.float32)

    full = (high - low) // STEP

    def many(turn, carry):
        add(low + STEP * turn, STEP, False)
        return carry

    def few(turn, carry):
        add(low + STEP * full + 2 * turn, 2, True)
        return carry

    lax.fori_loop(0, full, many, 0)
    lax.fori_loop(0, (high - low - STEP * full + 1) // 2, few, 0)

    if last:
        for h in range(heads):
            out_ref[0, :, h * dim:(h + 1) * dim] = total[:, h * rows:(h + 1) * rows].T.astype(jnp.bfloat16)
    else:
        out_ref[0] = total[...]


def attend(mixed, memories, places, acc, picks, starts, heads, dim, mem_dev, scale, last, only=None):
    tiles, span, rows = mixed.shape
    fresh = acc is None
    count = places[1] - places[0]
    blocks = mem_dev // BLOCK
    width = heads * rows
    big = 2 * heads * dim
    steps = tiles if only is None else 1
    acc_spec = pl.BlockSpec((1, dim, width), lambda t, o, *_: (o[0] + t, 0, 0))
    if last:
        out_shape = jax.ShapeDtypeStruct((steps, rows, heads * dim), jnp.bfloat16)
        out_spec = pl.BlockSpec((1, rows, heads * dim), lambda t, *_: (t, 0, 0))
    else:
        out_shape = jax.ShapeDtypeStruct((tiles, dim, width), jnp.float32)
        out_spec = acc_spec
    if memories is None:
        memories = [mixed]
        memory_specs = [pl.BlockSpec((tiles, 2 * mem_dev, dim), lambda t, *_: (0, 0, 0))]
    else:
        memory_specs = [pl.BlockSpec(m.shape, lambda t, *_: (0, 0, 0)) for m in memories]
    stat = heads * STAT_ROWS
    first = 2 * mem_dev // big
    last_block = (2 * mem_dev + big) // stat
    flops = steps * count * (blocks // 2) * BLOCK * width * dim * 6
    return pl.pallas_call(
        functools.partial(attend_kernel, heads, dim, rows, mem_dev, scale, fresh, last, places),
        out_shape=out_shape,
        grid_spec=pltpu.PrefetchScalarGridSpec(
            num_scalar_prefetch=3,
            grid=(steps,),
            in_specs=[
                pl.BlockSpec((1, big, rows), lambda t, o, *_: (o[0] + t, first, 0)),
                pl.BlockSpec((1, stat, rows), lambda t, o, *_: (o[0] + t, last_block, 0)),
            ]
            + memory_specs
            + ([] if fresh else [acc_spec]),
            out_specs=out_spec,
            scratch_shapes=[
                pltpu.VMEM((count * mem_dev, dim), jnp.bfloat16),
                pltpu.VMEM((count * mem_dev, dim), jnp.bfloat16),
                pltpu.VMEM((count * blocks, dim, BLOCK), jnp.bfloat16),
                pltpu.VMEM((dim, width), jnp.float32),
            ],
        ),
        compiler_params=pltpu.CompilerParams(vmem_limit_bytes=VMEM_LIMIT),
        cost_estimate=pl.CostEstimate(
            flops=flops * 4, bytes_accessed=0, transcendentals=0
        ),
    )(
        jnp.zeros((1,), jnp.int32) if only is None else only[None], picks, starts, mixed, mixed, *memories,
        *([] if fresh else [acc]),
    )


def after(value, *others):
    anywhere = pl.BlockSpec(memory_space=pl.ANY)
    return pl.pallas_call(
        lambda *refs: None,
        out_shape=jax.ShapeDtypeStruct(value.shape, value.dtype),
        in_specs=[anywhere] * (1 + len(others)),
        out_specs=anywhere,
        input_output_aliases={0: 0},
        cost_estimate=pl.CostEstimate(flops=0, bytes_accessed=0, transcendentals=0),
    )(value, *others)


def shards(grad_out, queries, mem_out, row_total, gate_logit, mem_keys, mem_values, retrieved):
    seq = lax.axis_size("seq")
    sections = lax.axis_size("section")
    position = lax.axis_index("seq")
    rows, width = grad_out.shape[1:]
    head_count = gate_logit.shape[1]
    dim = width // head_count
    kv_heads = mem_keys.shape[2] // dim
    heads = head_count // kv_heads
    mem_dev = mem_keys.shape[1]
    blocks = mem_dev // BLOCK
    group = min(kv_heads, seq // 2)
    own = kv_heads // group
    at = position % group
    home = position // group
    scale = dim ** (-0.5)

    def swapped(value, step):
        return lax.ppermute(value, "seq", [(p, p ^ step) for p in range(seq)])

    def delivered(value, step):
        pairs = [(s * seq + p, ((s - 1) % sections) * seq + (p ^ step)) for s in range(sections) for p in range(seq)]
        return lax.ppermute(value, ("section", "seq"), pairs)

    logs = jnp.log2(row_total[0].T.astype(jnp.float32)) - math.log2(scale)
    gates = jax.nn.sigmoid(gate_logit[0])

    mine = lax.dynamic_slice_in_dim(retrieved[0], at * own, own, 0)
    mine = lax.dynamic_slice_in_dim(mine, home * group, group, 1)
    holder = mine // blocks
    place = jnp.where(holder // group == home, holder % group, holder ^ position)
    block = place * blocks + mine % blocks
    rank = jnp.sum(block[..., None, :] < block[..., :, None], axis=-1)
    order = jnp.arange(block.shape[-1])
    picks = jnp.sum(jnp.where(rank[..., :, None] == order, block[..., :, None], 0), axis=-2).astype(jnp.int32)
    starts = jnp.sum(block[..., None, :] < (jnp.arange(seq + 1) * blocks)[:, None], axis=-1).astype(jnp.int32)

    half = group + (seq - group) // 2
    most = seq - 1

    def settle(acc, i, out):
        acc = lax.all_to_all(acc, "seq", split_axis=0, concat_axis=0, axis_index_groups=groups, tiled=True)
        acc = delivered(acc, 0)
        for t in range(group):
            out = lax.dynamic_update_slice_in_dim(out, acc[t], (t * own + i) * heads * dim, 1)
        return out

    groups = [list(range(g * group, (g + 1) * group)) for g in range(seq // group)]
    sends = list(pack(mem_keys[0], mem_values[0], at, own, group, dim))
    out = jnp.zeros((rows, width), jnp.bfloat16)
    def shared(i):
        mixed = prepare(
            grad_out[0], queries[0], mem_out[0], logs, gates, mem_keys[0], mem_values[0], kv_heads, dim, own, i
        )
        return lax.all_to_all(mixed, "seq", split_axis=0, concat_axis=0, axis_index_groups=groups, tiled=True)

    done = None
    coming = shared(0)
    for i in range(own):
        ending = i == own - 1
        mixed = coming
        arrived = {step: swapped(sends[i * group + step % group], step) for step in range(group, seq)}
        run = functools.partial(attend, mixed, heads=heads, dim=dim, mem_dev=mem_dev, scale=scale, picks=picks[i])
        where = starts[i]
        if not ending:
            coming = shared(i + 1)
            for step in range(group, half):
                later = (i + 1) * group + step % group
                sends[later] = after(sends[later], arrived[step])
            where = after(where, *[arrived[step] for step in range(group, half)])
        if i:
            where = after(where, done)
            out = settle(done, i - 1, out)
        acc = run(None, (0, group), None, starts=where, last=False)
        if not ending:
            for step in range(half, seq):
                later = (i + 1) * group + step % group
                sends[later] = after(sends[later], arrived[step], acc)
            where = after(where, coming)
            done = run([arrived[p] for p in range(group, seq)], (group, seq), acc, starts=where, last=True)
            continue
        acc = run([arrived[p] for p in range(group, half)], (group, half), acc, starts=where, last=False)
        if half < most:
            acc = run([arrived[p] for p in range(half, most)], (half, most), acc, starts=where, last=False)
        for x in range(group):
            only = (at ^ x).astype(jnp.int32)
            piece = run([arrived[most]], (most, seq), acc, starts=where, last=True, only=only)
            piece = delivered(piece[0], x)
            out = lax.dynamic_update_slice_in_dim(out, piece, ((at ^ x) * own + i) * heads * dim, 1)
    return out[None]


def solution(mesh):
    return jax.shard_map(
        shards,
        mesh=mesh,
        in_specs=(
            P("section", "seq", None),
            P("section", "seq", None),
            P("section", "seq", None),
            P("section", "seq", None),
            P("section", None),
            P("section", "seq", None),
            P("section", "seq", None),
            P("section", None, None, None),
        ),
        out_specs=P("section", "seq", None),
        check_vma=False,
    )
```

```python
import functools
import math

import jax
import jax.numpy as jnp
from jax import lax
from jax.experimental import pallas as pl
from jax.experimental.pallas import tpu as pltpu
from jax.sharding import PartitionSpec as P

BLOCK = 128
PARTS = 3
STAT_ROWS = 16
STEP = 4
VMEM_LIMIT = 48 * 1024 * 1024


def split_parts(value):
    terms = []
    for _ in range(PARTS):
        term = value.astype(jnp.bfloat16)
        terms.append(term.astype(jnp.float32))
        value = value - terms[-1]
    return terms


def pack_kernel(own, group, at_ref, keys_ref, values_ref, *outs):
    rows = keys_ref.shape[0]
    dim = outs[0].shape[2]
    for x in range(group):
        for index in range(own):
            column = pl.multiple_of(((at_ref[0] ^ x) * own + index) * dim, dim)
            out = outs[index * group + x]
            out[0, :rows, :] = keys_ref[:, pl.ds(column, dim)]
            out[0, rows:, :] = values_ref[:, pl.ds(column, dim)]


def pack(mem_keys, mem_values, at, own, group, dim):
    mem_dev, width = mem_keys.shape
    shape = jax.ShapeDtypeStruct((1, 2 * mem_dev, dim), mem_keys.dtype)
    whole = pl.BlockSpec((mem_dev, width), lambda i, _: (0, 0))
    return pl.pallas_call(
        functools.partial(pack_kernel, own, group),
        out_shape=[shape] * (own * group),
        grid_spec=pltpu.PrefetchScalarGridSpec(
            num_scalar_prefetch=1,
            grid=(1,),
            in_specs=[whole, whole],
            out_specs=[pl.BlockSpec((1, 2 * mem_dev, dim), lambda i, _: (0, 0, 0))] * (own * group),
        ),
        compiler_params=pltpu.CompilerParams(vmem_limit_bytes=VMEM_LIMIT),
        cost_estimate=pl.CostEstimate(flops=0, bytes_accessed=8 * mem_dev * width, transcendentals=0),
    )(at[None], mem_keys, mem_values)


def prepare_kernel(heads, dim, own, index, gate_ref, grad_ref, query_ref, out_ref, log_ref, keys_ref, values_ref, mixed_ref):
    rows = grad_ref.shape[0]
    mem_dev = keys_ref.shape[0]
    head = pl.program_id(0) * own + index
    column = pl.ds(pl.multiple_of(head * dim, dim), dim)
    mixed_ref[0, :mem_dev, :] = keys_ref[:, column]
    mixed_ref[0, mem_dev:2 * mem_dev, :] = values_ref[:, column]
    base = 2 * mem_dev
    for h in range(heads):
        columns = slice(h * dim, (h + 1) * dim)
        mixed_ref[0, base + h * dim:base + (h + 1) * dim, :] = query_ref[:, columns].T
        gated = (gate_ref[head * heads + h] * grad_ref[:, columns].T.astype(jnp.float32)).astype(jnp.bfloat16)
        mixed_ref[0, base + (heads + h) * dim:base + (heads + h + 1) * dim, :] = gated
        product = gated.astype(jnp.float32) * out_ref[:, columns].T.astype(jnp.float32)
        delta = jnp.sum(product, axis=0, keepdims=True)
        terms = split_parts(delta) + split_parts(log_ref[h:h + 1, :])
        filler = jnp.zeros((STAT_ROWS - len(terms), rows), jnp.float32)
        start = base + 2 * heads * dim + h * STAT_ROWS
        mixed_ref[0, start:start + STAT_ROWS, :] = jnp.concatenate(terms + [filler], axis=0).astype(jnp.bfloat16)


def prepare(grad_out, queries, mem_out, logs, gates, mem_keys, mem_values, kv_heads, dim, own, index):
    rows, width = grad_out.shape
    mem_dev, kv_width = mem_keys.shape
    heads = width // dim // kv_heads
    group = kv_heads // own
    span = 2 * mem_dev + heads * (2 * dim + STAT_ROWS)
    wide = pl.BlockSpec((rows, heads * dim), lambda k, _: (0, k * own + index))
    whole = pl.BlockSpec((mem_dev, kv_width), lambda k, _: (0, 0))
    return pl.pallas_call(
        functools.partial(prepare_kernel, heads, dim, own, index),
        out_shape=jax.ShapeDtypeStruct((group, span, rows), jnp.bfloat16),
        grid_spec=pltpu.PrefetchScalarGridSpec(
            num_scalar_prefetch=1,
            grid=(group,),
            in_specs=[
                wide, wide, wide, pl.BlockSpec((heads, rows), lambda k, _: (k * own + index, 0)), whole, whole,
            ],
            out_specs=pl.BlockSpec((1, span, rows), lambda k, _: (k, 0, 0)),
        ),
        compiler_params=pltpu.CompilerParams(vmem_limit_bytes=VMEM_LIMIT),
        cost_estimate=pl.CostEstimate(flops=rows * width * 4, bytes_accessed=rows * width * 12 // own, transcendentals=0),
    )(gates, grad_out, queries, mem_out, logs, mem_keys, mem_values)


def attend_kernel(heads, dim, rows, mem_dev, scale, fresh, last, places, only_ref, picks_ref, starts_ref, *refs):
    count = places[1] - places[0]
    query_ref, stat_ref = refs[:2]
    if fresh:
        memory_refs, acc_in = refs[2:-5], None
    else:
        memory_refs, acc_in = refs[2:-6], refs[-6]
    out_ref, keys_ref, values_ref, turned, total = refs[-5:]
    step = pl.program_id(0)
    tile = only_ref[0] + step
    blocks = mem_dev // BLOCK
    pair = 2 * rows

    @pl.when(step == 0)
    def _():
        at = 0
        for memory in memory_refs:
            for piece in range(memory.shape[0]):
                here = slice(at * mem_dev, (at + 1) * mem_dev)
                keys_ref[here, :] = memory[piece, :mem_dev, :]
                values_ref[here, :] = memory[piece, mem_dev:, :]
                for block in range(blocks):
                    turned[at * blocks + block] = memory[piece, block * BLOCK:(block + 1) * BLOCK, :].T
                at += 1

    if fresh:
        total[...] = jnp.zeros_like(total)
    else:
        total[...] = acc_in[0]

    deltas, logs = [], []
    for h in range(heads):
        stats = stat_ref[0, h * STAT_ROWS:(h + 1) * STAT_ROWS, :].astype(jnp.float32)
        deltas.append(jnp.sum(stats[:PARTS], axis=0, keepdims=True))
        logs.append(jnp.sum(stats[PARTS:2 * PARTS], axis=0, keepdims=True))

    def wide(ref, first):
        return jnp.concatenate([ref[0, first * dim:(first + 1) * dim, :], ref[0, (first + 1) * dim:(first + 2) * dim, :]], axis=1)

    low = starts_ref[tile, places[0]]
    high = starts_ref[tile, places[1]]
    offset = places[0] * blocks
    exponent = scale * math.log2(math.e)

    def add(here, number, checked):
        keys, values, across = [], [], []
        for j in range(number):
            valid = here + j < high
            block = picks_ref[tile, jnp.where(valid, here + j, here) if checked else here + j] - offset
            row = pl.ds(pl.multiple_of(block * BLOCK, BLOCK), BLOCK)
            keys.append(keys_ref[row, :])
            values.append(values_ref[row, :])
            side = turned[block]
            across.append(jnp.where(valid, side, jnp.zeros_like(side)) if checked and j else side)
        sides = [
            (
                jnp.concatenate(keys[j:j + 2], axis=0),
                jnp.concatenate(values[j:j + 2], axis=0),
                jnp.concatenate(across[j:j + 2], axis=1),
            )
            for j in range(0, number, 2)
        ]
        items = [(p, side) for p in range(heads // 2) for side in range(len(sides))]

        def products(item):
            p, side = item
            scores = jnp.dot(sides[side][0], wide(query_ref, 2 * p), preferred_element_type=jnp.float32)
            grad_probs = jnp.dot(sides[side][1], wide(query_ref, heads + 2 * p), preferred_element_type=jnp.float32)
            return scores, grad_probs

        ahead = products(items[0])
        gained = None
        for at, (p, side) in enumerate(items):
            scores, grad_probs = ahead
            if at + 1 < len(items):
                ahead = products(items[at + 1])
            log_row = jnp.concatenate(logs[2 * p:2 * p + 2], axis=1)
            delta_row = jnp.concatenate(deltas[2 * p:2 * p + 2], axis=1)
            probs = jnp.exp2(scores * exponent - log_row)
            grad_scores = (probs * (grad_probs - delta_row)).astype(jnp.bfloat16)
            part = jnp.dot(sides[side][2], grad_scores, preferred_element_type=jnp.float32)
            gained = part if side == 0 else gained + part
            if side == len(sides) - 1:
                total[:, p * pair:(p + 1) * pair] += gained

    full = (high - low) // STEP

    def many(turn, carry):
        add(low + STEP * turn, STEP, False)
        return carry

    def few(turn, carry):
        add(low + STEP * full + 2 * turn, 2, True)
        return carry

    lax.fori_loop(0, full, many, 0)
    lax.fori_loop(0, (high - low - STEP * full + 1) // 2, few, 0)

    if last:
        for h in range(heads):
            out_ref[0, :, h * dim:(h + 1) * dim] = total[:, h * rows:(h + 1) * rows].T.astype(jnp.bfloat16)
    else:
        out_ref[0] = total[...]


def attend(mixed, memories, places, acc, picks, starts, heads, dim, mem_dev, scale, last, only=None, weight=0):
    tiles, span, rows = mixed.shape
    fresh = acc is None
    count = places[1] - places[0]
    blocks = mem_dev // BLOCK
    width = heads * rows
    big = 2 * heads * dim
    steps = tiles if only is None else 1
    acc_spec = pl.BlockSpec((1, dim, width), lambda t, o, *_: (o[0] + t, 0, 0))
    if last:
        out_shape = jax.ShapeDtypeStruct((steps, rows, heads * dim), jnp.bfloat16)
        out_spec = pl.BlockSpec((1, rows, heads * dim), lambda t, *_: (t, 0, 0))
    else:
        out_shape = jax.ShapeDtypeStruct((tiles, dim, width), jnp.float32)
        out_spec = acc_spec
    if memories is None:
        memories = [mixed]
        memory_specs = [pl.BlockSpec((tiles, 2 * mem_dev, dim), lambda t, *_: (0, 0, 0))]
    else:
        memory_specs = [pl.BlockSpec(m.shape, lambda t, *_: (0, 0, 0)) for m in memories]
    stat = heads * STAT_ROWS
    first = 2 * mem_dev // big
    last_block = (2 * mem_dev + big) // stat
    flops = steps * count * (blocks // 2) * BLOCK * width * dim * 6
    return pl.pallas_call(
        functools.partial(attend_kernel, heads, dim, rows, mem_dev, scale, fresh, last, places),
        out_shape=out_shape,
        grid_spec=pltpu.PrefetchScalarGridSpec(
            num_scalar_prefetch=3,
            grid=(steps,),
            in_specs=[
                pl.BlockSpec((1, big, rows), lambda t, o, *_: (o[0] + t, first, 0)),
                pl.BlockSpec((1, stat, rows), lambda t, o, *_: (o[0] + t, last_block, 0)),
            ]
            + memory_specs
            + ([] if fresh else [acc_spec]),
            out_specs=out_spec,
            scratch_shapes=[
                pltpu.VMEM((count * mem_dev, dim), jnp.bfloat16),
                pltpu.VMEM((count * mem_dev, dim), jnp.bfloat16),
                pltpu.VMEM((count * blocks, dim, BLOCK), jnp.bfloat16),
                pltpu.VMEM((dim, width), jnp.float32),
            ],
        ),
        compiler_params=pltpu.CompilerParams(vmem_limit_bytes=VMEM_LIMIT),
        cost_estimate=pl.CostEstimate(
            flops=flops * weight, bytes_accessed=0, transcendentals=0
        ),
    )(
        jnp.zeros((1,), jnp.int32) if only is None else only[None], picks, starts, mixed, mixed, *memories,
        *([] if fresh else [acc]),
    )


def after(value, *others):
    anywhere = pl.BlockSpec(memory_space=pl.ANY)
    return pl.pallas_call(
        lambda *refs: None,
        out_shape=jax.ShapeDtypeStruct(value.shape, value.dtype),
        in_specs=[anywhere] * (1 + len(others)),
        out_specs=anywhere,
        input_output_aliases={0: 0},
        cost_estimate=pl.CostEstimate(flops=0, bytes_accessed=0, transcendentals=0),
    )(value, *others)


def sign(value):
    return value[:1, :STAT_ROWS]


def shards(grad_out, queries, mem_out, row_total, gate_logit, mem_keys, mem_values, retrieved):
    seq = lax.axis_size("seq")
    sections = lax.axis_size("section")
    position = lax.axis_index("seq")
    rows, width = grad_out.shape[1:]
    head_count = gate_logit.shape[1]
    dim = width // head_count
    kv_heads = mem_keys.shape[2] // dim
    heads = head_count // kv_heads
    mem_dev = mem_keys.shape[1]
    blocks = mem_dev // BLOCK
    group = min(kv_heads, seq // 2)
    own = kv_heads // group
    at = position % group
    home = position // group
    scale = dim ** (-0.5)

    def swapped(value, step):
        return lax.ppermute(value, "seq", [(p, p ^ step) for p in range(seq)])

    def delivered(value, step):
        pairs = [(s * seq + p, ((s - 1) % sections) * seq + (p ^ step)) for s in range(sections) for p in range(seq)]
        return lax.ppermute(value, ("section", "seq"), pairs)

    logs = jnp.log2(row_total[0].T.astype(jnp.float32)) - math.log2(scale)
    gates = jax.nn.sigmoid(gate_logit[0])

    mine = lax.dynamic_slice_in_dim(retrieved[0], at * own, own, 0)
    mine = lax.dynamic_slice_in_dim(mine, home * group, group, 1)
    holder = mine // blocks
    place = jnp.where(holder // group == home, holder % group, holder ^ position)
    block = place * blocks + mine % blocks
    rank = jnp.sum(block[..., None, :] < block[..., :, None], axis=-1)
    order = jnp.arange(block.shape[-1])
    picks = jnp.sum(jnp.where(rank[..., :, None] == order, block[..., :, None], 0), axis=-2).astype(jnp.int32)
    starts = jnp.sum(block[..., None, :] < (jnp.arange(seq + 1) * blocks)[:, None], axis=-1).astype(jnp.int32)

    half = group + (seq - group) // 2
    most = seq - 1

    def settle(acc, i, out):
        acc = lax.all_to_all(acc, "seq", split_axis=0, concat_axis=0, axis_index_groups=groups, tiled=True)
        acc = delivered(acc, 0)
        for t in range(group):
            out = lax.dynamic_update_slice_in_dim(out, acc[t], (t * own + i) * heads * dim, 1)
        return out

    groups = [list(range(g * group, (g + 1) * group)) for g in range(seq // group)]
    sends = list(pack(mem_keys[0], mem_values[0], at, own, group, dim))
    out = jnp.zeros((rows, width), jnp.bfloat16)
    def shared(i, first):
        mixed = prepare(
            grad_out[0], queries[0], mem_out[0], logs, after(gates, sign(first)), mem_keys[0], mem_values[0], kv_heads, dim, own, i
        )
        return lax.all_to_all(mixed, "seq", split_axis=0, concat_axis=0, axis_index_groups=groups, tiled=True)

    done = None
    coming = shared(0, sends[0])
    for i in range(own):
        ending = i == own - 1
        mixed = coming
        arrived = {step: swapped(sends[i * group + step % group], step) for step in range(group, seq)}
        run = functools.partial(attend, mixed, heads=heads, dim=dim, mem_dev=mem_dev, scale=scale, picks=picks[i])
        where = starts[i]
        if not ending:
            coming = shared(i + 1, arrived[group])
            for step in range(group, half):
                later = (i + 1) * group + step % group
                sends[later] = after(sends[later], sign(arrived[step]))
            where = after(where, *[sign(arrived[step]) for step in range(group, half)])
        if i:
            where = after(where, sign(done))
        acc = run(None, (0, group), None, starts=where, last=False, weight=0 if ending else 8)
        if not ending:
            for step in range(half, seq):
                later = (i + 1) * group + step % group
                sends[later] = after(sends[later], sign(arrived[step]), sign(acc))
            where = after(where, sign(coming))
            done = run([arrived[p] for p in range(group, seq)], (group, seq), acc, starts=where, last=True)
            continue
        acc = run([arrived[p] for p in range(group, half)], (group, half), acc, starts=where, last=False, weight=8)
        if i:
            out = settle(after(done, sign(acc)), i - 1, out)
        if half < most:
            acc = run([arrived[p] for p in range(half, most)], (half, most), acc, starts=where, last=False, weight=8)
        for x in range(group):
            only = (at ^ x).astype(jnp.int32)
            piece = run([arrived[most]], (most, seq), acc, starts=where, last=True, only=only, weight=8)
            piece = delivered(piece[0], x)
            out = lax.dynamic_update_slice_in_dim(out, piece, ((at ^ x) * own + i) * heads * dim, 1)
    return out[None]


def solution(mesh):
    return jax.shard_map(
        shards,
        mesh=mesh,
        in_specs=(
            P("section", "seq", None),
            P("section", "seq", None),
            P("section", "seq", None),
            P("section", "seq", None),
            P("section", None),
            P("section", "seq", None),
            P("section", "seq", None),
            P("section", None, None, None),
        ),
        out_specs=P("section", "seq", None),
        check_vma=False,
    )
```

```python
import functools
import math

import jax
import jax.numpy as jnp
from jax import lax
from jax.experimental import pallas as pl
from jax.experimental.pallas import tpu as pltpu
from jax.sharding import PartitionSpec as P

BLOCK = 128
PARTS = 3
STAT_ROWS = 16
STEP = 4
VMEM_LIMIT = 48 * 1024 * 1024


def split_parts(value):
    terms = []
    for _ in range(PARTS):
        term = value.astype(jnp.bfloat16)
        terms.append(term.astype(jnp.float32))
        value = value - terms[-1]
    return terms


def pack_kernel(own, group, at_ref, keys_ref, values_ref, *outs):
    rows = keys_ref.shape[0]
    dim = outs[0].shape[2]
    for x in range(group):
        for index in range(own):
            column = pl.multiple_of(((at_ref[0] ^ x) * own + index) * dim, dim)
            out = outs[index * group + x]
            out[0, :rows, :] = keys_ref[:, pl.ds(column, dim)]
            out[0, rows:, :] = values_ref[:, pl.ds(column, dim)]


def pack(mem_keys, mem_values, at, own, group, dim):
    mem_dev, width = mem_keys.shape
    shape = jax.ShapeDtypeStruct((1, 2 * mem_dev, dim), mem_keys.dtype)
    whole = pl.BlockSpec((mem_dev, width), lambda i, _: (0, 0))
    return pl.pallas_call(
        functools.partial(pack_kernel, own, group),
        out_shape=[shape] * (own * group),
        grid_spec=pltpu.PrefetchScalarGridSpec(
            num_scalar_prefetch=1,
            grid=(1,),
            in_specs=[whole, whole],
            out_specs=[pl.BlockSpec((1, 2 * mem_dev, dim), lambda i, _: (0, 0, 0))] * (own * group),
        ),
        compiler_params=pltpu.CompilerParams(vmem_limit_bytes=VMEM_LIMIT),
        cost_estimate=pl.CostEstimate(flops=0, bytes_accessed=8 * mem_dev * width, transcendentals=0),
    )(at[None], mem_keys, mem_values)


def prepare_kernel(heads, dim, own, index, gate_ref, grad_ref, query_ref, out_ref, log_ref, keys_ref, values_ref, mixed_ref):
    rows = grad_ref.shape[0]
    mem_dev = keys_ref.shape[0]
    head = pl.program_id(0) * own + index
    column = pl.ds(pl.multiple_of(head * dim, dim), dim)
    mixed_ref[0, :mem_dev, :] = keys_ref[:, column]
    mixed_ref[0, mem_dev:2 * mem_dev, :] = values_ref[:, column]
    base = 2 * mem_dev
    for h in range(heads):
        columns = slice(h * dim, (h + 1) * dim)
        mixed_ref[0, base + h * dim:base + (h + 1) * dim, :] = query_ref[:, columns].T
        gated = (gate_ref[head * heads + h] * grad_ref[:, columns].T.astype(jnp.float32)).astype(jnp.bfloat16)
        mixed_ref[0, base + (heads + h) * dim:base + (heads + h + 1) * dim, :] = gated
        product = gated.astype(jnp.float32) * out_ref[:, columns].T.astype(jnp.float32)
        delta = jnp.sum(product, axis=0, keepdims=True)
        terms = split_parts(delta) + split_parts(log_ref[h:h + 1, :])
        filler = jnp.zeros((STAT_ROWS - len(terms), rows), jnp.float32)
        start = base + 2 * heads * dim + h * STAT_ROWS
        mixed_ref[0, start:start + STAT_ROWS, :] = jnp.concatenate(terms + [filler], axis=0).astype(jnp.bfloat16)


def prepare(grad_out, queries, mem_out, logs, gates, mem_keys, mem_values, kv_heads, dim, own, index):
    rows, width = grad_out.shape
    mem_dev, kv_width = mem_keys.shape
    heads = width // dim // kv_heads
    group = kv_heads // own
    span = 2 * mem_dev + heads * (2 * dim + STAT_ROWS)
    wide = pl.BlockSpec((rows, heads * dim), lambda k, _: (0, k * own + index))
    whole = pl.BlockSpec((mem_dev, kv_width), lambda k, _: (0, 0))
    return pl.pallas_call(
        functools.partial(prepare_kernel, heads, dim, own, index),
        out_shape=jax.ShapeDtypeStruct((group, span, rows), jnp.bfloat16),
        grid_spec=pltpu.PrefetchScalarGridSpec(
            num_scalar_prefetch=1,
            grid=(group,),
            in_specs=[
                wide, wide, wide, pl.BlockSpec((heads, rows), lambda k, _: (k * own + index, 0)), whole, whole,
            ],
            out_specs=pl.BlockSpec((1, span, rows), lambda k, _: (k, 0, 0)),
        ),
        compiler_params=pltpu.CompilerParams(vmem_limit_bytes=VMEM_LIMIT),
        cost_estimate=pl.CostEstimate(
            flops=rows * width * (4 if index == 0 else 1 << 17), bytes_accessed=rows * width * 12 // own, transcendentals=0
        ),
    )(gates, grad_out, queries, mem_out, logs, mem_keys, mem_values)


def attend_kernel(heads, dim, rows, mem_dev, scale, fresh, last, places, only_ref, picks_ref, starts_ref, *refs):
    count = places[1] - places[0]
    query_ref, stat_ref = refs[:2]
    if fresh:
        memory_refs, acc_in = refs[2:-5], None
    else:
        memory_refs, acc_in = refs[2:-6], refs[-6]
    out_ref, keys_ref, values_ref, turned, total = refs[-5:]
    step = pl.program_id(0)
    tile = only_ref[0] + step
    blocks = mem_dev // BLOCK
    pair = 2 * rows

    @pl.when(step == 0)
    def _():
        at = 0
        for memory in memory_refs:
            for piece in range(memory.shape[0]):
                here = slice(at * mem_dev, (at + 1) * mem_dev)
                keys_ref[here, :] = memory[piece, :mem_dev, :]
                values_ref[here, :] = memory[piece, mem_dev:, :]
                for block in range(blocks):
                    turned[at * blocks + block] = memory[piece, block * BLOCK:(block + 1) * BLOCK, :].T
                at += 1

    if fresh:
        total[...] = jnp.zeros_like(total)
    else:
        total[...] = acc_in[0]

    deltas, logs = [], []
    for h in range(heads):
        stats = stat_ref[0, h * STAT_ROWS:(h + 1) * STAT_ROWS, :].astype(jnp.float32)
        deltas.append(jnp.sum(stats[:PARTS], axis=0, keepdims=True))
        logs.append(jnp.sum(stats[PARTS:2 * PARTS], axis=0, keepdims=True))

    def wide(ref, first):
        return jnp.concatenate([ref[0, first * dim:(first + 1) * dim, :], ref[0, (first + 1) * dim:(first + 2) * dim, :]], axis=1)

    low = starts_ref[tile, places[0]]
    high = starts_ref[tile, places[1]]
    offset = places[0] * blocks
    exponent = scale * math.log2(math.e)

    def add(here, number, checked):
        keys, values, across = [], [], []
        for j in range(number):
            valid = here + j < high
            block = picks_ref[tile, jnp.where(valid, here + j, here) if checked else here + j] - offset
            row = pl.ds(pl.multiple_of(block * BLOCK, BLOCK), BLOCK)
            keys.append(keys_ref[row, :])
            values.append(values_ref[row, :])
            side = turned[block]
            across.append(jnp.where(valid, side, jnp.zeros_like(side)) if checked and j else side)
        sides = [
            (
                jnp.concatenate(keys[j:j + 2], axis=0),
                jnp.concatenate(values[j:j + 2], axis=0),
                jnp.concatenate(across[j:j + 2], axis=1),
            )
            for j in range(0, number, 2)
        ]
        items = [(p, side) for p in range(heads // 2) for side in range(len(sides))]

        def products(item):
            p, side = item
            scores = jnp.dot(sides[side][0], wide(query_ref, 2 * p), preferred_element_type=jnp.float32)
            grad_probs = jnp.dot(sides[side][1], wide(query_ref, heads + 2 * p), preferred_element_type=jnp.float32)
            return scores, grad_probs

        ahead = products(items[0])
        gained = None
        for at, (p, side) in enumerate(items):
            scores, grad_probs = ahead
            if at + 1 < len(items):
                ahead = products(items[at + 1])
            log_row = jnp.concatenate(logs[2 * p:2 * p + 2], axis=1)
            delta_row = jnp.concatenate(deltas[2 * p:2 * p + 2], axis=1)
            probs = jnp.exp2(scores * exponent - log_row)
            grad_scores = (probs * (grad_probs - delta_row)).astype(jnp.bfloat16)
            part = jnp.dot(sides[side][2], grad_scores, preferred_element_type=jnp.float32)
            gained = part if side == 0 else gained + part
            if side == len(sides) - 1:
                total[:, p * pair:(p + 1) * pair] += gained

    full = (high - low) // STEP

    def many(turn, carry):
        add(low + STEP * turn, STEP, False)
        return carry

    def few(turn, carry):
        add(low + STEP * full + 2 * turn, 2, True)
        return carry

    lax.fori_loop(0, full, many, 0)
    lax.fori_loop(0, (high - low - STEP * full + 1) // 2, few, 0)

    if last:
        for h in range(heads):
            out_ref[0, :, h * dim:(h + 1) * dim] = total[:, h * rows:(h + 1) * rows].T.astype(jnp.bfloat16)
    else:
        out_ref[0] = total[...]


def attend(mixed, memories, places, acc, picks, starts, heads, dim, mem_dev, scale, last, only=None):
    tiles, span, rows = mixed.shape
    fresh = acc is None
    count = places[1] - places[0]
    blocks = mem_dev // BLOCK
    width = heads * rows
    big = 2 * heads * dim
    steps = tiles if only is None else 1
    acc_spec = pl.BlockSpec((1, dim, width), lambda t, o, *_: (o[0] + t, 0, 0))
    if last:
        out_shape = jax.ShapeDtypeStruct((steps, rows, heads * dim), jnp.bfloat16)
        out_spec = pl.BlockSpec((1, rows, heads * dim), lambda t, *_: (t, 0, 0))
    else:
        out_shape = jax.ShapeDtypeStruct((tiles, dim, width), jnp.float32)
        out_spec = acc_spec
    if memories is None:
        memories = [mixed]
        memory_specs = [pl.BlockSpec((tiles, 2 * mem_dev, dim), lambda t, *_: (0, 0, 0))]
    else:
        memory_specs = [pl.BlockSpec(m.shape, lambda t, *_: (0, 0, 0)) for m in memories]
    stat = heads * STAT_ROWS
    first = 2 * mem_dev // big
    last_block = (2 * mem_dev + big) // stat
    flops = steps * count * (blocks // 2) * BLOCK * width * dim * 6
    return pl.pallas_call(
        functools.partial(attend_kernel, heads, dim, rows, mem_dev, scale, fresh, last, places),
        out_shape=out_shape,
        grid_spec=pltpu.PrefetchScalarGridSpec(
            num_scalar_prefetch=3,
            grid=(steps,),
            in_specs=[
                pl.BlockSpec((1, big, rows), lambda t, o, *_: (o[0] + t, first, 0)),
                pl.BlockSpec((1, stat, rows), lambda t, o, *_: (o[0] + t, last_block, 0)),
            ]
            + memory_specs
            + ([] if fresh else [acc_spec]),
            out_specs=out_spec,
            scratch_shapes=[
                pltpu.VMEM((count * mem_dev, dim), jnp.bfloat16),
                pltpu.VMEM((count * mem_dev, dim), jnp.bfloat16),
                pltpu.VMEM((count * blocks, dim, BLOCK), jnp.bfloat16),
                pltpu.VMEM((dim, width), jnp.float32),
            ],
        ),
        compiler_params=pltpu.CompilerParams(vmem_limit_bytes=VMEM_LIMIT),
        cost_estimate=pl.CostEstimate(
            flops=flops * 4, bytes_accessed=0, transcendentals=0
        ),
    )(
        jnp.zeros((1,), jnp.int32) if only is None else only[None], picks, starts, mixed, mixed, *memories,
        *([] if fresh else [acc]),
    )


def after(value, *others):
    anywhere = pl.BlockSpec(memory_space=pl.ANY)
    return pl.pallas_call(
        lambda *refs: None,
        out_shape=jax.ShapeDtypeStruct(value.shape, value.dtype),
        in_specs=[anywhere] * (1 + len(others)),
        out_specs=anywhere,
        input_output_aliases={0: 0},
        cost_estimate=pl.CostEstimate(flops=0, bytes_accessed=0, transcendentals=0),
    )(value, *others)


def sign(value):
    return value[:1, :STAT_ROWS]


def shards(grad_out, queries, mem_out, row_total, gate_logit, mem_keys, mem_values, retrieved):
    seq = lax.axis_size("seq")
    sections = lax.axis_size("section")
    position = lax.axis_index("seq")
    rows, width = grad_out.shape[1:]
    head_count = gate_logit.shape[1]
    dim = width // head_count
    kv_heads = mem_keys.shape[2] // dim
    heads = head_count // kv_heads
    mem_dev = mem_keys.shape[1]
    blocks = mem_dev // BLOCK
    group = min(kv_heads, seq // 2)
    own = kv_heads // group
    at = position % group
    home = position // group
    scale = dim ** (-0.5)

    def swapped(value, step):
        return lax.ppermute(value, "seq", [(p, p ^ step) for p in range(seq)])

    def delivered(value, step):
        pairs = [(s * seq + p, ((s - 1) % sections) * seq + (p ^ step)) for s in range(sections) for p in range(seq)]
        return lax.ppermute(value, ("section", "seq"), pairs)

    logs = jnp.log2(row_total[0].T.astype(jnp.float32)) - math.log2(scale)
    gates = jax.nn.sigmoid(gate_logit[0])

    mine = lax.dynamic_slice_in_dim(retrieved[0], at * own, own, 0)
    mine = lax.dynamic_slice_in_dim(mine, home * group, group, 1)
    holder = mine // blocks
    place = jnp.where(holder // group == home, holder % group, holder ^ position)
    block = place * blocks + mine % blocks
    rank = jnp.sum(block[..., None, :] < block[..., :, None], axis=-1)
    order = jnp.arange(block.shape[-1])
    picks = jnp.sum(jnp.where(rank[..., :, None] == order, block[..., :, None], 0), axis=-2).astype(jnp.int32)
    starts = jnp.sum(block[..., None, :] < (jnp.arange(seq + 1) * blocks)[:, None], axis=-1).astype(jnp.int32)

    half = group + (seq - group) // 2
    most = seq - 1

    def settle(acc, i, out):
        acc = lax.all_to_all(acc, "seq", split_axis=0, concat_axis=0, axis_index_groups=groups, tiled=True)
        acc = delivered(acc, 0)
        for t in range(group):
            out = lax.dynamic_update_slice_in_dim(out, acc[t], (t * own + i) * heads * dim, 1)
        return out

    groups = [list(range(g * group, (g + 1) * group)) for g in range(seq // group)]
    sends = list(pack(mem_keys[0], mem_values[0], at, own, group, dim))
    out = jnp.zeros((rows, width), jnp.bfloat16)
    def ready(i, *first):
        return prepare(
            grad_out[0], queries[0], mem_out[0], logs, after(gates, *[sign(value) for value in first]),
            mem_keys[0], mem_values[0], kv_heads, dim, own, i,
        )

    def shared(mixed):
        return lax.all_to_all(mixed, "seq", split_axis=0, concat_axis=0, axis_index_groups=groups, tiled=True)

    done = None
    coming = shared(ready(0, sends[0]))
    for i in range(own):
        ending = i == own - 1
        mixed = coming
        arrived = {step: swapped(sends[i * group + step % group], step) for step in range(group, seq)}
        run = functools.partial(attend, mixed, heads=heads, dim=dim, mem_dev=mem_dev, scale=scale, picks=picks[i])
        where = starts[i]
        if not ending:
            first = [arrived[step] for step in range(group, half)]
            for step in range(group, half):
                later = (i + 1) * group + step % group
                sends[later] = after(sends[later], sign(arrived[step]))
            coming = ready(i + 1, *first)
            where = after(where, sign(coming), *[sign(value) for value in first])
        if i:
            where = after(where, sign(done))
        acc = run(None, (0, group), None, starts=where, last=False)
        if i:
            out = settle(after(done, sign(acc)), i - 1, out)
        if not ending:
            for step in range(half, seq):
                later = (i + 1) * group + step % group
                sends[later] = after(sends[later], sign(arrived[step]), sign(acc))
            coming = shared(after(coming, sign(acc)))
            done = run([arrived[p] for p in range(group, seq)], (group, seq), acc, starts=where, last=True)
            continue
        acc = run([arrived[p] for p in range(group, half)], (group, half), acc, starts=where, last=False)
        if half < most:
            acc = run([arrived[p] for p in range(half, most)], (half, most), acc, starts=where, last=False)
        for x in range(group):
            only = (at ^ x).astype(jnp.int32)
            piece = run([arrived[most]], (most, seq), acc, starts=where, last=True, only=only)
            piece = delivered(piece[0], x)
            out = lax.dynamic_update_slice_in_dim(out, piece, ((at ^ x) * own + i) * heads * dim, 1)
    return out[None]


def solution(mesh):
    return jax.shard_map(
        shards,
        mesh=mesh,
        in_specs=(
            P("section", "seq", None),
            P("section", "seq", None),
            P("section", "seq", None),
            P("section", "seq", None),
            P("section", None),
            P("section", "seq", None),
            P("section", "seq", None),
            P("section", None, None, None),
        ),
        out_specs=P("section", "seq", None),
        check_vma=False,
    )
```

```python
import functools
import math

import jax
import jax.numpy as jnp
from jax import lax
from jax.experimental import pallas as pl
from jax.experimental.pallas import tpu as pltpu
from jax.sharding import PartitionSpec as P

BLOCK = 128
PARTS = 3
STEP = 4
HINT = 16
VMEM_LIMIT = 48 * 1024 * 1024

NT = (((1,), (1,)), ((), ()))


def split_parts(value):
    terms = []
    for _ in range(PARTS):
        term = value.astype(jnp.bfloat16)
        terms.append(term.astype(jnp.float32))
        value = value - terms[-1]
    return terms


def pack_kernel(own, group, by_distance, at_ref, keys_ref, values_ref, *outs):
    rows = keys_ref.shape[0]
    dim = outs[0].shape[2]
    for x in range(group):
        for index in range(own):
            device = at_ref[0] ^ x if by_distance else x
            column = pl.multiple_of((device * own + index) * dim, dim)
            out, slot = (outs[index * group + x], 0) if by_distance else (outs[index], x)
            out[slot, :rows, :] = keys_ref[:, pl.ds(column, dim)]
            out[slot, rows:, :] = values_ref[:, pl.ds(column, dim)]


def pack(mem_keys, mem_values, at, own, group, dim, by_distance):
    mem_dev, width = mem_keys.shape
    count, slots = (own * group, 1) if by_distance else (own, group)
    whole = pl.BlockSpec((mem_dev, width), lambda i, _: (0, 0))
    return pl.pallas_call(
        functools.partial(pack_kernel, own, group, by_distance),
        out_shape=[jax.ShapeDtypeStruct((slots, 2 * mem_dev, dim), mem_keys.dtype)] * count,
        grid_spec=pltpu.PrefetchScalarGridSpec(
            num_scalar_prefetch=1,
            grid=(1,),
            in_specs=[whole, whole],
            out_specs=[pl.BlockSpec((slots, 2 * mem_dev, dim), lambda i, _: (0, 0, 0))] * count,
        ),
        compiler_params=pltpu.CompilerParams(vmem_limit_bytes=VMEM_LIMIT),
        cost_estimate=pl.CostEstimate(flops=0, bytes_accessed=8 * mem_dev * width, transcendentals=0),
    )(at, mem_keys, mem_values)


def prepare_kernel(heads, dim, scale, own, index, gate_ref, grad_ref, query_ref, out_ref, total_ref, packed_ref):
    rows = grad_ref.shape[0]
    head = pl.program_id(0) * own + index
    count = total_ref.shape[1]
    logs = split_parts(jnp.log2(total_ref[...].astype(jnp.float32)) - math.log2(scale))
    source = lax.broadcasted_iota(jnp.int32, (count, dim), 0) - head * heads
    target = lax.broadcasted_iota(jnp.int32, (count, dim), 1)
    lane = lax.broadcasted_iota(jnp.int32, (rows, dim), 1)
    mine = (source >= 0) & (source < heads)
    stats = jnp.zeros((rows, dim), jnp.float32)
    for part, term in enumerate(logs):
        chosen = jnp.where(mine & (target == source + (2 * part + 1) * heads), 1.0, 0.0).astype(jnp.bfloat16)
        stats += jnp.dot(term.astype(jnp.bfloat16), chosen, preferred_element_type=jnp.float32)
    for h in range(heads):
        columns = slice(h * dim, (h + 1) * dim)
        gated = (gate_ref[head * heads + h] * grad_ref[:, columns].astype(jnp.float32)).astype(jnp.bfloat16)
        packed_ref[0, h * rows:(h + 1) * rows, :] = query_ref[:, columns]
        packed_ref[0, (heads + h) * rows:(heads + h + 1) * rows, :] = gated
        product = gated.astype(jnp.float32) * out_ref[:, columns].astype(jnp.float32)
        delta = jnp.sum(product, axis=1, keepdims=True)
        for part, term in enumerate(split_parts(delta)):
            stats = jnp.where(lane == 2 * part * heads + h, term, stats)
    packed_ref[0, 2 * heads * rows:, :] = stats.astype(jnp.bfloat16)


def prepare(grad_out, queries, mem_out, row_total, gates, kv_heads, dim, scale, own, index):
    rows, width = grad_out.shape
    heads = width // dim // kv_heads
    group = kv_heads // own
    span = 2 * heads * rows + rows
    wide = pl.BlockSpec((rows, heads * dim), lambda k, _: (0, k * own + index))
    return pl.pallas_call(
        functools.partial(prepare_kernel, heads, dim, scale, own, index),
        out_shape=jax.ShapeDtypeStruct((group, span, dim), jnp.bfloat16),
        grid_spec=pltpu.PrefetchScalarGridSpec(
            num_scalar_prefetch=1,
            grid=(group,),
            in_specs=[wide, wide, wide, pl.BlockSpec(row_total.shape, lambda k, _: (0, 0))],
            out_specs=pl.BlockSpec((1, span, dim), lambda k, _: (k, 0, 0)),
        ),
        compiler_params=pltpu.CompilerParams(vmem_limit_bytes=VMEM_LIMIT),
        cost_estimate=pl.CostEstimate(
            flops=rows * width * (4 if index == 0 else 1 << 17), bytes_accessed=rows * width * 12 // own, transcendentals=0
        ),
    )(gates, grad_out, queries, mem_out, row_total)


def attend_kernel(heads, dim, rows, mem_dev, scale, fresh, last, places, local, where_ref, picks_ref, starts_ref, *refs):
    query_ref, stat_ref = refs[:2]
    memory_refs, acc_in = (refs[2:-6], None) if fresh else (refs[2:-7], refs[-7])
    out_ref, keys_ref, values_ref, log_ref, delta_ref, total = refs[-6:]
    step = pl.program_id(0)
    tile = where_ref[0] + step
    blocks = mem_dev // BLOCK
    count = heads * rows

    @pl.when(step == 0)
    def _():
        at = 0
        for number, memory in enumerate(memory_refs):
            for piece in range(memory.shape[0]):
                here = slice(at * mem_dev, (at + 1) * mem_dev)

                def fill(memory=memory, piece=piece, here=here):
                    keys_ref[here, :] = memory[piece, :mem_dev, :]
                    values_ref[here, :] = memory[piece, mem_dev:, :]

                if number == local:
                    pl.when(where_ref[1] != piece)(fill)
                else:
                    fill()
                at += 1

    if fresh:
        total[...] = jnp.zeros_like(total)
    else:
        total[...] = acc_in[0]

    stats = stat_ref[0].astype(jnp.float32)
    for h in range(heads):
        for target, first in ((delta_ref, h), (log_ref, heads + h)):
            terms = [stats[:, first + 2 * part * heads:first + 2 * part * heads + 1] for part in range(PARTS)]
            target[h * rows:(h + 1) * rows, :] = jnp.broadcast_to(terms[0] + terms[1] + terms[2], (rows, dim))

    low = starts_ref[tile, places[0]]
    high = starts_ref[tile, places[1]]
    offset = places[0] * blocks
    exponent = scale * math.log2(math.e)

    def add(here, number, checked):
        sides = []
        for two in range(0, number, 2):
            keys, values = [], []
            for j in (two, two + 1):
                valid = here + j < high
                block = picks_ref[tile, jnp.where(valid, here + j, here) if checked else here + j] - offset
                row = pl.ds(pl.multiple_of(block * BLOCK, BLOCK), BLOCK)
                key = keys_ref[row, :]
                keys.append(jnp.where(valid, key, jnp.zeros_like(key)) if checked and j else key)
                values.append(values_ref[row, :])
            sides.append((jnp.concatenate(keys, axis=0), jnp.concatenate(values, axis=0)))

        def products(side):
            keys, values = side
            scores = lax.dot_general(query_ref[0, :count, :], keys, NT, preferred_element_type=jnp.float32)
            grad_probs = lax.dot_general(query_ref[0, count:, :], values, NT, preferred_element_type=jnp.float32)
            return scores, grad_probs

        ahead = products(sides[0])
        gained = None
        for at, (keys, _) in enumerate(sides):
            scores, grad_probs = ahead
            if at + 1 < len(sides):
                ahead = products(sides[at + 1])
            log_wide = jnp.concatenate([log_ref[...]] * 2, axis=1)
            delta_wide = jnp.concatenate([delta_ref[...]] * 2, axis=1)
            probs = jnp.exp2(scores * exponent - log_wide)
            grad_scores = (probs * (grad_probs - delta_wide)).astype(jnp.bfloat16)
            part = jnp.dot(grad_scores, keys, preferred_element_type=jnp.float32)
            gained = part if gained is None else gained + part
        total[...] += gained

    full = (high - low) // STEP

    def many(turn, carry):
        add(low + STEP * turn, STEP, False)
        return carry

    def few(turn, carry):
        add(low + STEP * full + 2 * turn, 2, True)
        return carry

    lax.fori_loop(0, full, many, 0)
    lax.fori_loop(0, (high - low - STEP * full + 1) // 2, few, 0)

    if last:
        for h in range(heads):
            out_ref[0, :, h * dim:(h + 1) * dim] = total[h * rows:(h + 1) * rows, :].astype(jnp.bfloat16)
    else:
        out_ref[0] = total[...]


def attend(packed, memories, places, acc, at, picks, starts, heads, dim, mem_dev, scale, last, local=None, only=None):
    tiles, span, _ = packed.shape
    rows = span // (2 * heads + 1)
    fresh = acc is None
    count = places[1] - places[0]
    width = heads * rows
    steps = tiles if only is None else 1
    acc_spec = pl.BlockSpec((1, width, dim), lambda t, o, *_: (o[0] + t, 0, 0))
    if last:
        out_shape = jax.ShapeDtypeStruct((steps, rows, heads * dim), jnp.bfloat16)
        out_spec = pl.BlockSpec((1, rows, heads * dim), lambda t, *_: (t, 0, 0))
    else:
        out_shape = jax.ShapeDtypeStruct((tiles, width, dim), jnp.float32)
        out_spec = acc_spec
    flops = steps * count * (mem_dev // 2) * width * dim * 6
    where = jnp.stack([jnp.zeros((), jnp.int32) if only is None else only, at]).astype(jnp.int32)
    return pl.pallas_call(
        functools.partial(attend_kernel, heads, dim, rows, mem_dev, scale, fresh, last, places, local),
        out_shape=out_shape,
        grid_spec=pltpu.PrefetchScalarGridSpec(
            num_scalar_prefetch=3,
            grid=(steps,),
            in_specs=[
                pl.BlockSpec((1, 2 * width, dim), lambda t, o, *_: (o[0] + t, 0, 0)),
                pl.BlockSpec((1, rows, dim), lambda t, o, *_: (o[0] + t, 2 * heads, 0)),
            ]
            + [pl.BlockSpec(m.shape, lambda t, *_: (0, 0, 0)) for m in memories]
            + ([] if fresh else [acc_spec]),
            out_specs=out_spec,
            scratch_shapes=[
                pltpu.VMEM((count * mem_dev, dim), jnp.bfloat16),
                pltpu.VMEM((count * mem_dev, dim), jnp.bfloat16),
                pltpu.VMEM((width, dim), jnp.float32),
                pltpu.VMEM((width, dim), jnp.float32),
                pltpu.VMEM((width, dim), jnp.float32),
            ],
        ),
        compiler_params=pltpu.CompilerParams(vmem_limit_bytes=VMEM_LIMIT),
        cost_estimate=pl.CostEstimate(flops=flops * 4, bytes_accessed=0, transcendentals=0),
    )(where, picks, starts, packed, packed, *memories, *([] if fresh else [acc]))


def after(value, *others):
    anywhere = pl.BlockSpec(memory_space=pl.ANY)
    hints = [other[:1, :HINT] for other in others]
    return pl.pallas_call(
        lambda *refs: None,
        out_shape=jax.ShapeDtypeStruct(value.shape, value.dtype),
        in_specs=[anywhere] * (1 + len(hints)),
        out_specs=anywhere,
        input_output_aliases={0: 0},
        cost_estimate=pl.CostEstimate(flops=0, bytes_accessed=0, transcendentals=0),
    )(value, *hints)


def shards(grad_out, queries, mem_out, row_total, gate_logit, mem_keys, mem_values, retrieved):
    seq = lax.axis_size("seq")
    sections = lax.axis_size("section")
    position = lax.axis_index("seq")
    rows, width = grad_out.shape[1:]
    head_count = gate_logit.shape[1]
    dim = width // head_count
    kv_heads = mem_keys.shape[2] // dim
    heads = head_count // kv_heads
    mem_dev = mem_keys.shape[1]
    blocks = mem_dev // BLOCK
    group = min(kv_heads, seq // 2)
    own = kv_heads // group
    at = position % group
    home = position // group
    scale = dim ** (-0.5)
    groups = [list(range(g * group, (g + 1) * group)) for g in range(seq // group)]

    def swapped(value, step):
        return lax.ppermute(value, "seq", [(p, p ^ step) for p in range(seq)])

    def delivered(value, step):
        pairs = [(s * seq + p, ((s - 1) % sections) * seq + (p ^ step)) for s in range(sections) for p in range(seq)]
        return lax.ppermute(value, ("section", "seq"), pairs)

    def shared(value):
        return lax.all_to_all(value, "seq", split_axis=0, concat_axis=0, axis_index_groups=groups, tiled=True)

    half = group + (seq - group) // 2
    near = 1 + half - group
    far = near + group
    end = far + seq - half
    mine = lax.dynamic_slice_in_dim(retrieved[0], at * own, own, 0)
    mine = lax.dynamic_slice_in_dim(mine, home * group, group, 1)
    holder = mine // blocks
    distance = holder ^ position
    place = jnp.where(
        holder == position, 0,
        jnp.where(
            holder // group == home, near + holder % group,
            jnp.where(distance < half, 1 + distance - group, far + distance - half),
        ),
    )
    block = place * blocks + mine % blocks
    rank = jnp.sum(block[..., None, :] < block[..., :, None], axis=-1)
    order = jnp.arange(block.shape[-1])
    picks = jnp.sum(jnp.where(rank[..., :, None] == order, block[..., :, None], 0), axis=-2).astype(jnp.int32)
    starts = jnp.sum(block[..., None, :] < (jnp.arange(end + 1) * blocks)[:, None], axis=-1).astype(jnp.int32)

    keys, values = mem_keys[0], mem_values[0]
    sends = list(pack(keys, values, at[None], own, group, dim, True))
    gates = jax.nn.sigmoid(gate_logit[0])

    def ready(i, *first):
        return prepare(
            grad_out[0], queries[0], mem_out[0], row_total[0], after(gates, *first), kv_heads, dim, scale, own, i
        )

    packed = shared(ready(0, sends[0]))
    locals_of = list(pack(keys, values, after(at[None], sends[0]), own, group, dim, False))
    nearby = shared(after(locals_of[0], packed))
    out = jnp.zeros((rows, width), jnp.bfloat16)
    arrived, finished, done = {}, [], None
    for i in range(own):
        ending = i == own - 1
        for step in range(group, seq):
            piece = sends[i * group + step % group]
            ahead = step - (half - group) if step >= half else step + (half - group)
            if ahead in arrived:
                piece = after(piece, arrived[ahead])
            arrived[step] = swapped(piece, step)
        first = [arrived[step] for step in range(group, half)]
        second = [arrived[step] for step in range(half, seq)]
        run = functools.partial(
            attend, packed, at=at, picks=picks[i], heads=heads, dim=dim, mem_dev=mem_dev, scale=scale
        )
        where = starts[i]
        if not ending:
            coming = ready(i + 1, *first)
            where = after(where, coming)
        if i:
            where = after(where, done)
        acc = run([sends[i * group]] + first, (0, near), None, starts=where, last=False)
        if not ending:
            done = run([nearby] + second, (near, end), acc, starts=where, last=True, local=0)
            finished.append(delivered(done, 0))
            packed = shared(after(coming, nearby))
            nearby = shared(after(locals_of[i + 1], packed))
            continue
        acc = run([nearby], (near, far), acc, starts=where, last=False, local=0)
        for j, result in enumerate(finished):
            result = shared(after(result, nearby))
            for t in range(group):
                out = lax.dynamic_update_slice_in_dim(out, result[t], (t * own + j) * heads * dim, 1)
        for x in range(group):
            piece = run(second, (far, end), acc, starts=where, last=True, only=at ^ x)
            piece = delivered(piece[0], x)
            out = lax.dynamic_update_slice_in_dim(out, piece, ((at ^ x) * own + i) * heads * dim, 1)
    return out[None]


def solution(mesh):
    return jax.shard_map(
        shards,
        mesh=mesh,
        in_specs=(
            P("section", "seq", None),
            P("section", "seq", None),
            P("section", "seq", None),
            P("section", "seq", None),
            P("section", None),
            P("section", "seq", None),
            P("section", "seq", None),
            P("section", None, None, None),
        ),
        out_specs=P("section", "seq", None),
        check_vma=False,
    )
```

```python
import functools
import math

import jax
import jax.numpy as jnp
from jax import lax
from jax.experimental import pallas as pl
from jax.experimental.pallas import tpu as pltpu
from jax.sharding import PartitionSpec as P

BLOCK = 128
PARTS = 3
STEP = 4
MOST = 1 << 10
HINT = 16
VMEM_LIMIT = 48 * 1024 * 1024

NT = (((1,), (1,)), ((), ()))


def split_parts(value):
    terms = []
    for _ in range(PARTS):
        term = value.astype(jnp.bfloat16)
        terms.append(term.astype(jnp.float32))
        value = value - terms[-1]
    return terms


def pack_kernel(own, group, cuts, keys_ref, values_ref, *outs):
    dim = outs[0].shape[2]
    at = 0
    for index, pieces in enumerate(cuts):
        for low, high in pieces:
            out = outs[at]
            at += 1
            rows = (high - low) * BLOCK
            for device in range(out.shape[0]):
                head = device % group * own + index
                for half, source in enumerate((keys_ref, values_ref)):
                    out[device, half * rows:(half + 1) * rows, :] = source[
                        low * BLOCK:high * BLOCK, head * dim:(head + 1) * dim
                    ]


def pack(mem_keys, mem_values, seq, own, group, dim, cuts):
    mem_dev, width = mem_keys.shape
    whole = pl.BlockSpec((mem_dev, width), lambda i: (0, 0))
    shapes = [(seq, 2 * (high - low) * BLOCK, dim) for pieces in cuts for low, high in pieces]
    return pl.pallas_call(
        functools.partial(pack_kernel, own, group, cuts),
        out_shape=[jax.ShapeDtypeStruct(shape, mem_keys.dtype) for shape in shapes],
        grid=(1,),
        in_specs=[whole, whole],
        out_specs=[pl.BlockSpec(shape, lambda i: (0, 0, 0)) for shape in shapes],
        compiler_params=pltpu.CompilerParams(vmem_limit_bytes=VMEM_LIMIT),
        cost_estimate=pl.CostEstimate(flops=0, bytes_accessed=8 * mem_dev * width, transcendentals=0),
    )(mem_keys, mem_values)


def prepare_kernel(heads, dim, scale, own, index, gate_ref, at_ref, grad_ref, query_ref, out_ref, total_ref, *packed_refs):
    rows = grad_ref.shape[0]
    count = total_ref.shape[1]
    logs = split_parts(jnp.log2(total_ref[...].astype(jnp.float32)) - math.log2(scale))
    target = lax.broadcasted_iota(jnp.int32, (count, dim), 1)
    lane = lax.broadcasted_iota(jnp.int32, (rows, dim), 1)
    for x, packed_ref in enumerate(packed_refs):
        head = (at_ref[0] ^ x) * own + index
        source = lax.broadcasted_iota(jnp.int32, (count, dim), 0) - head * heads
        mine = (source >= 0) & (source < heads)
        stats = jnp.zeros((rows, dim), jnp.float32)
        for part, term in enumerate(logs):
            chosen = jnp.where(mine & (target == source + (2 * part + 1) * heads), 1.0, 0.0).astype(jnp.bfloat16)
            stats += jnp.dot(term.astype(jnp.bfloat16), chosen, preferred_element_type=jnp.float32)
        for h in range(heads):
            columns = pl.ds(pl.multiple_of((head * heads + h) * dim, dim), dim)
            gated = (gate_ref[head * heads + h] * grad_ref[:, columns].astype(jnp.float32)).astype(jnp.bfloat16)
            packed_ref[h * rows:(h + 1) * rows, :] = query_ref[:, columns]
            packed_ref[(heads + h) * rows:(heads + h + 1) * rows, :] = gated
            product = gated.astype(jnp.float32) * out_ref[:, columns].astype(jnp.float32)
            delta = jnp.sum(product, axis=1, keepdims=True)
            for part, term in enumerate(split_parts(delta)):
                stats = jnp.where(lane == 2 * part * heads + h, term, stats)
        packed_ref[2 * heads * rows:, :] = stats.astype(jnp.bfloat16)


def prepare(grad_out, queries, mem_out, row_total, gates, at, kv_heads, dim, scale, own, index):
    rows, width = grad_out.shape
    heads = width // dim // kv_heads
    group = kv_heads // own
    span = 2 * heads * rows + rows
    wide = pl.BlockSpec((rows, width), lambda i, *_: (0, 0))
    return pl.pallas_call(
        functools.partial(prepare_kernel, heads, dim, scale, own, index),
        out_shape=[jax.ShapeDtypeStruct((span, dim), jnp.bfloat16)] * group,
        grid_spec=pltpu.PrefetchScalarGridSpec(
            num_scalar_prefetch=2,
            grid=(1,),
            in_specs=[wide, wide, wide, pl.BlockSpec(row_total.shape, lambda i, *_: (0, 0))],
            out_specs=[pl.BlockSpec((span, dim), lambda i, *_: (0, 0))] * group,
        ),
        compiler_params=pltpu.CompilerParams(vmem_limit_bytes=VMEM_LIMIT),
        cost_estimate=pl.CostEstimate(flops=rows * width * 4, bytes_accessed=rows * width * 12 // own, transcendentals=0),
    )(gates, at[None], grad_out, queries, mem_out, row_total)


def attend_kernel(heads, dim, rows, scale, fresh, last, first, picks_ref, starts_ref, query_ref, stat_ref, memory_ref, *refs):
    acc_in = None if fresh else refs[0]
    out_ref, log_ref, delta_ref, total = refs[-4:]
    tile = first + pl.program_id(0)
    blocks = memory_ref.shape[1] // 2
    count = heads * rows

    if fresh:
        total[...] = jnp.zeros_like(total)
    else:
        total[...] = acc_in[0]

    stats = stat_ref[0].astype(jnp.float32)
    for h in range(heads):
        for target, first in ((delta_ref, h), (log_ref, heads + h)):
            terms = [stats[:, first + 2 * part * heads:first + 2 * part * heads + 1] for part in range(PARTS)]
            target[h * rows:(h + 1) * rows, :] = jnp.broadcast_to(terms[0] + terms[1] + terms[2], (rows, dim))

    low = starts_ref[tile, 0]
    high = starts_ref[tile, 1]
    exponent = scale * math.log2(math.e)

    def add(here, number, checked):
        sides = []
        for two in range(0, number, 2):
            keys, values = [], []
            for j in (two, two + 1):
                valid = here + j < high
                pick = picks_ref[tile, jnp.where(valid, here + j, here) if checked else here + j]
                holder = pick // MOST
                block = pick % MOST
                key = memory_ref[holder, block]
                keys.append(jnp.where(valid, key, jnp.zeros_like(key)) if checked and j else key)
                values.append(memory_ref[holder, blocks + block])
            sides.append((jnp.concatenate(keys, axis=0), jnp.concatenate(values, axis=0)))

        def products(side):
            keys, values = side
            scores = lax.dot_general(query_ref[0, :count, :], keys, NT, preferred_element_type=jnp.float32)
            grad_probs = lax.dot_general(query_ref[0, count:, :], values, NT, preferred_element_type=jnp.float32)
            return scores, grad_probs

        ahead = products(sides[0])
        gained = None
        for at, (keys, _) in enumerate(sides):
            scores, grad_probs = ahead
            if at + 1 < len(sides):
                ahead = products(sides[at + 1])
            log_wide = jnp.concatenate([log_ref[...]] * 2, axis=1)
            delta_wide = jnp.concatenate([delta_ref[...]] * 2, axis=1)
            probs = jnp.exp2(scores * exponent - log_wide)
            grad_scores = (probs * (grad_probs - delta_wide)).astype(jnp.bfloat16)
            part = jnp.dot(grad_scores, keys, preferred_element_type=jnp.float32)
            gained = part if gained is None else gained + part
        total[...] += gained

    full = (high - low) // STEP

    def many(turn, carry):
        add(low + STEP * turn, STEP, False)
        return carry

    def few(turn, carry):
        add(low + STEP * full + 2 * turn, 2, True)
        return carry

    lax.fori_loop(0, full, many, 0)
    lax.fori_loop(0, (high - low - STEP * full + 1) // 2, few, 0)

    if last:
        for h in range(heads):
            out_ref[0, :, h * dim:(h + 1) * dim] = total[h * rows:(h + 1) * rows, :].astype(jnp.bfloat16)
    else:
        out_ref[0] = total[...]


def attend(packed, memory, acc, picks, starts, heads, dim, scale, last, only=None):
    tiles, span, _ = packed.shape
    rows = span // (2 * heads + 1)
    fresh = acc is None
    width = heads * rows
    holders = memory.shape[0]
    memory = memory.reshape(holders, -1, BLOCK, dim)
    steps, first = (tiles, 0) if only is None else (1, only)
    acc_spec = pl.BlockSpec((1, width, dim), lambda t, *_: (first + t, 0, 0))
    if last:
        out_shape = jax.ShapeDtypeStruct((steps, rows, heads * dim), jnp.bfloat16)
        out_spec = pl.BlockSpec((1, rows, heads * dim), lambda t, *_: (t, 0, 0))
    else:
        out_shape = jax.ShapeDtypeStruct((tiles, width, dim), jnp.float32)
        out_spec = acc_spec
    flops = steps * holders * (memory.shape[1] // 4) * BLOCK * width * dim * 6
    return pl.pallas_call(
        functools.partial(attend_kernel, heads, dim, rows, scale, fresh, last, first),
        out_shape=out_shape,
        grid_spec=pltpu.PrefetchScalarGridSpec(
            num_scalar_prefetch=2,
            grid=(steps,),
            in_specs=[
                pl.BlockSpec((1, 2 * width, dim), lambda t, *_: (first + t, 0, 0)),
                pl.BlockSpec((1, rows, dim), lambda t, *_: (first + t, 2 * heads, 0)),
                pl.BlockSpec(memory.shape, lambda t, *_: (0, 0, 0, 0)),
            ]
            + ([] if fresh else [acc_spec]),
            out_specs=out_spec,
            scratch_shapes=[pltpu.VMEM((width, dim), jnp.float32)] * 3,
        ),
        compiler_params=pltpu.CompilerParams(vmem_limit_bytes=VMEM_LIMIT),
        cost_estimate=pl.CostEstimate(flops=flops * 4, bytes_accessed=0, transcendentals=0),
    )(picks, starts, packed, packed, memory, *([] if fresh else [acc]))


def after(value, *others):
    anywhere = pl.BlockSpec(memory_space=pl.ANY)
    corners = [pl.BlockSpec((HINT, other.shape[1]), lambda i: (0, 0)) for other in others]
    return pl.pallas_call(
        lambda *refs: None,
        out_shape=jax.ShapeDtypeStruct(value.shape, value.dtype),
        grid=(1,),
        in_specs=[anywhere] + corners,
        out_specs=anywhere,
        input_output_aliases={0: 0},
        cost_estimate=pl.CostEstimate(flops=0, bytes_accessed=0, transcendentals=0),
    )(value, *others)


def shards(grad_out, queries, mem_out, row_total, gate_logit, mem_keys, mem_values, retrieved):
    seq = lax.axis_size("seq")
    sections = lax.axis_size("section")
    position = lax.axis_index("seq")
    rows, width = grad_out.shape[1:]
    head_count = gate_logit.shape[1]
    dim = width // head_count
    kv_heads = mem_keys.shape[2] // dim
    heads = head_count // kv_heads
    mem_dev = mem_keys.shape[1]
    blocks = mem_dev // BLOCK
    group = min(kv_heads, seq // 2)
    own = kv_heads // group
    at = position % group
    home = position // group
    scale = dim ** (-0.5)

    def swapped(value, step):
        return lax.ppermute(value, "seq", [(p, p ^ step) for p in range(seq)])

    def delivered(value, step):
        pairs = [(s * seq + p, ((s - 1) % sections) * seq + (p ^ step)) for s in range(sections) for p in range(seq)]
        return lax.ppermute(value, ("section", "seq"), pairs)

    cut = (5 * blocks + 7) // 8
    cuts = [[(0, blocks)]] * (own - 1) + [[(0, cut), (cut, blocks)]]

    def listed(i):
        mine = lax.dynamic_index_in_dim(retrieved[0], at * own + i, 0, keepdims=False)
        mine = jnp.stack(
            [lax.dynamic_index_in_dim(mine, home * group + (at ^ x), 0, keepdims=False) for x in range(group)]
        )
        holder, block = mine // blocks, mine % blocks
        piece = sum((block >= low).astype(jnp.int32) for low, _ in cuts[i][1:]) if len(cuts[i]) > 1 else 0 * block
        key = piece * seq * blocks + mine
        rank = jnp.sum(key[:, None, :] < key[:, :, None], axis=-1)
        order = jnp.arange(mine.shape[-1])
        low = sum((piece == j) * cuts[i][j][0] for j in range(len(cuts[i])))
        value = holder * MOST + block - low
        picks = jnp.sum(jnp.where(rank[:, :, None] == order, value[:, :, None], 0), axis=1).astype(jnp.int32)
        bounds = [jnp.sum(piece < j, axis=-1) for j in range(len(cuts[i]) + 1)]
        return picks, [
            jnp.stack([bounds[j], bounds[j + 1]], axis=1).astype(jnp.int32) for j in range(len(cuts[i]))
        ]

    gates = jax.nn.sigmoid(gate_logit[0])
    memories = list(pack(mem_keys[0], mem_values[0], seq, own, group, dim, cuts))
    out = jnp.zeros((rows, width), jnp.bfloat16)
    before = []
    for i in range(own):
        pieces = []
        for _ in cuts[i]:
            piece = memories.pop(0)
            pieces.append(lax.all_to_all(piece, "seq", split_axis=0, concat_axis=0, tiled=True))
        packed = prepare(grad_out[0], queries[0], mem_out[0], row_total[0], gates, at, kv_heads, dim, scale, own, i)
        packed = jnp.stack([packed[0]] + [swapped(packed[x], x) for x in range(1, group)])
        picks, starts = listed(i)
        run = functools.partial(attend, packed, picks=picks, heads=heads, dim=dim, scale=scale)
        acc = None
        for j in range(len(pieces) - 1):
            acc = run(pieces[j], acc, starts=starts[j], last=False)
        ending = i == own - 1
        if ending:
            bounds = after(starts[-1], *before) if before else starts[-1]
            results = [run(pieces[-1], acc, starts=bounds, last=True, only=x)[0] for x in range(group)]
        else:
            results = list(run(pieces[-1], acc, starts=starts[-1], last=True))
        for x in range(group):
            result = delivered(results[x], x)
            if not ending:
                before.append(result)
            out = lax.dynamic_update_slice_in_dim(out, result, ((at ^ x) * own + i) * heads * dim, 1)
    return out[None]


def solution(mesh):
    return jax.shard_map(
        shards,
        mesh=mesh,
        in_specs=(
            P("section", "seq", None),
            P("section", "seq", None),
            P("section", "seq", None),
            P("section", "seq", None),
            P("section", None),
            P("section", "seq", None),
            P("section", "seq", None),
            P("section", None, None, None),
        ),
        out_specs=P("section", "seq", None),
        check_vma=False,
    )
```

```python
import functools
import math

import jax
import jax.numpy as jnp
from jax import lax
from jax.experimental import pallas as pl
from jax.experimental.pallas import tpu as pltpu
from jax.sharding import PartitionSpec as P

BLOCK = 128
PARTS = 3
STEP = 4
MOST = 1 << 10
HINT = 16
VMEM_LIMIT = 48 * 1024 * 1024

NT = (((1,), (1,)), ((), ()))


def split_parts(value):
    terms = []
    for _ in range(PARTS):
        term = value.astype(jnp.bfloat16)
        terms.append(term.astype(jnp.float32))
        value = value - terms[-1]
    return terms


def pack_kernel(own, group, cuts, keys_ref, values_ref, *outs):
    dim = outs[0].shape[2]
    at = 0
    for index, pieces in enumerate(cuts):
        for low, high in pieces:
            out = outs[at]
            at += 1
            rows = (high - low) * BLOCK
            for device in range(out.shape[0]):
                head = device % group * own + index
                for half, source in enumerate((keys_ref, values_ref)):
                    out[device, half * rows:(half + 1) * rows, :] = source[
                        low * BLOCK:high * BLOCK, head * dim:(head + 1) * dim
                    ]


def pack(mem_keys, mem_values, seq, own, group, dim, cuts):
    mem_dev, width = mem_keys.shape
    whole = pl.BlockSpec((mem_dev, width), lambda i: (0, 0))
    shapes = [(seq, 2 * (high - low) * BLOCK, dim) for pieces in cuts for low, high in pieces]
    return pl.pallas_call(
        functools.partial(pack_kernel, own, group, cuts),
        out_shape=[jax.ShapeDtypeStruct(shape, mem_keys.dtype) for shape in shapes],
        grid=(1,),
        in_specs=[whole, whole],
        out_specs=[pl.BlockSpec(shape, lambda i: (0, 0, 0)) for shape in shapes],
        compiler_params=pltpu.CompilerParams(vmem_limit_bytes=VMEM_LIMIT),
        cost_estimate=pl.CostEstimate(flops=0, bytes_accessed=8 * mem_dev * width, transcendentals=0),
    )(mem_keys, mem_values)


def prepare_kernel(heads, dim, scale, own, index, gate_ref, at_ref, grad_ref, query_ref, out_ref, total_ref, *packed_refs):
    rows = grad_ref.shape[0]
    count = total_ref.shape[1]
    logs = split_parts(jnp.log2(total_ref[...].astype(jnp.float32)) - math.log2(scale))
    target = lax.broadcasted_iota(jnp.int32, (count, dim), 1)
    lane = lax.broadcasted_iota(jnp.int32, (rows, dim), 1)
    for x, packed_ref in enumerate(packed_refs):
        head = (at_ref[0] ^ x) * own + index
        source = lax.broadcasted_iota(jnp.int32, (count, dim), 0) - head * heads
        mine = (source >= 0) & (source < heads)
        stats = jnp.zeros((rows, dim), jnp.float32)
        for part, term in enumerate(logs):
            chosen = jnp.where(mine & (target == source + (2 * part + 1) * heads), 1.0, 0.0).astype(jnp.bfloat16)
            stats += jnp.dot(term.astype(jnp.bfloat16), chosen, preferred_element_type=jnp.float32)
        for h in range(heads):
            columns = pl.ds(pl.multiple_of((head * heads + h) * dim, dim), dim)
            gated = (gate_ref[head * heads + h] * grad_ref[:, columns].astype(jnp.float32)).astype(jnp.bfloat16)
            packed_ref[h * rows:(h + 1) * rows, :] = query_ref[:, columns]
            packed_ref[(heads + h) * rows:(heads + h + 1) * rows, :] = gated
            product = gated.astype(jnp.float32) * out_ref[:, columns].astype(jnp.float32)
            delta = jnp.sum(product, axis=1, keepdims=True)
            for part, term in enumerate(split_parts(delta)):
                stats = jnp.where(lane == 2 * part * heads + h, term, stats)
        packed_ref[2 * heads * rows:, :] = stats.astype(jnp.bfloat16)


def prepare(grad_out, queries, mem_out, row_total, gates, at, kv_heads, dim, scale, own, index):
    rows, width = grad_out.shape
    heads = width // dim // kv_heads
    group = kv_heads // own
    span = 2 * heads * rows + rows
    wide = pl.BlockSpec((rows, width), lambda i, *_: (0, 0))
    return pl.pallas_call(
        functools.partial(prepare_kernel, heads, dim, scale, own, index),
        out_shape=[jax.ShapeDtypeStruct((span, dim), jnp.bfloat16)] * group,
        grid_spec=pltpu.PrefetchScalarGridSpec(
            num_scalar_prefetch=2,
            grid=(1,),
            in_specs=[wide, wide, wide, pl.BlockSpec(row_total.shape, lambda i, *_: (0, 0))],
            out_specs=[pl.BlockSpec((span, dim), lambda i, *_: (0, 0))] * group,
        ),
        compiler_params=pltpu.CompilerParams(vmem_limit_bytes=VMEM_LIMIT),
        cost_estimate=pl.CostEstimate(flops=rows * width * 4, bytes_accessed=rows * width * 12 // own, transcendentals=0),
    )(gates, at[None], grad_out, queries, mem_out, row_total)


def attend_kernel(heads, dim, rows, scale, fresh, last, first, picks_ref, starts_ref, query_ref, stat_ref, memory_ref, *refs):
    acc_in = None if fresh else refs[0]
    out_ref, log_ref, delta_ref, total = refs[-4:]
    tile = first + pl.program_id(0)
    blocks = memory_ref.shape[1] // 2
    count = heads * rows

    if fresh:
        total[...] = jnp.zeros_like(total)
    else:
        total[...] = acc_in[0]

    stats = stat_ref[0].astype(jnp.float32)
    for h in range(heads):
        for target, first in ((delta_ref, h), (log_ref, heads + h)):
            terms = [stats[:, first + 2 * part * heads:first + 2 * part * heads + 1] for part in range(PARTS)]
            target[h * rows:(h + 1) * rows, :] = jnp.broadcast_to(terms[0] + terms[1] + terms[2], (rows, dim))

    low = starts_ref[tile, 0]
    high = starts_ref[tile, 1]
    exponent = scale * math.log2(math.e)

    def add(here, number, checked):
        sides = []
        for two in range(0, number, 2):
            keys, values = [], []
            for j in (two, two + 1):
                valid = here + j < high
                pick = picks_ref[tile, jnp.where(valid, here + j, here) if checked else here + j]
                holder = pick // MOST
                block = pick % MOST
                key = memory_ref[holder, block]
                keys.append(jnp.where(valid, key, jnp.zeros_like(key)) if checked and j else key)
                values.append(memory_ref[holder, blocks + block])
            sides.append((jnp.concatenate(keys, axis=0), jnp.concatenate(values, axis=0)))

        def products(side):
            keys, values = side
            scores = lax.dot_general(query_ref[0, :count, :], keys, NT, preferred_element_type=jnp.float32)
            grad_probs = lax.dot_general(query_ref[0, count:, :], values, NT, preferred_element_type=jnp.float32)
            return scores, grad_probs

        ahead = products(sides[0])
        gained = None
        for at, (keys, _) in enumerate(sides):
            scores, grad_probs = ahead
            if at + 1 < len(sides):
                ahead = products(sides[at + 1])
            log_wide = jnp.concatenate([log_ref[...]] * 2, axis=1)
            delta_wide = jnp.concatenate([delta_ref[...]] * 2, axis=1)
            probs = jnp.exp2(scores * exponent - log_wide)
            grad_scores = (probs * (grad_probs - delta_wide)).astype(jnp.bfloat16)
            part = jnp.dot(grad_scores, keys, preferred_element_type=jnp.float32)
            gained = part if gained is None else gained + part
        total[...] += gained

    full = (high - low) // STEP

    def many(turn, carry):
        add(low + STEP * turn, STEP, False)
        return carry

    def few(turn, carry):
        add(low + STEP * full + 2 * turn, 2, True)
        return carry

    lax.fori_loop(0, full, many, 0)
    lax.fori_loop(0, (high - low - STEP * full + 1) // 2, few, 0)

    if last:
        for h in range(heads):
            out_ref[0, :, h * dim:(h + 1) * dim] = total[h * rows:(h + 1) * rows, :].astype(jnp.bfloat16)
    else:
        out_ref[0] = total[...]


def attend(packed, memory, acc, picks, starts, heads, dim, scale, last, only=None):
    tiles, span, _ = packed.shape
    rows = span // (2 * heads + 1)
    fresh = acc is None
    width = heads * rows
    holders = memory.shape[0]
    memory = memory.reshape(holders, -1, BLOCK, dim)
    steps, first = (tiles, 0) if only is None else (1, only)
    acc_spec = pl.BlockSpec((1, width, dim), lambda t, *_: (first + t, 0, 0))
    if last:
        out_shape = jax.ShapeDtypeStruct((steps, rows, heads * dim), jnp.bfloat16)
        out_spec = pl.BlockSpec((1, rows, heads * dim), lambda t, *_: (t, 0, 0))
    else:
        out_shape = jax.ShapeDtypeStruct((tiles, width, dim), jnp.float32)
        out_spec = acc_spec
    flops = steps * holders * (memory.shape[1] // 4) * BLOCK * width * dim * 6
    return pl.pallas_call(
        functools.partial(attend_kernel, heads, dim, rows, scale, fresh, last, first),
        out_shape=out_shape,
        grid_spec=pltpu.PrefetchScalarGridSpec(
            num_scalar_prefetch=2,
            grid=(steps,),
            in_specs=[
                pl.BlockSpec((1, 2 * width, dim), lambda t, *_: (first + t, 0, 0)),
                pl.BlockSpec((1, rows, dim), lambda t, *_: (first + t, 2 * heads, 0)),
                pl.BlockSpec(memory.shape, lambda t, *_: (0, 0, 0, 0)),
            ]
            + ([] if fresh else [acc_spec]),
            out_specs=out_spec,
            scratch_shapes=[pltpu.VMEM((width, dim), jnp.float32)] * 3,
        ),
        compiler_params=pltpu.CompilerParams(vmem_limit_bytes=VMEM_LIMIT),
        cost_estimate=pl.CostEstimate(flops=flops * 4, bytes_accessed=0, transcendentals=0),
    )(picks, starts, packed, packed, memory, *([] if fresh else [acc]))


def after(value, *others):
    anywhere = pl.BlockSpec(memory_space=pl.ANY)
    corners = [
        pl.BlockSpec((1,) * (other.ndim - 2) + (HINT, 128), lambda i, count=other.ndim: (0,) * count) for other in others
    ]
    return pl.pallas_call(
        lambda *refs: None,
        out_shape=jax.ShapeDtypeStruct(value.shape, value.dtype),
        grid=(1,),
        in_specs=[anywhere] + corners,
        out_specs=anywhere,
        input_output_aliases={0: 0},
        cost_estimate=pl.CostEstimate(flops=0, bytes_accessed=0, transcendentals=0),
    )(value, *others)


def shards(grad_out, queries, mem_out, row_total, gate_logit, mem_keys, mem_values, retrieved):
    seq = lax.axis_size("seq")
    sections = lax.axis_size("section")
    position = lax.axis_index("seq")
    rows, width = grad_out.shape[1:]
    head_count = gate_logit.shape[1]
    dim = width // head_count
    kv_heads = mem_keys.shape[2] // dim
    heads = head_count // kv_heads
    mem_dev = mem_keys.shape[1]
    blocks = mem_dev // BLOCK
    group = min(kv_heads, seq // 2)
    own = kv_heads // group
    at = position % group
    home = position // group
    scale = dim ** (-0.5)

    def swapped(value, step):
        return lax.ppermute(value, "seq", [(p, p ^ step) for p in range(seq)])

    def delivered(value, step):
        pairs = [(s * seq + p, ((s - 1) % sections) * seq + (p ^ step)) for s in range(sections) for p in range(seq)]
        return lax.ppermute(value, ("section", "seq"), pairs)

    cut = (3 * blocks + 3) // 4
    cuts = [[(0, blocks)]] * (own - 1) + [[(0, cut), (cut, blocks)]]

    def listed(i):
        mine = lax.dynamic_index_in_dim(retrieved[0], at * own + i, 0, keepdims=False)
        mine = jnp.stack(
            [lax.dynamic_index_in_dim(mine, home * group + (at ^ x), 0, keepdims=False) for x in range(group)]
        )
        holder, block = mine // blocks, mine % blocks
        piece = sum((block >= low).astype(jnp.int32) for low, _ in cuts[i][1:]) if len(cuts[i]) > 1 else 0 * block
        key = piece * seq * blocks + mine
        rank = jnp.sum(key[:, None, :] < key[:, :, None], axis=-1)
        order = jnp.arange(mine.shape[-1])
        low = sum((piece == j) * cuts[i][j][0] for j in range(len(cuts[i])))
        value = holder * MOST + block - low
        picks = jnp.sum(jnp.where(rank[:, :, None] == order, value[:, :, None], 0), axis=1).astype(jnp.int32)
        bounds = [jnp.sum(piece < j, axis=-1) for j in range(len(cuts[i]) + 1)]
        return picks, [
            jnp.stack([bounds[j], bounds[j + 1]], axis=1).astype(jnp.int32) for j in range(len(cuts[i]))
        ]

    gates = jax.nn.sigmoid(gate_logit[0])
    memories = list(pack(mem_keys[0], mem_values[0], seq, own, group, dim, cuts))
    out = jnp.zeros((rows, width), jnp.bfloat16)
    before, worked, latest = [], [], None
    for i in range(own):
        opened = gates if latest is None else after(gates, latest)
        packed = prepare(grad_out[0], queries[0], mem_out[0], row_total[0], opened, at, kv_heads, dim, scale, own, i)
        packed = jnp.stack([packed[0]] + [swapped(packed[x], x) for x in range(1, group)])
        pieces = []
        for _ in cuts[i]:
            piece = memories.pop(0)
            piece = piece if latest is None else after(piece, latest)
            latest = lax.all_to_all(piece, "seq", split_axis=0, concat_axis=0, tiled=True)
            pieces.append(latest)
        picks, starts = listed(i)
        run = functools.partial(attend, packed, picks=picks, heads=heads, dim=dim, scale=scale)
        acc = None
        for j in range(len(pieces) - 1):
            acc = run(pieces[j], acc, starts=after(starts[j], *worked), last=False)
            worked = [acc]
        results = []
        if i < own - 1:
            done = run(pieces[-1], acc, starts=after(starts[-1], *worked), last=True)
            worked = [done]
            results = [delivered(done[x], x) for x in range(group)]
            before += results
        else:
            for x in range(group):
                ready = before if x == 0 else results[x - 2:x - 1] if x > 1 else []
                done = run(pieces[-1], acc, starts=after(starts[-1], *worked, *ready), last=True, only=x)
                worked = [done]
                results.append(delivered(done[0], x))
        for x, result in enumerate(results):
            out = lax.dynamic_update_slice_in_dim(out, result, ((at ^ x) * own + i) * heads * dim, 1)
    return out[None]


def solution(mesh):
    return jax.shard_map(
        shards,
        mesh=mesh,
        in_specs=(
            P("section", "seq", None),
            P("section", "seq", None),
            P("section", "seq", None),
            P("section", "seq", None),
            P("section", None),
            P("section", "seq", None),
            P("section", "seq", None),
            P("section", None, None, None),
        ),
        out_specs=P("section", "seq", None),
        check_vma=False,
    )
```

```python
import functools
import math

import jax
import jax.numpy as jnp
from jax import lax
from jax.experimental import pallas as pl
from jax.experimental.pallas import tpu as pltpu
from jax.sharding import PartitionSpec as P

BLOCK = 128
PARTS = 3
STEP = 4
MOST = 1 << 10
HINT = 16
VMEM_LIMIT = 48 * 1024 * 1024
VMEM_MOST = 60 * 1024 * 1024

NT = (((1,), (1,)), ((), ()))


def split_parts(value):
    terms = []
    for _ in range(PARTS):
        term = value.astype(jnp.bfloat16)
        terms.append(term.astype(jnp.float32))
        value = value - terms[-1]
    return terms


def pack_kernel(own, group, cuts, keys_ref, values_ref, *outs):
    dim = outs[0].shape[2]
    at = 0
    for index, pieces in enumerate(cuts):
        for low, high in pieces:
            out = outs[at]
            at += 1
            rows = (high - low) * BLOCK
            for device in range(out.shape[0]):
                head = device % group * own + index
                for half, source in enumerate((keys_ref, values_ref)):
                    out[device, half * rows:(half + 1) * rows, :] = source[
                        low * BLOCK:high * BLOCK, head * dim:(head + 1) * dim
                    ]


def pack(mem_keys, mem_values, seq, own, group, dim, cuts):
    mem_dev, width = mem_keys.shape
    whole = pl.BlockSpec((mem_dev, width), lambda i: (0, 0))
    shapes = [(seq, 2 * (high - low) * BLOCK, dim) for pieces in cuts for low, high in pieces]
    return pl.pallas_call(
        functools.partial(pack_kernel, own, group, cuts),
        out_shape=[jax.ShapeDtypeStruct(shape, mem_keys.dtype) for shape in shapes],
        grid=(1,),
        in_specs=[whole, whole],
        out_specs=[pl.BlockSpec(shape, lambda i: (0, 0, 0)) for shape in shapes],
        compiler_params=pltpu.CompilerParams(vmem_limit_bytes=VMEM_LIMIT),
        cost_estimate=pl.CostEstimate(flops=0, bytes_accessed=8 * mem_dev * width, transcendentals=0),
    )(mem_keys, mem_values)


def prepare_kernel(heads, dim, scale, own, index, gate_ref, at_ref, grad_ref, query_ref, out_ref, total_ref, *packed_refs):
    rows = grad_ref.shape[0]
    count = total_ref.shape[1]
    logs = split_parts(jnp.log2(total_ref[...].astype(jnp.float32)) - math.log2(scale))
    target = lax.broadcasted_iota(jnp.int32, (count, dim), 1)
    lane = lax.broadcasted_iota(jnp.int32, (rows, dim), 1)
    for x, packed_ref in enumerate(packed_refs):
        head = (at_ref[0] ^ x) * own + index
        source = lax.broadcasted_iota(jnp.int32, (count, dim), 0) - head * heads
        mine = (source >= 0) & (source < heads)
        stats = jnp.zeros((rows, dim), jnp.float32)
        for part, term in enumerate(logs):
            chosen = jnp.where(mine & (target == source + (2 * part + 1) * heads), 1.0, 0.0).astype(jnp.bfloat16)
            stats += jnp.dot(term.astype(jnp.bfloat16), chosen, preferred_element_type=jnp.float32)
        for h in range(heads):
            columns = pl.ds(pl.multiple_of((head * heads + h) * dim, dim), dim)
            gated = (gate_ref[head * heads + h] * grad_ref[:, columns].astype(jnp.float32)).astype(jnp.bfloat16)
            packed_ref[h * rows:(h + 1) * rows, :] = query_ref[:, columns]
            packed_ref[(heads + h) * rows:(heads + h + 1) * rows, :] = gated
            product = gated.astype(jnp.float32) * out_ref[:, columns].astype(jnp.float32)
            delta = jnp.sum(product, axis=1, keepdims=True)
            for part, term in enumerate(split_parts(delta)):
                stats = jnp.where(lane == 2 * part * heads + h, term, stats)
        packed_ref[2 * heads * rows:, :] = stats.astype(jnp.bfloat16)


def prepare(grad_out, queries, mem_out, row_total, gates, at, kv_heads, dim, scale, own, index):
    rows, width = grad_out.shape
    heads = width // dim // kv_heads
    group = kv_heads // own
    span = 2 * heads * rows + rows
    wide = pl.BlockSpec((rows, width), lambda i, *_: (0, 0))
    return pl.pallas_call(
        functools.partial(prepare_kernel, heads, dim, scale, own, index),
        out_shape=[jax.ShapeDtypeStruct((span, dim), jnp.bfloat16)] * group,
        grid_spec=pltpu.PrefetchScalarGridSpec(
            num_scalar_prefetch=2,
            grid=(1,),
            in_specs=[wide, wide, wide, pl.BlockSpec(row_total.shape, lambda i, *_: (0, 0))],
            out_specs=[pl.BlockSpec((span, dim), lambda i, *_: (0, 0))] * group,
        ),
        compiler_params=pltpu.CompilerParams(vmem_limit_bytes=VMEM_LIMIT),
        cost_estimate=pl.CostEstimate(flops=rows * width * 4, bytes_accessed=rows * width * 12 // own, transcendentals=0),
    )(gates, at[None], grad_out, queries, mem_out, row_total)


def attend_kernel(heads, dim, rows, scale, fresh, last, first, picks_ref, starts_ref, query_ref, stat_ref, memory_ref, *refs):
    acc_in = None if fresh else refs[0]
    out_ref, log_ref, delta_ref, total = refs[-4:]
    tile = first + pl.program_id(0)
    blocks = memory_ref.shape[1] // 2
    count = heads * rows

    if fresh:
        total[...] = jnp.zeros_like(total)
    else:
        total[...] = acc_in[0]

    stats = stat_ref[0].astype(jnp.float32)
    for h in range(heads):
        for target, first in ((delta_ref, h), (log_ref, heads + h)):
            terms = [stats[:, first + 2 * part * heads:first + 2 * part * heads + 1] for part in range(PARTS)]
            target[h * rows:(h + 1) * rows, :] = jnp.broadcast_to(terms[0] + terms[1] + terms[2], (rows, dim))

    low = starts_ref[tile, 0]
    high = starts_ref[tile, 1]
    exponent = scale * math.log2(math.e)

    def add(here, number, checked):
        sides = []
        for two in range(0, number, 2):
            keys, values = [], []
            for j in (two, two + 1):
                valid = here + j < high
                pick = picks_ref[tile, jnp.where(valid, here + j, here) if checked else here + j]
                holder = pick // MOST
                block = pick % MOST
                key = memory_ref[holder, block]
                keys.append(jnp.where(valid, key, jnp.zeros_like(key)) if checked and j else key)
                values.append(memory_ref[holder, blocks + block])
            sides.append((jnp.concatenate(keys, axis=0), jnp.concatenate(values, axis=0)))

        def products(side):
            keys, values = side
            scores = lax.dot_general(query_ref[0, :count, :], keys, NT, preferred_element_type=jnp.float32)
            grad_probs = lax.dot_general(query_ref[0, count:, :], values, NT, preferred_element_type=jnp.float32)
            return scores, grad_probs

        ahead = products(sides[0])
        gained = None
        for at, (keys, _) in enumerate(sides):
            scores, grad_probs = ahead
            if at + 1 < len(sides):
                ahead = products(sides[at + 1])
            log_wide = jnp.concatenate([log_ref[...]] * 2, axis=1)
            delta_wide = jnp.concatenate([delta_ref[...]] * 2, axis=1)
            probs = jnp.exp2(scores * exponent - log_wide)
            grad_scores = (probs * (grad_probs - delta_wide)).astype(jnp.bfloat16)
            part = jnp.dot(grad_scores, keys, preferred_element_type=jnp.float32)
            gained = part if gained is None else gained + part
        total[...] += gained

    full = (high - low) // STEP

    def many(turn, carry):
        add(low + STEP * turn, STEP, False)
        return carry

    def few(turn, carry):
        add(low + STEP * full + 2 * turn, 2, True)
        return carry

    lax.fori_loop(0, full, many, 0)
    lax.fori_loop(0, (high - low - STEP * full + 1) // 2, few, 0)

    if last:
        for h in range(heads):
            out_ref[0, :, h * dim:(h + 1) * dim] = total[h * rows:(h + 1) * rows, :].astype(jnp.bfloat16)
    else:
        out_ref[0] = total[...]


def attend(packed, memory, acc, picks, starts, heads, dim, scale, last, only=None):
    tiles, span, _ = packed.shape
    rows = span // (2 * heads + 1)
    fresh = acc is None
    width = heads * rows
    holders = memory.shape[0]
    memory = memory.reshape(holders, -1, BLOCK, dim)
    steps, first = (tiles, 0) if only is None else (1, only)
    acc_spec = pl.BlockSpec((1, width, dim), lambda t, *_: (first + t, 0, 0))
    if last:
        out_shape = jax.ShapeDtypeStruct((steps, rows, heads * dim), jnp.bfloat16)
        out_spec = pl.BlockSpec((1, rows, heads * dim), lambda t, *_: (t, 0, 0))
    else:
        out_shape = jax.ShapeDtypeStruct((tiles, width, dim), jnp.float32)
        out_spec = acc_spec
    flops = steps * holders * (memory.shape[1] // 4) * BLOCK * width * dim * 6
    return pl.pallas_call(
        functools.partial(attend_kernel, heads, dim, rows, scale, fresh, last, first),
        out_shape=out_shape,
        grid_spec=pltpu.PrefetchScalarGridSpec(
            num_scalar_prefetch=2,
            grid=(steps,),
            in_specs=[
                pl.BlockSpec((1, 2 * width, dim), lambda t, *_: (first + t, 0, 0)),
                pl.BlockSpec((1, rows, dim), lambda t, *_: (first + t, 2 * heads, 0)),
                pl.BlockSpec(memory.shape, lambda t, *_: (0, 0, 0, 0)),
            ]
            + ([] if fresh else [acc_spec]),
            out_specs=out_spec,
            scratch_shapes=[pltpu.VMEM((width, dim), jnp.float32)] * 3,
        ),
        compiler_params=pltpu.CompilerParams(vmem_limit_bytes=VMEM_MOST),
        cost_estimate=pl.CostEstimate(flops=flops * 4, bytes_accessed=0, transcendentals=0),
    )(picks, starts, packed, packed, memory, *([] if fresh else [acc]))


def assemble_kernel(own, group, at_ref, *refs):
    pieces, out_ref = refs[:-1], refs[-1]
    span = pieces[0].shape[1]
    for index in range(own):
        for x in range(group):
            column = pl.multiple_of(((at_ref[0] ^ x) * own + index) * span, span)
            out_ref[:, pl.ds(column, span)] = pieces[index * group + x][...]


def assemble(pieces, at, own, group):
    rows, span = pieces[0].shape
    width = own * group * span
    return pl.pallas_call(
        functools.partial(assemble_kernel, own, group),
        out_shape=jax.ShapeDtypeStruct((rows, width), pieces[0].dtype),
        grid_spec=pltpu.PrefetchScalarGridSpec(
            num_scalar_prefetch=1,
            grid=(1,),
            in_specs=[pl.BlockSpec((rows, span), lambda i, _: (0, 0))] * len(pieces),
            out_specs=pl.BlockSpec((rows, width), lambda i, _: (0, 0)),
        ),
        compiler_params=pltpu.CompilerParams(vmem_limit_bytes=VMEM_LIMIT),
        cost_estimate=pl.CostEstimate(flops=0, bytes_accessed=4 * rows * width, transcendentals=0),
    )(at[None], *pieces)


def after(value, *others):
    anywhere = pl.BlockSpec(memory_space=pl.ANY)
    corners = [
        pl.BlockSpec((1,) * (other.ndim - 2) + (HINT, 128), lambda i, count=other.ndim: (0,) * count) for other in others
    ]
    return pl.pallas_call(
        lambda *refs: None,
        out_shape=jax.ShapeDtypeStruct(value.shape, value.dtype),
        grid=(1,),
        in_specs=[anywhere] + corners,
        out_specs=anywhere,
        input_output_aliases={0: 0},
        cost_estimate=pl.CostEstimate(flops=0, bytes_accessed=0, transcendentals=0),
    )(value, *others)


def shards(grad_out, queries, mem_out, row_total, gate_logit, mem_keys, mem_values, retrieved):
    seq = lax.axis_size("seq")
    sections = lax.axis_size("section")
    position = lax.axis_index("seq")
    rows, width = grad_out.shape[1:]
    head_count = gate_logit.shape[1]
    dim = width // head_count
    kv_heads = mem_keys.shape[2] // dim
    heads = head_count // kv_heads
    mem_dev = mem_keys.shape[1]
    blocks = mem_dev // BLOCK
    group = min(kv_heads, seq // 2)
    own = kv_heads // group
    at = position % group
    home = position // group
    scale = dim ** (-0.5)

    def swapped(value, step):
        return lax.ppermute(value, "seq", [(p, p ^ step) for p in range(seq)])

    def delivered(value, step):
        pairs = [(s * seq + p, ((s - 1) % sections) * seq + (p ^ step)) for s in range(sections) for p in range(seq)]
        return lax.ppermute(value, ("section", "seq"), pairs)

    cut = (3 * blocks + 3) // 4
    cuts = [[(0, blocks)]] * (own - 1) + [[(0, cut), (cut, blocks)]]

    def listed(i):
        mine = lax.dynamic_index_in_dim(retrieved[0], at * own + i, 0, keepdims=False)
        mine = jnp.stack(
            [lax.dynamic_index_in_dim(mine, home * group + (at ^ x), 0, keepdims=False) for x in range(group)]
        )
        holder, block = mine // blocks, mine % blocks
        piece = sum((block >= low).astype(jnp.int32) for low, _ in cuts[i][1:]) if len(cuts[i]) > 1 else 0 * block
        key = piece * seq * blocks + mine
        rank = jnp.sum(key[:, None, :] < key[:, :, None], axis=-1)
        order = jnp.arange(mine.shape[-1])
        low = sum((piece == j) * cuts[i][j][0] for j in range(len(cuts[i])))
        value = holder * MOST + block - low
        picks = jnp.sum(jnp.where(rank[:, :, None] == order, value[:, :, None], 0), axis=1).astype(jnp.int32)
        bounds = [jnp.sum(piece < j, axis=-1) for j in range(len(cuts[i]) + 1)]
        return picks, [
            jnp.stack([bounds[j], bounds[j + 1]], axis=1).astype(jnp.int32) for j in range(len(cuts[i]))
        ]

    gates = jax.nn.sigmoid(gate_logit[0])
    memories = list(pack(mem_keys[0], mem_values[0], seq, own, group, dim, cuts))
    gathered, worked, latest = [], [], None

    def queries_of(i):
        opened = gates if latest is None else after(gates, latest)
        packed = prepare(grad_out[0], queries[0], mem_out[0], row_total[0], opened, at, kv_heads, dim, scale, own, i)
        return [packed[0]] + [swapped(packed[x], x) for x in range(1, group)]

    coming = queries_of(0)
    for i in range(own):
        packed = jnp.stack(coming)
        pieces = []
        for _ in cuts[i]:
            piece = memories.pop(0)
            piece = piece if latest is None else after(piece, latest)
            latest = lax.all_to_all(piece, "seq", split_axis=0, concat_axis=0, tiled=True)
            pieces.append(latest)
        picks, starts = listed(i)
        run = functools.partial(attend, packed, picks=picks, heads=heads, dim=dim, scale=scale)
        acc = None
        for j in range(len(pieces) - 1):
            acc = run(pieces[j], acc, starts=after(starts[j], *worked), last=False)
            worked = [acc]
        results = []
        if i < own - 1:
            coming = queries_of(i + 1)
            done = run(pieces[-1], acc, starts=after(starts[-1], *worked), last=True)
            worked = [done]
            done = after(done, *coming)
            results = [delivered(done[x], x) for x in range(group)]
        else:
            for x in range(group):
                ready = gathered if x == 0 else results[x - 2:x - 1] if x > 1 else []
                done = run(pieces[-1], acc, starts=after(starts[-1], *worked, *ready), last=True, only=x)
                worked = [done]
                results.append(delivered(done[0], x))
        gathered = gathered + results
    return assemble(gathered, at, own, group)[None]


def solution(mesh):
    return jax.shard_map(
        shards,
        mesh=mesh,
        in_specs=(
            P("section", "seq", None),
            P("section", "seq", None),
            P("section", "seq", None),
            P("section", "seq", None),
            P("section", None),
            P("section", "seq", None),
            P("section", "seq", None),
            P("section", None, None, None),
        ),
        out_specs=P("section", "seq", None),
        check_vma=False,
    )
```

```python
import functools
import math

import jax
import jax.numpy as jnp
from jax import lax
from jax.experimental import pallas as pl
from jax.experimental.pallas import tpu as pltpu
from jax.sharding import PartitionSpec as P

BLOCK = 128
PARTS = 3
STEP = 4
MOST = 1 << 10
HINT = 16
VMEM_LIMIT = 48 * 1024 * 1024
VMEM_MOST = 60 * 1024 * 1024

NT = (((1,), (1,)), ((), ()))


def split_parts(value):
    terms = []
    for _ in range(PARTS):
        term = value.astype(jnp.bfloat16)
        terms.append(term.astype(jnp.float32))
        value = value - terms[-1]
    return terms


def pack_kernel(own, group, cuts, keys_ref, values_ref, *outs):
    dim = outs[0].shape[2]
    at = 0
    for index, pieces in enumerate(cuts):
        for low, high in pieces:
            out = outs[at]
            at += 1
            rows = (high - low) * BLOCK
            for device in range(out.shape[0]):
                head = device % group * own + index
                for half, source in enumerate((keys_ref, values_ref)):
                    out[device, half * rows:(half + 1) * rows, :] = source[
                        low * BLOCK:high * BLOCK, head * dim:(head + 1) * dim
                    ]


def pack(mem_keys, mem_values, seq, own, group, dim, cuts):
    mem_dev, width = mem_keys.shape
    whole = pl.BlockSpec((mem_dev, width), lambda i: (0, 0))
    shapes = [(seq, 2 * (high - low) * BLOCK, dim) for pieces in cuts for low, high in pieces]
    return pl.pallas_call(
        functools.partial(pack_kernel, own, group, cuts),
        out_shape=[jax.ShapeDtypeStruct(shape, mem_keys.dtype) for shape in shapes],
        grid=(1,),
        in_specs=[whole, whole],
        out_specs=[pl.BlockSpec(shape, lambda i: (0, 0, 0)) for shape in shapes],
        compiler_params=pltpu.CompilerParams(vmem_limit_bytes=VMEM_LIMIT),
        cost_estimate=pl.CostEstimate(flops=0, bytes_accessed=8 * mem_dev * width, transcendentals=0),
    )(mem_keys, mem_values)


def prepare_kernel(heads, dim, scale, own, index, gate_ref, at_ref, grad_ref, query_ref, out_ref, total_ref, *packed_refs):
    rows = grad_ref.shape[0]
    count = total_ref.shape[1]
    logs = split_parts(jnp.log2(total_ref[...].astype(jnp.float32)) - math.log2(scale))
    target = lax.broadcasted_iota(jnp.int32, (count, dim), 1)
    lane = lax.broadcasted_iota(jnp.int32, (rows, dim), 1)
    for x, packed_ref in enumerate(packed_refs):
        head = (at_ref[0] ^ x) * own + index
        source = lax.broadcasted_iota(jnp.int32, (count, dim), 0) - head * heads
        mine = (source >= 0) & (source < heads)
        stats = jnp.zeros((rows, dim), jnp.float32)
        for part, term in enumerate(logs):
            chosen = jnp.where(mine & (target == source + (2 * part + 1) * heads), 1.0, 0.0).astype(jnp.bfloat16)
            stats += jnp.dot(term.astype(jnp.bfloat16), chosen, preferred_element_type=jnp.float32)
        for h in range(heads):
            columns = pl.ds(pl.multiple_of((head * heads + h) * dim, dim), dim)
            gated = (gate_ref[head * heads + h] * grad_ref[:, columns].astype(jnp.float32)).astype(jnp.bfloat16)
            packed_ref[h * rows:(h + 1) * rows, :] = query_ref[:, columns]
            packed_ref[(heads + h) * rows:(heads + h + 1) * rows, :] = gated
            product = gated.astype(jnp.float32) * out_ref[:, columns].astype(jnp.float32)
            delta = jnp.sum(product, axis=1, keepdims=True)
            for part, term in enumerate(split_parts(delta)):
                stats = jnp.where(lane == 2 * part * heads + h, term, stats)
        packed_ref[2 * heads * rows:, :] = stats.astype(jnp.bfloat16)


def prepare(grad_out, queries, mem_out, row_total, gates, at, kv_heads, dim, scale, own, index):
    rows, width = grad_out.shape
    heads = width // dim // kv_heads
    group = kv_heads // own
    span = 2 * heads * rows + rows
    wide = pl.BlockSpec((rows, width), lambda i, *_: (0, 0))
    return pl.pallas_call(
        functools.partial(prepare_kernel, heads, dim, scale, own, index),
        out_shape=[jax.ShapeDtypeStruct((span, dim), jnp.bfloat16)] * group,
        grid_spec=pltpu.PrefetchScalarGridSpec(
            num_scalar_prefetch=2,
            grid=(1,),
            in_specs=[wide, wide, wide, pl.BlockSpec(row_total.shape, lambda i, *_: (0, 0))],
            out_specs=[pl.BlockSpec((span, dim), lambda i, *_: (0, 0))] * group,
        ),
        compiler_params=pltpu.CompilerParams(vmem_limit_bytes=VMEM_LIMIT),
        cost_estimate=pl.CostEstimate(flops=rows * width * 4, bytes_accessed=rows * width * 12 // own, transcendentals=0),
    )(gates, at[None], grad_out, queries, mem_out, row_total)


def attend_kernel(heads, dim, rows, scale, tiles, fresh, last, picks_ref, starts_ref, *refs):
    packed_refs, memory_ref = refs[:tiles], refs[tiles]
    acc_in = None if fresh else refs[tiles + 1]
    out_ref, query_ref, log_ref, delta_ref, total = refs[-5:]
    tile = pl.program_id(0)
    blocks = memory_ref.shape[1] // 2
    count = heads * rows

    if fresh:
        total[...] = jnp.zeros_like(total)
    else:
        total[...] = acc_in[0]

    for x, packed in enumerate(packed_refs):

        @pl.when(tile == x)
        def _(packed=packed):
            query_ref[...] = packed[...]

    stats = query_ref[2 * count:, :].astype(jnp.float32)
    for h in range(heads):
        for target, first in ((delta_ref, h), (log_ref, heads + h)):
            terms = [stats[:, first + 2 * part * heads:first + 2 * part * heads + 1] for part in range(PARTS)]
            target[h * rows:(h + 1) * rows, :] = jnp.broadcast_to(terms[0] + terms[1] + terms[2], (rows, dim))

    low = starts_ref[tile, 0]
    high = starts_ref[tile, 1]
    exponent = scale * math.log2(math.e)

    def add(here, number, checked):
        sides = []
        for two in range(0, number, 2):
            keys, values = [], []
            for j in (two, two + 1):
                valid = here + j < high
                pick = picks_ref[tile, jnp.where(valid, here + j, here) if checked else here + j]
                holder = pick // MOST
                block = pick % MOST
                key = memory_ref[holder, block]
                keys.append(jnp.where(valid, key, jnp.zeros_like(key)) if checked and j else key)
                values.append(memory_ref[holder, blocks + block])
            sides.append((jnp.concatenate(keys, axis=0), jnp.concatenate(values, axis=0)))

        def products(side):
            keys, values = side
            scores = lax.dot_general(query_ref[:count, :], keys, NT, preferred_element_type=jnp.float32)
            grad_probs = lax.dot_general(query_ref[count:2 * count, :], values, NT, preferred_element_type=jnp.float32)
            return scores, grad_probs

        ahead = products(sides[0])
        gained = None
        for at, (keys, _) in enumerate(sides):
            scores, grad_probs = ahead
            if at + 1 < len(sides):
                ahead = products(sides[at + 1])
            log_wide = jnp.concatenate([log_ref[...]] * 2, axis=1)
            delta_wide = jnp.concatenate([delta_ref[...]] * 2, axis=1)
            probs = jnp.exp2(scores * exponent - log_wide)
            grad_scores = (probs * (grad_probs - delta_wide)).astype(jnp.bfloat16)
            part = jnp.dot(grad_scores, keys, preferred_element_type=jnp.float32)
            gained = part if gained is None else gained + part
        total[...] += gained

    full = (high - low) // STEP

    def many(turn, carry):
        add(low + STEP * turn, STEP, False)
        return carry

    def few(turn, carry):
        add(low + STEP * full + 2 * turn, 2, True)
        return carry

    lax.fori_loop(0, full, many, 0)
    lax.fori_loop(0, (high - low - STEP * full + 1) // 2, few, 0)

    if last:
        for h in range(heads):
            out_ref[0, :, h * dim:(h + 1) * dim] = total[h * rows:(h + 1) * rows, :].astype(jnp.bfloat16)
    else:
        out_ref[0] = total[...]


def attend(packed, memory, acc, picks, starts, heads, dim, scale, last):
    tiles = len(packed)
    span = packed[0].shape[0]
    rows = span // (2 * heads + 1)
    fresh = acc is None
    width = heads * rows
    holders = memory.shape[0]
    memory = memory.reshape(holders, -1, BLOCK, dim)
    acc_spec = pl.BlockSpec((1, width, dim), lambda t, *_: (t, 0, 0))
    if last:
        out_shape = jax.ShapeDtypeStruct((tiles, rows, heads * dim), jnp.bfloat16)
        out_spec = pl.BlockSpec((1, rows, heads * dim), lambda t, *_: (t, 0, 0))
    else:
        out_shape = jax.ShapeDtypeStruct((tiles, width, dim), jnp.float32)
        out_spec = acc_spec
    flops = tiles * holders * memory.shape[1] * (BLOCK // 4) * width * dim * 6
    return pl.pallas_call(
        functools.partial(attend_kernel, heads, dim, rows, scale, tiles, fresh, last),
        out_shape=out_shape,
        grid_spec=pltpu.PrefetchScalarGridSpec(
            num_scalar_prefetch=2,
            grid=(tiles,),
            in_specs=[pl.BlockSpec((span, dim), lambda t, *_: (0, 0))] * tiles
            + [pl.BlockSpec(memory.shape, lambda t, *_: (0, 0, 0, 0))]
            + ([] if fresh else [acc_spec]),
            out_specs=out_spec,
            scratch_shapes=[pltpu.VMEM((span, dim), jnp.bfloat16)] + [pltpu.VMEM((width, dim), jnp.float32)] * 3,
        ),
        compiler_params=pltpu.CompilerParams(vmem_limit_bytes=VMEM_MOST),
        cost_estimate=pl.CostEstimate(flops=flops * 4, bytes_accessed=0, transcendentals=0),
    )(picks, starts, *packed, memory, *([] if fresh else [acc]))


def assemble_kernel(own, group, at_ref, *refs):
    pieces, out_ref = refs[:-1], refs[-1]
    span = pieces[0].shape[1]
    for index in range(own):
        for x in range(group):
            column = pl.multiple_of(((at_ref[0] ^ x) * own + index) * span, span)
            out_ref[:, pl.ds(column, span)] = pieces[index * group + x][...]


def assemble(pieces, at, own, group):
    rows, span = pieces[0].shape
    width = own * group * span
    return pl.pallas_call(
        functools.partial(assemble_kernel, own, group),
        out_shape=jax.ShapeDtypeStruct((rows, width), pieces[0].dtype),
        grid_spec=pltpu.PrefetchScalarGridSpec(
            num_scalar_prefetch=1,
            grid=(1,),
            in_specs=[pl.BlockSpec((rows, span), lambda i, _: (0, 0))] * len(pieces),
            out_specs=pl.BlockSpec((rows, width), lambda i, _: (0, 0)),
        ),
        compiler_params=pltpu.CompilerParams(vmem_limit_bytes=VMEM_LIMIT),
        cost_estimate=pl.CostEstimate(flops=0, bytes_accessed=4 * rows * width, transcendentals=0),
    )(at[None], *pieces)


def after(value, *others):
    anywhere = pl.BlockSpec(memory_space=pl.ANY)
    corners = [
        pl.BlockSpec((1,) * (other.ndim - 2) + (HINT, 128), lambda i, count=other.ndim: (0,) * count) for other in others
    ]
    return pl.pallas_call(
        lambda *refs: None,
        out_shape=jax.ShapeDtypeStruct(value.shape, value.dtype),
        grid=(1,),
        in_specs=[anywhere] + corners,
        out_specs=anywhere,
        input_output_aliases={0: 0},
        cost_estimate=pl.CostEstimate(flops=0, bytes_accessed=0, transcendentals=0),
    )(value, *others)


def shards(grad_out, queries, mem_out, row_total, gate_logit, mem_keys, mem_values, retrieved):
    seq = lax.axis_size("seq")
    sections = lax.axis_size("section")
    position = lax.axis_index("seq")
    rows, width = grad_out.shape[1:]
    head_count = gate_logit.shape[1]
    dim = width // head_count
    kv_heads = mem_keys.shape[2] // dim
    heads = head_count // kv_heads
    mem_dev = mem_keys.shape[1]
    blocks = mem_dev // BLOCK
    group = min(kv_heads, seq // 2)
    own = kv_heads // group
    at = position % group
    home = position // group
    scale = dim ** (-0.5)

    def swapped(value, step):
        return lax.ppermute(value, "seq", [(p, p ^ step) for p in range(seq)])

    def delivered(value, step):
        pairs = [(s * seq + p, ((s - 1) % sections) * seq + (p ^ step)) for s in range(sections) for p in range(seq)]
        return lax.ppermute(value, ("section", "seq"), pairs)

    marks = [0, (blocks + 1) // 2, blocks - max(blocks // 8, 1), blocks]
    cuts = [[(0, blocks)]] * (own - 1) + [list(zip(marks[:-1], marks[1:]))]

    def listed(i):
        mine = lax.dynamic_index_in_dim(retrieved[0], at * own + i, 0, keepdims=False)
        mine = jnp.stack(
            [lax.dynamic_index_in_dim(mine, home * group + (at ^ x), 0, keepdims=False) for x in range(group)]
        )
        holder, block = mine // blocks, mine % blocks
        piece = sum((block >= low).astype(jnp.int32) for low, _ in cuts[i][1:]) if len(cuts[i]) > 1 else 0 * block
        key = piece * seq * blocks + mine
        rank = jnp.sum(key[:, None, :] < key[:, :, None], axis=-1)
        order = jnp.arange(mine.shape[-1])
        low = sum((piece == j) * cuts[i][j][0] for j in range(len(cuts[i])))
        value = holder * MOST + block - low
        picks = jnp.sum(jnp.where(rank[:, :, None] == order, value[:, :, None], 0), axis=1).astype(jnp.int32)
        bounds = [jnp.sum(piece < j, axis=-1) for j in range(len(cuts[i]) + 1)]
        return picks, [
            jnp.stack([bounds[j], bounds[j + 1]], axis=1).astype(jnp.int32) for j in range(len(cuts[i]))
        ]

    gates = jax.nn.sigmoid(gate_logit[0])
    memories = list(pack(mem_keys[0], mem_values[0], seq, own, group, dim, cuts))
    gathered, worked, latest = [], [], None

    def queries_of(i):
        opened = gates if latest is None else after(gates, latest)
        packed = prepare(grad_out[0], queries[0], mem_out[0], row_total[0], opened, at, kv_heads, dim, scale, own, i)
        return [packed[0]] + [swapped(packed[x], x) for x in range(1, group)]

    coming = queries_of(0)
    for i in range(own):
        packed = coming
        pieces = []
        for _ in cuts[i]:
            piece = memories.pop(0)
            piece = piece if latest is None else after(piece, latest)
            latest = lax.all_to_all(piece, "seq", split_axis=0, concat_axis=0, tiled=True)
            pieces.append(latest)
        picks, starts = listed(i)
        run = functools.partial(attend, packed, picks=picks, heads=heads, dim=dim, scale=scale)
        acc = None
        for j in range(len(pieces) - 1):
            acc = run(pieces[j], acc, starts=after(starts[j], *worked), last=False)
            worked = [acc]
        if i < own - 1:
            coming = queries_of(i + 1)
        ready = [] if i < own - 1 else gathered
        done = run(pieces[-1], acc, starts=after(starts[-1], *worked, *ready), last=True)
        worked = [done]
        if i < own - 1:
            done = after(done, *coming)
        results = [delivered(done[x], x) for x in range(group)]
        gathered = gathered + results
    return assemble(gathered, at, own, group)[None]


def solution(mesh):
    return jax.shard_map(
        shards,
        mesh=mesh,
        in_specs=(
            P("section", "seq", None),
            P("section", "seq", None),
            P("section", "seq", None),
            P("section", "seq", None),
            P("section", None),
            P("section", "seq", None),
            P("section", "seq", None),
            P("section", None, None, None),
        ),
        out_specs=P("section", "seq", None),
        check_vma=False,
    )
```

```python
import functools
import math

import jax
import jax.numpy as jnp
from jax import lax
from jax.experimental import pallas as pl
from jax.experimental.pallas import tpu as pltpu
from jax.sharding import PartitionSpec as P

BLOCK = 128
PARTS = 3
STEP = 4
MOST = 1 << 10
HINT = 16
VMEM_LIMIT = 48 * 1024 * 1024
VMEM_MOST = 60 * 1024 * 1024

NT = (((1,), (1,)), ((), ()))


def split_parts(value):
    terms = []
    for _ in range(PARTS):
        term = value.astype(jnp.bfloat16)
        terms.append(term.astype(jnp.float32))
        value = value - terms[-1]
    return terms


def pack_kernel(own, group, cuts, keys_ref, values_ref, *outs):
    dim = outs[0].shape[2]
    at = 0
    for index, pieces in enumerate(cuts):
        for low, high in pieces:
            out = outs[at]
            at += 1
            rows = (high - low) * BLOCK
            for device in range(out.shape[0]):
                head = device % group * own + index
                for half, source in enumerate((keys_ref, values_ref)):
                    out[device, half * rows:(half + 1) * rows, :] = source[
                        low * BLOCK:high * BLOCK, head * dim:(head + 1) * dim
                    ]


def pack(mem_keys, mem_values, seq, own, group, dim, cuts):
    mem_dev, width = mem_keys.shape
    whole = pl.BlockSpec((mem_dev, width), lambda i: (0, 0))
    shapes = [(seq, 2 * (high - low) * BLOCK, dim) for pieces in cuts for low, high in pieces]
    return pl.pallas_call(
        functools.partial(pack_kernel, own, group, cuts),
        out_shape=[jax.ShapeDtypeStruct(shape, mem_keys.dtype) for shape in shapes],
        grid=(1,),
        in_specs=[whole, whole],
        out_specs=[pl.BlockSpec(shape, lambda i: (0, 0, 0)) for shape in shapes],
        compiler_params=pltpu.CompilerParams(vmem_limit_bytes=VMEM_LIMIT),
        cost_estimate=pl.CostEstimate(flops=0, bytes_accessed=8 * mem_dev * width, transcendentals=0),
    )(mem_keys, mem_values)


def prepare_kernel(heads, dim, scale, own, index, gate_ref, at_ref, grad_ref, query_ref, out_ref, total_ref, *packed_refs):
    rows = grad_ref.shape[0]
    count = total_ref.shape[1]
    logs = split_parts(jnp.log2(total_ref[...].astype(jnp.float32)) - math.log2(scale))
    target = lax.broadcasted_iota(jnp.int32, (count, dim), 1)
    lane = lax.broadcasted_iota(jnp.int32, (rows, dim), 1)
    for x, packed_ref in enumerate(packed_refs):
        head = (at_ref[0] ^ x) * own + index
        source = lax.broadcasted_iota(jnp.int32, (count, dim), 0) - head * heads
        mine = (source >= 0) & (source < heads)
        stats = jnp.zeros((rows, dim), jnp.float32)
        for part, term in enumerate(logs):
            chosen = jnp.where(mine & (target == source + (2 * part + 1) * heads), 1.0, 0.0).astype(jnp.bfloat16)
            stats += jnp.dot(term.astype(jnp.bfloat16), chosen, preferred_element_type=jnp.float32)
        for h in range(heads):
            columns = pl.ds(pl.multiple_of((head * heads + h) * dim, dim), dim)
            gated = (gate_ref[head * heads + h] * grad_ref[:, columns].astype(jnp.float32)).astype(jnp.bfloat16)
            packed_ref[h * rows:(h + 1) * rows, :] = query_ref[:, columns]
            packed_ref[(heads + h) * rows:(heads + h + 1) * rows, :] = gated
            product = gated.astype(jnp.float32) * out_ref[:, columns].astype(jnp.float32)
            delta = jnp.sum(product, axis=1, keepdims=True)
            for part, term in enumerate(split_parts(delta)):
                stats = jnp.where(lane == 2 * part * heads + h, term, stats)
        packed_ref[2 * heads * rows:, :] = stats.astype(jnp.bfloat16)


def prepare(grad_out, queries, mem_out, row_total, gates, at, kv_heads, dim, scale, own, index):
    rows, width = grad_out.shape
    heads = width // dim // kv_heads
    group = kv_heads // own
    span = 2 * heads * rows + rows
    wide = pl.BlockSpec((rows, width), lambda i, *_: (0, 0))
    return pl.pallas_call(
        functools.partial(prepare_kernel, heads, dim, scale, own, index),
        out_shape=[jax.ShapeDtypeStruct((span, dim), jnp.bfloat16)] * group,
        grid_spec=pltpu.PrefetchScalarGridSpec(
            num_scalar_prefetch=2,
            grid=(1,),
            in_specs=[wide, wide, wide, pl.BlockSpec(row_total.shape, lambda i, *_: (0, 0))],
            out_specs=[pl.BlockSpec((span, dim), lambda i, *_: (0, 0))] * group,
        ),
        compiler_params=pltpu.CompilerParams(vmem_limit_bytes=VMEM_LIMIT),
        cost_estimate=pl.CostEstimate(flops=rows * width * 4, bytes_accessed=rows * width * 12 // own, transcendentals=0),
    )(gates, at[None], grad_out, queries, mem_out, row_total)


def attend_kernel(heads, dim, rows, scale, tiles, fresh, last, picks_ref, starts_ref, *refs):
    packed_refs, memory_ref = refs[:tiles], refs[tiles]
    acc_in = None if fresh else refs[tiles + 1]
    out_refs, (query_ref, log_ref, delta_ref, total) = refs[tiles + (1 if fresh else 2):-4], refs[-4:]
    tile = pl.program_id(0)
    blocks = memory_ref.shape[1] // 2
    count = heads * rows

    if fresh:
        total[...] = jnp.zeros_like(total)
    else:
        total[...] = acc_in[0]

    for x, packed in enumerate(packed_refs):

        @pl.when(tile == x)
        def _(packed=packed):
            query_ref[...] = packed[...]

    terms = query_ref[2 * count:, :].astype(jnp.float32)
    stats = terms
    for part in range(1, PARTS):
        stats = stats + pltpu.roll(terms, dim - 2 * part * heads, 1)
    for h in range(heads):
        for target, lane in ((delta_ref, h), (log_ref, heads + h)):
            target[h * rows:(h + 1) * rows, :] = jnp.broadcast_to(stats[:, lane:lane + 1], (rows, dim))

    low = starts_ref[tile, 0]
    high = starts_ref[tile, 1]
    exponent = scale * math.log2(math.e)

    def add(here, number, checked):
        sides = []
        for two in range(0, number, 2):
            keys, values = [], []
            for j in (two, two + 1):
                valid = here + j < high
                pick = picks_ref[tile, jnp.where(valid, here + j, here) if checked else here + j]
                holder = pick // MOST
                block = pick % MOST
                key = memory_ref[holder, block]
                keys.append(jnp.where(valid, key, jnp.zeros_like(key)) if checked and j else key)
                values.append(memory_ref[holder, blocks + block])
            sides.append((jnp.concatenate(keys, axis=0), jnp.concatenate(values, axis=0)))

        def products(side):
            keys, values = side
            scores = lax.dot_general(query_ref[:count, :], keys, NT, preferred_element_type=jnp.float32)
            grad_probs = lax.dot_general(query_ref[count:2 * count, :], values, NT, preferred_element_type=jnp.float32)
            return scores, grad_probs

        ahead = products(sides[0])
        gained = None
        for at, (keys, _) in enumerate(sides):
            scores, grad_probs = ahead
            if at + 1 < len(sides):
                ahead = products(sides[at + 1])
            log_wide = jnp.concatenate([log_ref[...]] * 2, axis=1)
            delta_wide = jnp.concatenate([delta_ref[...]] * 2, axis=1)
            probs = jnp.exp2(scores * exponent - log_wide)
            grad_scores = (probs * (grad_probs - delta_wide)).astype(jnp.bfloat16)
            part = jnp.dot(grad_scores, keys, preferred_element_type=jnp.float32)
            gained = part if gained is None else gained + part
        total[...] += gained

    full = (high - low) // STEP

    def many(turn, carry):
        add(low + STEP * turn, STEP, False)
        return carry

    def few(turn, carry):
        add(low + STEP * full + 2 * turn, 2, True)
        return carry

    lax.fori_loop(0, full, many, 0)
    lax.fori_loop(0, (high - low - STEP * full + 1) // 2, few, 0)

    if not last:
        out_refs[0][0] = total[...]
        return
    for x, out_ref in enumerate(out_refs):

        @pl.when(tile == x)
        def _(out_ref=out_ref):
            for h in range(heads):
                out_ref[:, h * dim:(h + 1) * dim] = total[h * rows:(h + 1) * rows, :].astype(jnp.bfloat16)


def attend(packed, memory, acc, picks, starts, heads, dim, scale, last):
    tiles = len(packed)
    span = packed[0].shape[0]
    rows = span // (2 * heads + 1)
    fresh = acc is None
    width = heads * rows
    holders = memory.shape[0]
    memory = memory.reshape(holders, -1, BLOCK, dim)
    acc_spec = pl.BlockSpec((1, width, dim), lambda t, *_: (t, 0, 0))
    if last:
        out_shape = [jax.ShapeDtypeStruct((rows, heads * dim), jnp.bfloat16)] * tiles
        out_spec = [pl.BlockSpec((rows, heads * dim), lambda t, *_: (0, 0))] * tiles
    else:
        out_shape = jax.ShapeDtypeStruct((tiles, width, dim), jnp.float32)
        out_spec = acc_spec
    flops = tiles * holders * memory.shape[1] * (BLOCK // 4) * width * dim * 6
    return pl.pallas_call(
        functools.partial(attend_kernel, heads, dim, rows, scale, tiles, fresh, last),
        out_shape=out_shape,
        grid_spec=pltpu.PrefetchScalarGridSpec(
            num_scalar_prefetch=2,
            grid=(tiles,),
            in_specs=[pl.BlockSpec((span, dim), lambda t, *_: (0, 0))] * tiles
            + [pl.BlockSpec(memory.shape, lambda t, *_: (0, 0, 0, 0))]
            + ([] if fresh else [acc_spec]),
            out_specs=out_spec,
            scratch_shapes=[pltpu.VMEM((span, dim), jnp.bfloat16)] + [pltpu.VMEM((width, dim), jnp.float32)] * 3,
        ),
        compiler_params=pltpu.CompilerParams(vmem_limit_bytes=VMEM_MOST),
        cost_estimate=pl.CostEstimate(flops=flops * 4, bytes_accessed=0, transcendentals=0),
    )(picks, starts, *packed, memory, *([] if fresh else [acc]))


def assemble_kernel(own, group, at_ref, *refs):
    pieces, out_ref = refs[:-1], refs[-1]
    span = pieces[0].shape[1]
    for index in range(own):
        for x in range(group):
            column = pl.multiple_of(((at_ref[0] ^ x) * own + index) * span, span)
            out_ref[:, pl.ds(column, span)] = pieces[index * group + x][...]


def assemble(pieces, at, own, group):
    rows, span = pieces[0].shape
    width = own * group * span
    return pl.pallas_call(
        functools.partial(assemble_kernel, own, group),
        out_shape=jax.ShapeDtypeStruct((rows, width), pieces[0].dtype),
        grid_spec=pltpu.PrefetchScalarGridSpec(
            num_scalar_prefetch=1,
            grid=(1,),
            in_specs=[pl.BlockSpec((rows, span), lambda i, _: (0, 0))] * len(pieces),
            out_specs=pl.BlockSpec((rows, width), lambda i, _: (0, 0)),
        ),
        compiler_params=pltpu.CompilerParams(vmem_limit_bytes=VMEM_LIMIT),
        cost_estimate=pl.CostEstimate(flops=0, bytes_accessed=4 * rows * width, transcendentals=0),
    )(at[None], *pieces)


def after(value, *others):
    anywhere = pl.BlockSpec(memory_space=pl.ANY)
    corners = [
        pl.BlockSpec((1,) * (other.ndim - 2) + (HINT, 128), lambda i, count=other.ndim: (0,) * count) for other in others
    ]
    return pl.pallas_call(
        lambda *refs: None,
        out_shape=jax.ShapeDtypeStruct(value.shape, value.dtype),
        grid=(1,),
        in_specs=[anywhere] + corners,
        out_specs=anywhere,
        input_output_aliases={0: 0},
        cost_estimate=pl.CostEstimate(flops=0, bytes_accessed=0, transcendentals=0),
    )(value, *others)


def shards(grad_out, queries, mem_out, row_total, gate_logit, mem_keys, mem_values, retrieved):
    seq = lax.axis_size("seq")
    sections = lax.axis_size("section")
    position = lax.axis_index("seq")
    rows, width = grad_out.shape[1:]
    head_count = gate_logit.shape[1]
    dim = width // head_count
    kv_heads = mem_keys.shape[2] // dim
    heads = head_count // kv_heads
    mem_dev = mem_keys.shape[1]
    blocks = mem_dev // BLOCK
    group = min(kv_heads, seq // 2)
    own = kv_heads // group
    at = position % group
    home = position // group
    scale = dim ** (-0.5)

    def swapped(value, step):
        return lax.ppermute(value, "seq", [(p, p ^ step) for p in range(seq)])

    def delivered(value, step):
        pairs = [(s * seq + p, ((s - 1) % sections) * seq + (p ^ step)) for s in range(sections) for p in range(seq)]
        return lax.ppermute(value, ("section", "seq"), pairs)

    cut = (3 * blocks + 3) // 4
    cuts = [[(0, blocks)]] * (own - 1) + [[(0, cut), (cut, blocks)]]

    def listed(i):
        mine = lax.dynamic_index_in_dim(retrieved[0], at * own + i, 0, keepdims=False)
        mine = jnp.stack(
            [lax.dynamic_index_in_dim(mine, home * group + (at ^ x), 0, keepdims=False) for x in range(group)]
        )
        holder, block = mine // blocks, mine % blocks
        piece = sum((block >= low).astype(jnp.int32) for low, _ in cuts[i][1:]) if len(cuts[i]) > 1 else 0 * block
        key = piece * seq * blocks + mine
        rank = jnp.sum(key[:, None, :] < key[:, :, None], axis=-1)
        order = jnp.arange(mine.shape[-1])
        low = sum((piece == j) * cuts[i][j][0] for j in range(len(cuts[i])))
        value = holder * MOST + block - low
        picks = jnp.sum(jnp.where(rank[:, :, None] == order, value[:, :, None], 0), axis=1).astype(jnp.int32)
        bounds = [jnp.sum(piece < j, axis=-1) for j in range(len(cuts[i]) + 1)]
        return picks, [
            jnp.stack([bounds[j], bounds[j + 1]], axis=1).astype(jnp.int32) for j in range(len(cuts[i]))
        ]

    gates = jax.nn.sigmoid(gate_logit[0])
    memories = list(pack(mem_keys[0], mem_values[0], seq, own, group, dim, cuts))
    gathered, worked, latest, held = [], [], None, []

    def queries_of(i):
        opened = gates if latest is None else after(gates, latest)
        packed = prepare(grad_out[0], queries[0], mem_out[0], row_total[0], opened, at, kv_heads, dim, scale, own, i)
        return [packed[0]] + [swapped(packed[x], x) for x in range(1, group)]

    coming = queries_of(0)
    for i in range(own):
        packed = coming
        pieces = []
        for _ in cuts[i]:
            piece = memories.pop(0)
            piece = piece if latest is None else after(piece, latest, *held)
            latest = lax.all_to_all(piece, "seq", split_axis=0, concat_axis=0, tiled=True)
            pieces.append(latest)
            held = packed
        picks, starts = listed(i)
        run = functools.partial(attend, packed, picks=picks, heads=heads, dim=dim, scale=scale)
        acc = None
        for j in range(len(pieces) - 1):
            acc = run(pieces[j], acc, starts=after(starts[j], *worked), last=False)
            worked = [acc]
        if i < own - 1:
            coming = queries_of(i + 1)
        ready = [] if i < own - 1 else gathered
        done = run(pieces[-1], acc, starts=after(starts[-1], *worked, *ready), last=True)
        worked = done[:1]
        if i < own - 1:
            done = [after(result, *coming) for result in done]
        results = [delivered(done[x], x) for x in range(group)]
        gathered = gathered + results
    return assemble(gathered, at, own, group)[None]


def solution(mesh):
    return jax.shard_map(
        shards,
        mesh=mesh,
        in_specs=(
            P("section", "seq", None),
            P("section", "seq", None),
            P("section", "seq", None),
            P("section", "seq", None),
            P("section", None),
            P("section", "seq", None),
            P("section", "seq", None),
            P("section", None, None, None),
        ),
        out_specs=P("section", "seq", None),
        check_vma=False,
    )
```

```python
import functools
import math

import jax
import jax.numpy as jnp
from jax import lax
from jax.experimental import pallas as pl
from jax.experimental.pallas import tpu as pltpu
from jax.sharding import PartitionSpec as P

BLOCK = 128
PARTS = 3
STEP = 4
MOST = 1 << 10
HINT = 16
VMEM_LIMIT = 48 * 1024 * 1024
VMEM_MOST = 60 * 1024 * 1024

NT = (((1,), (1,)), ((), ()))


def split_parts(value):
    terms = []
    for _ in range(PARTS):
        term = value.astype(jnp.bfloat16)
        terms.append(term.astype(jnp.float32))
        value = value - terms[-1]
    return terms


def pack_kernel(own, group, cuts, keys_ref, values_ref, *outs):
    dim = outs[0].shape[3]
    block = pl.program_id(0)
    at = 0
    for index, pieces in enumerate(cuts):
        for low, high in pieces:

            @pl.when((block >= low) & (block < high))
            def _(out=outs[at], index=index):
                for device in range(out.shape[0]):
                    head = device % group * own + index
                    for half, source in enumerate((keys_ref, values_ref)):
                        out[device, half] = source[:, head * dim:(head + 1) * dim]

            at += 1


def pack(mem_keys, mem_values, seq, own, group, dim, cuts):
    mem_dev, width = mem_keys.shape
    rows = pl.BlockSpec((BLOCK, width), lambda i: (i, 0))
    spans = [span for pieces in cuts for span in pieces]

    def place(low, high):
        return pl.BlockSpec((seq, 2, BLOCK, dim), lambda i: (0, 0, jnp.clip(i - low, 0, high - low - 1), 0))

    outs = pl.pallas_call(
        functools.partial(pack_kernel, own, group, cuts),
        out_shape=[
            jax.ShapeDtypeStruct((seq, 2, (high - low) * BLOCK, dim), mem_keys.dtype) for low, high in spans
        ],
        grid=(mem_dev // BLOCK,),
        in_specs=[rows, rows],
        out_specs=[place(low, high) for low, high in spans],
        compiler_params=pltpu.CompilerParams(vmem_limit_bytes=VMEM_MOST),
        cost_estimate=pl.CostEstimate(flops=0, bytes_accessed=8 * mem_dev * width, transcendentals=0),
    )(mem_keys, mem_values)
    return [out.reshape(seq, -1, dim) for out in outs]


def prepare_kernel(heads, dim, scale, own, index, gate_ref, at_ref, grad_ref, query_ref, out_ref, total_ref, *packed_refs):
    rows = grad_ref.shape[0]
    count = total_ref.shape[1]
    logs = split_parts(jnp.log2(total_ref[...].astype(jnp.float32)) - math.log2(scale))
    target = lax.broadcasted_iota(jnp.int32, (count, dim), 1)
    lane = lax.broadcasted_iota(jnp.int32, (rows, dim), 1)
    for x, packed_ref in enumerate(packed_refs):
        head = (at_ref[0] ^ x) * own + index
        source = lax.broadcasted_iota(jnp.int32, (count, dim), 0) - head * heads
        mine = (source >= 0) & (source < heads)
        stats = jnp.zeros((rows, dim), jnp.float32)
        for part, term in enumerate(logs):
            chosen = jnp.where(mine & (target == source + (2 * part + 1) * heads), 1.0, 0.0).astype(jnp.bfloat16)
            stats += jnp.dot(term.astype(jnp.bfloat16), chosen, preferred_element_type=jnp.float32)
        for h in range(heads):
            columns = pl.ds(pl.multiple_of((head * heads + h) * dim, dim), dim)
            gated = (gate_ref[head * heads + h] * grad_ref[:, columns].astype(jnp.float32)).astype(jnp.bfloat16)
            packed_ref[h * rows:(h + 1) * rows, :] = query_ref[:, columns]
            packed_ref[(heads + h) * rows:(heads + h + 1) * rows, :] = gated
            product = gated.astype(jnp.float32) * out_ref[:, columns].astype(jnp.float32)
            delta = jnp.sum(product, axis=1, keepdims=True)
            for part, term in enumerate(split_parts(delta)):
                stats = jnp.where(lane == 2 * part * heads + h, term, stats)
        packed_ref[2 * heads * rows:, :] = stats.astype(jnp.bfloat16)


def prepare(grad_out, queries, mem_out, row_total, gates, at, kv_heads, dim, scale, own, index):
    rows, width = grad_out.shape
    heads = width // dim // kv_heads
    group = kv_heads // own
    span = 2 * heads * rows + rows
    wide = pl.BlockSpec((rows, width), lambda i, *_: (0, 0))
    return pl.pallas_call(
        functools.partial(prepare_kernel, heads, dim, scale, own, index),
        out_shape=[jax.ShapeDtypeStruct((span, dim), jnp.bfloat16)] * group,
        grid_spec=pltpu.PrefetchScalarGridSpec(
            num_scalar_prefetch=2,
            grid=(1,),
            in_specs=[wide, wide, wide, pl.BlockSpec(row_total.shape, lambda i, *_: (0, 0))],
            out_specs=[pl.BlockSpec((span, dim), lambda i, *_: (0, 0))] * group,
        ),
        compiler_params=pltpu.CompilerParams(vmem_limit_bytes=VMEM_LIMIT),
        cost_estimate=pl.CostEstimate(flops=rows * width * 4, bytes_accessed=rows * width * 12 // own, transcendentals=0),
    )(gates, at[None], grad_out, queries, mem_out, row_total)


def attend_kernel(heads, dim, rows, scale, tiles, fresh, last, picks_ref, starts_ref, *refs):
    packed_refs, memory_ref = refs[:tiles], refs[tiles]
    acc_in = None if fresh else refs[tiles + 1]
    out_refs, (query_ref, log_ref, delta_ref, total) = refs[tiles + (1 if fresh else 2):-4], refs[-4:]
    tile = pl.program_id(0)
    blocks = memory_ref.shape[1] // 2
    count = heads * rows

    if fresh:
        total[...] = jnp.zeros_like(total)
    else:
        total[...] = acc_in[0]

    for x, packed in enumerate(packed_refs):

        @pl.when(tile == x)
        def _(packed=packed):
            query_ref[...] = packed[...]

    terms = query_ref[2 * count:, :].astype(jnp.float32)
    stats = terms
    for part in range(1, PARTS):
        stats = stats + pltpu.roll(terms, dim - 2 * part * heads, 1)
    for h in range(heads):
        for target, lane in ((delta_ref, h), (log_ref, heads + h)):
            target[h * rows:(h + 1) * rows, :] = jnp.broadcast_to(stats[:, lane:lane + 1], (rows, dim))

    low = starts_ref[tile, 0]
    high = starts_ref[tile, 1]
    exponent = scale * math.log2(math.e)

    def add(here, number, checked):
        sides = []
        for two in range(0, number, 2):
            keys, values = [], []
            for j in (two, two + 1):
                valid = here + j < high
                pick = picks_ref[tile, jnp.where(valid, here + j, here) if checked else here + j]
                holder = pick // MOST
                block = pick % MOST
                key = memory_ref[holder, block]
                keys.append(jnp.where(valid, key, jnp.zeros_like(key)) if checked and j else key)
                values.append(memory_ref[holder, blocks + block])
            sides.append((jnp.concatenate(keys, axis=0), jnp.concatenate(values, axis=0)))

        def products(side):
            keys, values = side
            scores = lax.dot_general(query_ref[:count, :], keys, NT, preferred_element_type=jnp.float32)
            grad_probs = lax.dot_general(query_ref[count:2 * count, :], values, NT, preferred_element_type=jnp.float32)
            return scores, grad_probs

        ahead = products(sides[0])
        gained = None
        for at, (keys, _) in enumerate(sides):
            scores, grad_probs = ahead
            if at + 1 < len(sides):
                ahead = products(sides[at + 1])
            log_wide = jnp.concatenate([log_ref[...]] * 2, axis=1)
            delta_wide = jnp.concatenate([delta_ref[...]] * 2, axis=1)
            probs = jnp.exp2(scores * exponent - log_wide)
            grad_scores = (probs * (grad_probs - delta_wide)).astype(jnp.bfloat16)
            part = jnp.dot(grad_scores, keys, preferred_element_type=jnp.float32)
            gained = part if gained is None else gained + part
        total[...] += gained

    full = (high - low) // STEP

    def many(turn, carry):
        add(low + STEP * turn, STEP, False)
        return carry

    def few(turn, carry):
        add(low + STEP * full + 2 * turn, 2, True)
        return carry

    lax.fori_loop(0, full, many, 0)
    lax.fori_loop(0, (high - low - STEP * full + 1) // 2, few, 0)

    if not last:
        out_refs[0][0] = total[...]
        return
    for x, out_ref in enumerate(out_refs):

        @pl.when(tile == x)
        def _(out_ref=out_ref):
            for h in range(heads):
                out_ref[:, h * dim:(h + 1) * dim] = total[h * rows:(h + 1) * rows, :].astype(jnp.bfloat16)


def attend(packed, memory, acc, picks, starts, heads, dim, scale, last):
    tiles = len(packed)
    span = packed[0].shape[0]
    rows = span // (2 * heads + 1)
    fresh = acc is None
    width = heads * rows
    holders = memory.shape[0]
    memory = memory.reshape(holders, -1, BLOCK, dim)
    acc_spec = pl.BlockSpec((1, width, dim), lambda t, *_: (t, 0, 0))
    if last:
        out_shape = [jax.ShapeDtypeStruct((rows, heads * dim), jnp.bfloat16)] * tiles
        out_spec = [pl.BlockSpec((rows, heads * dim), lambda t, *_: (0, 0))] * tiles
    else:
        out_shape = jax.ShapeDtypeStruct((tiles, width, dim), jnp.float32)
        out_spec = acc_spec
    flops = tiles * holders * memory.shape[1] * (BLOCK // 4) * width * dim * 6
    return pl.pallas_call(
        functools.partial(attend_kernel, heads, dim, rows, scale, tiles, fresh, last),
        out_shape=out_shape,
        grid_spec=pltpu.PrefetchScalarGridSpec(
            num_scalar_prefetch=2,
            grid=(tiles,),
            in_specs=[pl.BlockSpec((span, dim), lambda t, *_: (0, 0))] * tiles
            + [pl.BlockSpec(memory.shape, lambda t, *_: (0, 0, 0, 0))]
            + ([] if fresh else [acc_spec]),
            out_specs=out_spec,
            scratch_shapes=[pltpu.VMEM((span, dim), jnp.bfloat16)] + [pltpu.VMEM((width, dim), jnp.float32)] * 3,
        ),
        compiler_params=pltpu.CompilerParams(vmem_limit_bytes=VMEM_MOST),
        cost_estimate=pl.CostEstimate(flops=flops * 4, bytes_accessed=0, transcendentals=0),
    )(picks, starts, *packed, memory, *([] if fresh else [acc]))


def assemble_kernel(own, group, at_ref, *refs):
    pieces, out_ref = refs[:-1], refs[-1]
    span = pieces[0].shape[1]
    for index in range(own):
        for x in range(group):
            column = pl.multiple_of(((at_ref[0] ^ x) * own + index) * span, span)
            out_ref[:, pl.ds(column, span)] = pieces[index * group + x][...]


def assemble(pieces, at, own, group):
    rows, span = pieces[0].shape
    width = own * group * span
    return pl.pallas_call(
        functools.partial(assemble_kernel, own, group),
        out_shape=jax.ShapeDtypeStruct((rows, width), pieces[0].dtype),
        grid_spec=pltpu.PrefetchScalarGridSpec(
            num_scalar_prefetch=1,
            grid=(1,),
            in_specs=[pl.BlockSpec((rows, span), lambda i, _: (0, 0))] * len(pieces),
            out_specs=pl.BlockSpec((rows, width), lambda i, _: (0, 0)),
        ),
        compiler_params=pltpu.CompilerParams(vmem_limit_bytes=VMEM_LIMIT),
        cost_estimate=pl.CostEstimate(flops=0, bytes_accessed=4 * rows * width, transcendentals=0),
    )(at[None], *pieces)


def after(value, *others):
    anywhere = pl.BlockSpec(memory_space=pl.ANY)
    corners = [
        pl.BlockSpec((1,) * (other.ndim - 2) + (HINT, 128), lambda i, count=other.ndim: (0,) * count) for other in others
    ]
    return pl.pallas_call(
        lambda *refs: None,
        out_shape=jax.ShapeDtypeStruct(value.shape, value.dtype),
        grid=(1,),
        in_specs=[anywhere] + corners,
        out_specs=anywhere,
        input_output_aliases={0: 0},
        cost_estimate=pl.CostEstimate(flops=0, bytes_accessed=0, transcendentals=0),
    )(value, *others)


def shards(grad_out, queries, mem_out, row_total, gate_logit, mem_keys, mem_values, retrieved):
    seq = lax.axis_size("seq")
    sections = lax.axis_size("section")
    position = lax.axis_index("seq")
    rows, width = grad_out.shape[1:]
    head_count = gate_logit.shape[1]
    dim = width // head_count
    kv_heads = mem_keys.shape[2] // dim
    heads = head_count // kv_heads
    mem_dev = mem_keys.shape[1]
    blocks = mem_dev // BLOCK
    group = min(kv_heads, seq // 2)
    own = kv_heads // group
    at = position % group
    home = position // group
    scale = dim ** (-0.5)

    def swapped(value, step):
        return lax.ppermute(value, "seq", [(p, p ^ step) for p in range(seq)])

    def delivered(value, step):
        pairs = [(s * seq + p, ((s - 1) % sections) * seq + (p ^ step)) for s in range(sections) for p in range(seq)]
        return lax.ppermute(value, ("section", "seq"), pairs)

    cut = (5 * blocks + 7) // 8
    cuts = [[(0, blocks)]] * (own - 1) + [[(0, cut), (cut, blocks)]]

    def listed(i):
        mine = lax.dynamic_index_in_dim(retrieved[0], at * own + i, 0, keepdims=False)
        mine = jnp.stack(
            [lax.dynamic_index_in_dim(mine, home * group + (at ^ x), 0, keepdims=False) for x in range(group)]
        )
        holder, block = mine // blocks, mine % blocks
        piece = sum((block >= low).astype(jnp.int32) for low, _ in cuts[i][1:]) if len(cuts[i]) > 1 else 0 * block
        key = piece * seq * blocks + mine
        rank = jnp.sum(key[:, None, :] < key[:, :, None], axis=-1)
        order = jnp.arange(mine.shape[-1])
        low = sum((piece == j) * cuts[i][j][0] for j in range(len(cuts[i])))
        value = holder * MOST + block - low
        picks = jnp.sum(jnp.where(rank[:, :, None] == order, value[:, :, None], 0), axis=1).astype(jnp.int32)
        bounds = [jnp.sum(piece < j, axis=-1) for j in range(len(cuts[i]) + 1)]
        return picks, [
            jnp.stack([bounds[j], bounds[j + 1]], axis=1).astype(jnp.int32) for j in range(len(cuts[i]))
        ]

    gates = jax.nn.sigmoid(gate_logit[0])
    memories = list(pack(mem_keys[0], mem_values[0], seq, own, group, dim, cuts))
    gathered, worked, latest, held = [], [], None, []

    def queries_of(i):
        opened = gates if latest is None else after(gates, latest)
        packed = prepare(grad_out[0], queries[0], mem_out[0], row_total[0], opened, at, kv_heads, dim, scale, own, i)
        return [packed[0]] + [swapped(packed[x], x) for x in range(1, group)]

    coming = queries_of(0)
    for i in range(own):
        packed = coming
        pieces = []
        for _ in cuts[i]:
            piece = memories.pop(0)
            piece = piece if latest is None else after(piece, latest, *held)
            latest = lax.all_to_all(piece, "seq", split_axis=0, concat_axis=0, tiled=True)
            pieces.append(latest)
            held = packed
        picks, starts = listed(i)
        run = functools.partial(attend, packed, picks=picks, heads=heads, dim=dim, scale=scale)
        acc = None
        for j in range(len(pieces) - 1):
            acc = run(pieces[j], acc, starts=after(starts[j], *worked), last=False)
            worked = [acc]
        if i < own - 1:
            coming = queries_of(i + 1)
        ready = coming[:1] if i < own - 1 else gathered
        done = run(pieces[-1], acc, starts=after(starts[-1], *worked, *ready), last=True)
        worked = done[:1]
        results = [delivered(done[x], x) for x in range(group)]
        gathered = gathered + results
    return assemble(gathered, at, own, group)[None]


def solution(mesh):
    return jax.shard_map(
        shards,
        mesh=mesh,
        in_specs=(
            P("section", "seq", None),
            P("section", "seq", None),
            P("section", "seq", None),
            P("section", "seq", None),
            P("section", None),
            P("section", "seq", None),
            P("section", "seq", None),
            P("section", None, None, None),
        ),
        out_specs=P("section", "seq", None),
        check_vma=False,
    )
```

```python
import functools
import math

import jax
import jax.numpy as jnp
from jax import lax
from jax.experimental import pallas as pl
from jax.experimental.pallas import tpu as pltpu
from jax.sharding import PartitionSpec as P

BLOCK = 128
PARTS = 3
STEPS = (8, 4)
MOST = 1 << 10
HINT = 16
VMEM_LIMIT = 48 * 1024 * 1024
VMEM_MOST = 60 * 1024 * 1024

NT = (((1,), (1,)), ((), ()))


def split_parts(value):
    terms = []
    for _ in range(PARTS):
        term = value.astype(jnp.bfloat16)
        terms.append(term.astype(jnp.float32))
        value = value - terms[-1]
    return terms


def pack_kernel(own, group, index, spans, at_ref, keys_ref, values_ref, *outs):
    dim = outs[0].shape[3]
    block = pl.program_id(0)
    for (low, high), out in zip(spans, outs):

        @pl.when((block >= low) & (block < high))
        def _(out=out):
            for device in range(out.shape[0]):
                head = device % group * own + index
                for half, source in enumerate((keys_ref, values_ref)):
                    out[device, half] = source[:, head * dim:(head + 1) * dim]


def pack(mem_keys, mem_values, at, seq, own, group, dim, index, spans):
    mem_dev, width = mem_keys.shape
    rows = pl.BlockSpec((BLOCK, width), lambda i, _: (i, 0))

    def place(low, high):
        return pl.BlockSpec((seq, 2, BLOCK, dim), lambda i, _: (0, 0, jnp.clip(i - low, 0, high - low - 1), 0))

    outs = pl.pallas_call(
        functools.partial(pack_kernel, own, group, index, spans),
        out_shape=[
            jax.ShapeDtypeStruct((seq, 2, (high - low) * BLOCK, dim), mem_keys.dtype) for low, high in spans
        ],
        grid_spec=pltpu.PrefetchScalarGridSpec(
            num_scalar_prefetch=1,
            grid=(mem_dev // BLOCK,),
            in_specs=[rows, rows],
            out_specs=[place(low, high) for low, high in spans],
        ),
        compiler_params=pltpu.CompilerParams(vmem_limit_bytes=VMEM_MOST),
        cost_estimate=pl.CostEstimate(flops=0, bytes_accessed=8 * mem_dev * width // own, transcendentals=0),
    )(at, mem_keys, mem_values)
    return [out.reshape(seq, -1, dim) for out in outs]


def prepare_kernel(heads, dim, scale, own, index, gate_ref, at_ref, grad_ref, query_ref, out_ref, total_ref, *packed_refs):
    rows = grad_ref.shape[0]
    count = total_ref.shape[1]
    logs = split_parts(jnp.log2(total_ref[...].astype(jnp.float32)) - math.log2(scale))
    target = lax.broadcasted_iota(jnp.int32, (count, dim), 1)
    lane = lax.broadcasted_iota(jnp.int32, (rows, dim), 1)
    for x, packed_ref in enumerate(packed_refs):
        head = (at_ref[0] ^ x) * own + index
        source = lax.broadcasted_iota(jnp.int32, (count, dim), 0) - head * heads
        mine = (source >= 0) & (source < heads)
        stats = jnp.zeros((rows, dim), jnp.float32)
        for part, term in enumerate(logs):
            chosen = jnp.where(mine & (target == source + (2 * part + 1) * heads), 1.0, 0.0).astype(jnp.bfloat16)
            stats += jnp.dot(term.astype(jnp.bfloat16), chosen, preferred_element_type=jnp.float32)
        for h in range(heads):
            columns = pl.ds(pl.multiple_of((head * heads + h) * dim, dim), dim)
            gated = (gate_ref[head * heads + h] * grad_ref[:, columns].astype(jnp.float32)).astype(jnp.bfloat16)
            packed_ref[h * rows:(h + 1) * rows, :] = query_ref[:, columns]
            packed_ref[(heads + h) * rows:(heads + h + 1) * rows, :] = gated
            product = gated.astype(jnp.float32) * out_ref[:, columns].astype(jnp.float32)
            delta = jnp.sum(product, axis=1, keepdims=True)
            for part, term in enumerate(split_parts(delta)):
                stats = jnp.where(lane == 2 * part * heads + h, term, stats)
        packed_ref[2 * heads * rows:, :] = stats.astype(jnp.bfloat16)


def prepare(grad_out, queries, mem_out, row_total, gates, at, kv_heads, dim, scale, own, index):
    rows, width = grad_out.shape
    heads = width // dim // kv_heads
    group = kv_heads // own
    span = 2 * heads * rows + rows
    wide = pl.BlockSpec((rows, width), lambda i, *_: (0, 0))
    return pl.pallas_call(
        functools.partial(prepare_kernel, heads, dim, scale, own, index),
        out_shape=[jax.ShapeDtypeStruct((span, dim), jnp.bfloat16)] * group,
        grid_spec=pltpu.PrefetchScalarGridSpec(
            num_scalar_prefetch=2,
            grid=(1,),
            in_specs=[wide, wide, wide, pl.BlockSpec(row_total.shape, lambda i, *_: (0, 0))],
            out_specs=[pl.BlockSpec((span, dim), lambda i, *_: (0, 0))] * group,
        ),
        compiler_params=pltpu.CompilerParams(vmem_limit_bytes=VMEM_LIMIT),
        cost_estimate=pl.CostEstimate(flops=rows * width * 4, bytes_accessed=rows * width * 12 // own, transcendentals=0),
    )(gates, at[None], grad_out, queries, mem_out, row_total)


def attend_kernel(heads, dim, rows, scale, first, tiles, fresh, last, picks_ref, starts_ref, *refs):
    packed_refs, memory_ref = refs[:tiles], refs[tiles]
    acc_in = None if fresh else refs[tiles + 1]
    out_refs, (query_ref, log_ref, delta_ref, total) = refs[tiles + (1 if fresh else 2):-4], refs[-4:]
    step = pl.program_id(0)
    tile = first + step
    blocks = memory_ref.shape[1] // 2
    count = heads * rows

    if fresh:
        total[...] = jnp.zeros_like(total)
    else:
        total[...] = acc_in[0]

    for x, packed in enumerate(packed_refs):

        @pl.when(step == x)
        def _(packed=packed):
            query_ref[...] = packed[...]

    terms = query_ref[2 * count:, :].astype(jnp.float32)
    stats = terms
    for part in range(1, PARTS):
        stats = stats + pltpu.roll(terms, dim - 2 * part * heads, 1)
    for h in range(heads):
        for target, lane in ((delta_ref, h), (log_ref, heads + h)):
            target[h * rows:(h + 1) * rows, :] = jnp.broadcast_to(stats[:, lane:lane + 1], (rows, dim))

    low = starts_ref[tile, 0]
    high = starts_ref[tile, 1]
    exponent = scale * math.log2(math.e)

    def add(here, number, checked):
        sides = []
        for two in range(0, number, 2):
            keys, values = [], []
            for j in (two, two + 1):
                valid = here + j < high
                pick = picks_ref[tile, jnp.where(valid, here + j, here) if checked else here + j]
                holder = pick // MOST
                block = pick % MOST
                key = memory_ref[holder, block]
                keys.append(jnp.where(valid, key, jnp.zeros_like(key)) if checked and j else key)
                values.append(memory_ref[holder, blocks + block])
            sides.append((jnp.concatenate(keys, axis=0), jnp.concatenate(values, axis=0)))

        def products(side):
            keys, values = side
            scores = lax.dot_general(query_ref[:count, :], keys, NT, preferred_element_type=jnp.float32)
            grad_probs = lax.dot_general(query_ref[count:2 * count, :], values, NT, preferred_element_type=jnp.float32)
            return scores, grad_probs

        ahead = products(sides[0])
        gained = None
        for at, (keys, _) in enumerate(sides):
            scores, grad_probs = ahead
            if at + 1 < len(sides):
                ahead = products(sides[at + 1])
            log_wide = jnp.concatenate([log_ref[...]] * 2, axis=1)
            delta_wide = jnp.concatenate([delta_ref[...]] * 2, axis=1)
            probs = jnp.exp2(scores * exponent - log_wide)
            grad_scores = (probs * (grad_probs - delta_wide)).astype(jnp.bfloat16)
            part = jnp.dot(grad_scores, keys, preferred_element_type=jnp.float32)
            gained = part if gained is None else gained + part
        total[...] += gained

    for number in STEPS:
        full = (high - low) // number

        def many(turn, carry, low=low, number=number):
            add(low + number * turn, number, False)
            return carry

        lax.fori_loop(0, full, many, 0)
        low = low + number * full

    def few(turn, carry):
        add(low + 2 * turn, 2, True)
        return carry

    lax.fori_loop(0, (high - low + 1) // 2, few, 0)

    if not last:
        out_refs[0][0] = total[...]
        return
    for x, out_ref in enumerate(out_refs):

        @pl.when(step == x)
        def _(out_ref=out_ref):
            for h in range(heads):
                out_ref[:, h * dim:(h + 1) * dim] = total[h * rows:(h + 1) * rows, :].astype(jnp.bfloat16)


def attend(packed, memory, acc, picks, starts, heads, dim, scale, last, first=0):
    tiles = len(packed)
    span = packed[0].shape[0]
    rows = span // (2 * heads + 1)
    fresh = acc is None
    width = heads * rows
    holders = memory.shape[0]
    memory = memory.reshape(holders, -1, BLOCK, dim)
    acc_spec = pl.BlockSpec((1, width, dim), lambda t, *_: (first + t, 0, 0))
    if last:
        out_shape = [jax.ShapeDtypeStruct((rows, heads * dim), jnp.bfloat16)] * tiles
        out_spec = [pl.BlockSpec((rows, heads * dim), lambda t, *_: (0, 0))] * tiles
    else:
        out_shape = jax.ShapeDtypeStruct((tiles, width, dim), jnp.float32)
        out_spec = acc_spec
    flops = tiles * holders * memory.shape[1] * (BLOCK // 4) * width * dim * 6
    return pl.pallas_call(
        functools.partial(attend_kernel, heads, dim, rows, scale, first, tiles, fresh, last),
        out_shape=out_shape,
        grid_spec=pltpu.PrefetchScalarGridSpec(
            num_scalar_prefetch=2,
            grid=(tiles,),
            in_specs=[pl.BlockSpec((span, dim), lambda t, *_: (0, 0))] * tiles
            + [pl.BlockSpec(memory.shape, lambda t, *_: (0, 0, 0, 0))]
            + ([] if fresh else [acc_spec]),
            out_specs=out_spec,
            scratch_shapes=[pltpu.VMEM((span, dim), jnp.bfloat16)] + [pltpu.VMEM((width, dim), jnp.float32)] * 3,
        ),
        compiler_params=pltpu.CompilerParams(vmem_limit_bytes=VMEM_MOST),
        cost_estimate=pl.CostEstimate(flops=flops * 4, bytes_accessed=0, transcendentals=0),
    )(picks, starts, *packed, memory, *([] if fresh else [acc]))


def assemble_kernel(own, group, at_ref, *refs):
    pieces, out_ref = refs[:-1], refs[-1]
    span = pieces[0].shape[1]
    for index in range(own):
        for x in range(group):
            column = pl.multiple_of(((at_ref[0] ^ x) * own + index) * span, span)
            out_ref[:, pl.ds(column, span)] = pieces[index * group + x][...]


def assemble(pieces, at, own, group):
    rows, span = pieces[0].shape
    width = own * group * span
    return pl.pallas_call(
        functools.partial(assemble_kernel, own, group),
        out_shape=jax.ShapeDtypeStruct((rows, width), pieces[0].dtype),
        grid_spec=pltpu.PrefetchScalarGridSpec(
            num_scalar_prefetch=1,
            grid=(1,),
            in_specs=[pl.BlockSpec((rows, span), lambda i, _: (0, 0))] * len(pieces),
            out_specs=pl.BlockSpec((rows, width), lambda i, _: (0, 0)),
        ),
        compiler_params=pltpu.CompilerParams(vmem_limit_bytes=VMEM_LIMIT),
        cost_estimate=pl.CostEstimate(flops=0, bytes_accessed=4 * rows * width, transcendentals=0),
    )(at[None], *pieces)


def after(value, *others):
    anywhere = pl.BlockSpec(memory_space=pl.ANY)
    corners = [
        pl.BlockSpec((1,) * (other.ndim - 2) + (HINT, 128), lambda i, count=other.ndim: (0,) * count) for other in others
    ]
    return pl.pallas_call(
        lambda *refs: None,
        out_shape=jax.ShapeDtypeStruct(value.shape, value.dtype),
        grid=(1,),
        in_specs=[anywhere] + corners,
        out_specs=anywhere,
        input_output_aliases={0: 0},
        cost_estimate=pl.CostEstimate(flops=0, bytes_accessed=0, transcendentals=0),
    )(value, *others)


def shards(grad_out, queries, mem_out, row_total, gate_logit, mem_keys, mem_values, retrieved):
    seq = lax.axis_size("seq")
    sections = lax.axis_size("section")
    position = lax.axis_index("seq")
    rows, width = grad_out.shape[1:]
    head_count = gate_logit.shape[1]
    dim = width // head_count
    kv_heads = mem_keys.shape[2] // dim
    heads = head_count // kv_heads
    mem_dev = mem_keys.shape[1]
    blocks = mem_dev // BLOCK
    group = min(kv_heads, seq // 2)
    own = kv_heads // group
    at = position % group
    home = position // group
    scale = dim ** (-0.5)

    def swapped(value, step):
        return lax.ppermute(value, "seq", [(p, p ^ step) for p in range(seq)])

    def delivered(value, step):
        pairs = [(s * seq + p, ((s - 1) % sections) * seq + (p ^ step)) for s in range(sections) for p in range(seq)]
        return lax.ppermute(value, ("section", "seq"), pairs)

    cut = (5 * blocks + 7) // 8
    cuts = [[(0, blocks)]] * (own - 1) + [[(0, cut), (cut, blocks)]]

    def listed(i):
        mine = lax.dynamic_index_in_dim(retrieved[0], at * own + i, 0, keepdims=False)
        mine = jnp.stack(
            [lax.dynamic_index_in_dim(mine, home * group + (at ^ x), 0, keepdims=False) for x in range(group)]
        )
        holder, block = mine // blocks, mine % blocks
        piece = sum((block >= low).astype(jnp.int32) for low, _ in cuts[i][1:]) if len(cuts[i]) > 1 else 0 * block
        key = piece * seq * blocks + mine
        rank = jnp.sum(key[:, None, :] < key[:, :, None], axis=-1)
        order = jnp.arange(mine.shape[-1])
        low = sum((piece == j) * cuts[i][j][0] for j in range(len(cuts[i])))
        value = holder * MOST + block - low
        picks = jnp.sum(jnp.where(rank[:, :, None] == order, value[:, :, None], 0), axis=1).astype(jnp.int32)
        bounds = [jnp.sum(piece < j, axis=-1) for j in range(len(cuts[i]) + 1)]
        return picks, [
            jnp.stack([bounds[j], bounds[j + 1]], axis=1).astype(jnp.int32) for j in range(len(cuts[i]))
        ]

    gates = jax.nn.sigmoid(gate_logit[0])
    gathered, worked, latest, held = [], [], None, []

    def memory_of(i, hint):
        return pack(mem_keys[0], mem_values[0], hint, seq, own, group, dim, i, cuts[i])

    def queries_of(i, memories):
        opened = gates if latest is None else after(gates, latest)
        packed = prepare(grad_out[0], queries[0], mem_out[0], row_total[0], opened, at, kv_heads, dim, scale, own, i)
        if i + 1 < own:
            memories += memory_of(i + 1, after(at[None], packed[0]))
        sent = [after(packed[x], *memories[len(cuts[i]):]) if i + 1 < own else packed[x] for x in range(group)]
        return [packed[0]] + [swapped(sent[x], x) for x in range(1, group)]

    memories = memory_of(0, at[None])
    coming = queries_of(0, memories)
    for i in range(own):
        packed = coming
        pieces = []
        for _ in cuts[i]:
            piece = memories.pop(0)
            piece = piece if latest is None else after(piece, latest, *held)
            latest = lax.all_to_all(piece, "seq", split_axis=0, concat_axis=0, tiled=True)
            pieces.append(latest)
            held = packed
        picks, starts = listed(i)
        run = functools.partial(attend, picks=picks, heads=heads, dim=dim, scale=scale)
        acc = None
        for j in range(len(pieces) - 1):
            acc = run(packed, pieces[j], acc, starts=after(starts[j], *worked), last=False)
            worked = [acc]
        if i < own - 1:
            coming = queries_of(i + 1, memories)
            done = run(packed, pieces[-1], acc, starts=after(starts[-1], *worked, coming[0]), last=True)
            worked = done[:1]
            gathered += [delivered(done[x], x) for x in range(group)]
            continue
        results, half = [], group // 2
        for low, high in ((0, half), (half, group)):
            bounds = after(starts[-1], *worked, *([] if low else gathered))
            done = run(packed[low:high], pieces[-1], acc, starts=bounds, last=True, first=low)
            worked = done[:1]
            for x in range(low, high):
                result = done[x - low]
                result = after(result, results[x - half]) if low else result
                results.append(delivered(result, x))
    return assemble(gathered + results, at, own, group)[None]


def solution(mesh):
    return jax.shard_map(
        shards,
        mesh=mesh,
        in_specs=(
            P("section", "seq", None),
            P("section", "seq", None),
            P("section", "seq", None),
            P("section", "seq", None),
            P("section", None),
            P("section", "seq", None),
            P("section", "seq", None),
            P("section", None, None, None),
        ),
        out_specs=P("section", "seq", None),
        check_vma=False,
    )
```

```python
import functools
import math

import jax
import jax.numpy as jnp
from jax import lax
from jax.experimental import pallas as pl
from jax.experimental.pallas import tpu as pltpu
from jax.sharding import PartitionSpec as P

BLOCK = 128
PARTS = 3
STEPS = (8, 4)
MOST = 1 << 10
HINT = 16
VMEM_LIMIT = 48 * 1024 * 1024
VMEM_MOST = 60 * 1024 * 1024

NT = (((1,), (1,)), ((), ()))


def split_parts(value):
    terms = []
    for _ in range(PARTS):
        term = value.astype(jnp.bfloat16)
        terms.append(term.astype(jnp.float32))
        value = value - terms[-1]
    return terms


def pack_kernel(own, group, index, spans, at_ref, keys_ref, values_ref, *outs):
    dim = outs[0].shape[3]
    block = pl.program_id(0)
    for (low, high), out in zip(spans, outs):

        @pl.when((block >= low) & (block < high))
        def _(out=out):
            for device in range(out.shape[0]):
                head = device % group * own + index
                for half, source in enumerate((keys_ref, values_ref)):
                    out[device, half] = source[:, head * dim:(head + 1) * dim]


def pack(mem_keys, mem_values, at, seq, own, group, dim, index, spans):
    mem_dev, width = mem_keys.shape
    rows = pl.BlockSpec((BLOCK, width), lambda i, _: (i, 0))

    def place(low, high):
        return pl.BlockSpec((seq, 2, BLOCK, dim), lambda i, _: (0, 0, jnp.clip(i - low, 0, high - low - 1), 0))

    outs = pl.pallas_call(
        functools.partial(pack_kernel, own, group, index, spans),
        out_shape=[
            jax.ShapeDtypeStruct((seq, 2, (high - low) * BLOCK, dim), mem_keys.dtype) for low, high in spans
        ],
        grid_spec=pltpu.PrefetchScalarGridSpec(
            num_scalar_prefetch=1,
            grid=(mem_dev // BLOCK,),
            in_specs=[rows, rows],
            out_specs=[place(low, high) for low, high in spans],
        ),
        compiler_params=pltpu.CompilerParams(vmem_limit_bytes=VMEM_MOST),
        cost_estimate=pl.CostEstimate(flops=0, bytes_accessed=8 * mem_dev * width // own, transcendentals=0),
    )(at, mem_keys, mem_values)
    return [out.reshape(seq, -1, dim) for out in outs]


def prepare_kernel(heads, dim, scale, own, index, gate_ref, at_ref, grad_ref, query_ref, out_ref, total_ref, *packed_refs):
    rows = grad_ref.shape[0]
    count = total_ref.shape[1]
    logs = split_parts(jnp.log2(total_ref[...].astype(jnp.float32)) - math.log2(scale))
    target = lax.broadcasted_iota(jnp.int32, (count, dim), 1)
    lane = lax.broadcasted_iota(jnp.int32, (rows, dim), 1)
    for x, packed_ref in enumerate(packed_refs):
        head = (at_ref[0] ^ x) * own + index
        source = lax.broadcasted_iota(jnp.int32, (count, dim), 0) - head * heads
        mine = (source >= 0) & (source < heads)
        stats = jnp.zeros((rows, dim), jnp.float32)
        for part, term in enumerate(logs):
            chosen = jnp.where(mine & (target == source + (2 * part + 1) * heads), 1.0, 0.0).astype(jnp.bfloat16)
            stats += jnp.dot(term.astype(jnp.bfloat16), chosen, preferred_element_type=jnp.float32)
        for h in range(heads):
            columns = pl.ds(pl.multiple_of((head * heads + h) * dim, dim), dim)
            gated = (gate_ref[head * heads + h] * grad_ref[:, columns].astype(jnp.float32)).astype(jnp.bfloat16)
            packed_ref[h * rows:(h + 1) * rows, :] = query_ref[:, columns]
            packed_ref[(heads + h) * rows:(heads + h + 1) * rows, :] = gated
            product = gated.astype(jnp.float32) * out_ref[:, columns].astype(jnp.float32)
            delta = jnp.sum(product, axis=1, keepdims=True)
            for part, term in enumerate(split_parts(delta)):
                stats = jnp.where(lane == 2 * part * heads + h, term, stats)
        packed_ref[2 * heads * rows:, :] = stats.astype(jnp.bfloat16)


def prepare(grad_out, queries, mem_out, row_total, gates, at, kv_heads, dim, scale, own, index):
    rows, width = grad_out.shape
    heads = width // dim // kv_heads
    group = kv_heads // own
    span = 2 * heads * rows + rows
    wide = pl.BlockSpec((rows, width), lambda i, *_: (0, 0))
    return pl.pallas_call(
        functools.partial(prepare_kernel, heads, dim, scale, own, index),
        out_shape=[jax.ShapeDtypeStruct((span, dim), jnp.bfloat16)] * group,
        grid_spec=pltpu.PrefetchScalarGridSpec(
            num_scalar_prefetch=2,
            grid=(1,),
            in_specs=[wide, wide, wide, pl.BlockSpec(row_total.shape, lambda i, *_: (0, 0))],
            out_specs=[pl.BlockSpec((span, dim), lambda i, *_: (0, 0))] * group,
        ),
        compiler_params=pltpu.CompilerParams(vmem_limit_bytes=VMEM_LIMIT),
        cost_estimate=pl.CostEstimate(flops=rows * width * 4, bytes_accessed=rows * width * 12 // own, transcendentals=0),
    )(gates, at[None], grad_out, queries, mem_out, row_total)


def attend_kernel(heads, dim, rows, scale, first, tiles, fresh, last, picks_ref, starts_ref, *refs):
    packed_refs, memory_ref = refs[:tiles], refs[tiles]
    acc_in = None if fresh else refs[tiles + 1]
    out_refs, (query_ref, log_ref, delta_ref, total) = refs[tiles + (1 if fresh else 2):-4], refs[-4:]
    step = pl.program_id(0)
    tile = first + step
    blocks = memory_ref.shape[1] // 2
    count = heads * rows

    if fresh:
        total[...] = jnp.zeros_like(total)
    else:
        total[...] = acc_in[0]

    for x, packed in enumerate(packed_refs):

        @pl.when(step == x)
        def _(packed=packed):
            query_ref[...] = packed[...]

    terms = query_ref[2 * count:, :].astype(jnp.float32)
    stats = terms
    for part in range(1, PARTS):
        stats = stats + pltpu.roll(terms, dim - 2 * part * heads, 1)
    for h in range(heads):
        for target, lane in ((delta_ref, h), (log_ref, heads + h)):
            target[h * rows:(h + 1) * rows, :] = jnp.broadcast_to(stats[:, lane:lane + 1], (rows, dim))

    low = starts_ref[tile, 0]
    high = starts_ref[tile, 1]
    exponent = scale * math.log2(math.e)

    def add(here, number, checked):
        sides = []
        for two in range(0, number, 2):
            keys, values = [], []
            for j in (two, two + 1):
                valid = here + j < high
                pick = picks_ref[tile, jnp.where(valid, here + j, here) if checked else here + j]
                holder = pick // MOST
                block = pick % MOST
                key = memory_ref[holder, block]
                keys.append(jnp.where(valid, key, jnp.zeros_like(key)) if checked and j else key)
                values.append(memory_ref[holder, blocks + block])
            sides.append((jnp.concatenate(keys, axis=0), jnp.concatenate(values, axis=0)))

        def products(side):
            keys, values = side
            scores = lax.dot_general(query_ref[:count, :], keys, NT, preferred_element_type=jnp.float32)
            grad_probs = lax.dot_general(query_ref[count:2 * count, :], values, NT, preferred_element_type=jnp.float32)
            return scores, grad_probs

        ahead = products(sides[0])
        gained = None
        for at, (keys, _) in enumerate(sides):
            scores, grad_probs = ahead
            if at + 1 < len(sides):
                ahead = products(sides[at + 1])
            log_wide = jnp.concatenate([log_ref[...]] * 2, axis=1)
            delta_wide = jnp.concatenate([delta_ref[...]] * 2, axis=1)
            probs = jnp.exp2(scores * exponent - log_wide)
            grad_scores = (probs * (grad_probs - delta_wide)).astype(jnp.bfloat16)
            part = jnp.dot(grad_scores, keys, preferred_element_type=jnp.float32)
            gained = part if gained is None else gained + part
        total[...] += gained

    for number in STEPS:
        full = (high - low) // number

        def many(turn, carry, low=low, number=number):
            add(low + number * turn, number, False)
            return carry

        lax.fori_loop(0, full, many, 0)
        low = low + number * full

    def few(turn, carry):
        add(low + 2 * turn, 2, True)
        return carry

    lax.fori_loop(0, (high - low + 1) // 2, few, 0)

    if not last:
        out_refs[0][0] = total[...]
        return
    for x, out_ref in enumerate(out_refs):

        @pl.when(step == x)
        def _(out_ref=out_ref):
            for h in range(heads):
                out_ref[:, h * dim:(h + 1) * dim] = total[h * rows:(h + 1) * rows, :].astype(jnp.bfloat16)


def attend(packed, memory, acc, picks, starts, heads, dim, scale, last, first=0):
    tiles = len(packed)
    span = packed[0].shape[0]
    rows = span // (2 * heads + 1)
    fresh = acc is None
    width = heads * rows
    holders = memory.shape[0]
    memory = memory.reshape(holders, -1, BLOCK, dim)
    acc_spec = pl.BlockSpec((1, width, dim), lambda t, *_: (first + t, 0, 0))
    if last:
        out_shape = [jax.ShapeDtypeStruct((rows, heads * dim), jnp.bfloat16)] * tiles
        out_spec = [pl.BlockSpec((rows, heads * dim), lambda t, *_: (0, 0))] * tiles
    else:
        out_shape = jax.ShapeDtypeStruct((tiles, width, dim), jnp.float32)
        out_spec = acc_spec
    flops = tiles * holders * memory.shape[1] * (BLOCK // 4) * width * dim * 6
    return pl.pallas_call(
        functools.partial(attend_kernel, heads, dim, rows, scale, first, tiles, fresh, last),
        out_shape=out_shape,
        grid_spec=pltpu.PrefetchScalarGridSpec(
            num_scalar_prefetch=2,
            grid=(tiles,),
            in_specs=[pl.BlockSpec((span, dim), lambda t, *_: (0, 0))] * tiles
            + [pl.BlockSpec(memory.shape, lambda t, *_: (0, 0, 0, 0))]
            + ([] if fresh else [acc_spec]),
            out_specs=out_spec,
            scratch_shapes=[pltpu.VMEM((span, dim), jnp.bfloat16)] + [pltpu.VMEM((width, dim), jnp.float32)] * 3,
        ),
        compiler_params=pltpu.CompilerParams(vmem_limit_bytes=VMEM_MOST),
        cost_estimate=pl.CostEstimate(flops=flops * 4, bytes_accessed=0, transcendentals=0),
    )(picks, starts, *packed, memory, *([] if fresh else [acc]))


def assemble_kernel(own, group, at_ref, *refs):
    pieces, out_ref = refs[:-1], refs[-1]
    span = pieces[0].shape[1]
    for index in range(own):
        for x in range(group):
            column = pl.multiple_of(((at_ref[0] ^ x) * own + index) * span, span)
            out_ref[:, pl.ds(column, span)] = pieces[index * group + x][...]


def assemble(pieces, at, own, group):
    rows, span = pieces[0].shape
    width = own * group * span
    return pl.pallas_call(
        functools.partial(assemble_kernel, own, group),
        out_shape=jax.ShapeDtypeStruct((rows, width), pieces[0].dtype),
        grid_spec=pltpu.PrefetchScalarGridSpec(
            num_scalar_prefetch=1,
            grid=(1,),
            in_specs=[pl.BlockSpec((rows, span), lambda i, _: (0, 0))] * len(pieces),
            out_specs=pl.BlockSpec((rows, width), lambda i, _: (0, 0)),
        ),
        compiler_params=pltpu.CompilerParams(vmem_limit_bytes=VMEM_LIMIT),
        cost_estimate=pl.CostEstimate(flops=0, bytes_accessed=4 * rows * width, transcendentals=0),
    )(at[None], *pieces)


def after(value, *others):
    anywhere = pl.BlockSpec(memory_space=pl.ANY)
    corners = [
        pl.BlockSpec((1,) * (other.ndim - 2) + (HINT, 128), lambda i, count=other.ndim: (0,) * count) for other in others
    ]
    return pl.pallas_call(
        lambda *refs: None,
        out_shape=jax.ShapeDtypeStruct(value.shape, value.dtype),
        grid=(1,),
        in_specs=[anywhere] + corners,
        out_specs=anywhere,
        input_output_aliases={0: 0},
        cost_estimate=pl.CostEstimate(flops=0, bytes_accessed=0, transcendentals=0),
    )(value, *others)


def shards(grad_out, queries, mem_out, row_total, gate_logit, mem_keys, mem_values, retrieved):
    seq = lax.axis_size("seq")
    sections = lax.axis_size("section")
    position = lax.axis_index("seq")
    rows, width = grad_out.shape[1:]
    head_count = gate_logit.shape[1]
    dim = width // head_count
    kv_heads = mem_keys.shape[2] // dim
    heads = head_count // kv_heads
    mem_dev = mem_keys.shape[1]
    blocks = mem_dev // BLOCK
    group = min(kv_heads, seq // 2)
    own = kv_heads // group
    at = position % group
    home = position // group
    scale = dim ** (-0.5)

    def swapped(value, step):
        return lax.ppermute(value, "seq", [(p, p ^ step) for p in range(seq)])

    def delivered(value, step):
        pairs = [(s * seq + p, ((s - 1) % sections) * seq + (p ^ step)) for s in range(sections) for p in range(seq)]
        return lax.ppermute(value, ("section", "seq"), pairs)

    cut = (3 * blocks + 3) // 4
    cuts = [[(0, blocks)]] * (own - 1) + [[(0, cut), (cut, blocks)]]

    def listed(i):
        mine = lax.dynamic_index_in_dim(retrieved[0], at * own + i, 0, keepdims=False)
        mine = jnp.stack(
            [lax.dynamic_index_in_dim(mine, home * group + (at ^ x), 0, keepdims=False) for x in range(group)]
        )
        holder, block = mine // blocks, mine % blocks
        piece = sum((block >= low).astype(jnp.int32) for low, _ in cuts[i][1:]) if len(cuts[i]) > 1 else 0 * block
        key = piece * seq * blocks + mine
        rank = jnp.sum(key[:, None, :] < key[:, :, None], axis=-1)
        order = jnp.arange(mine.shape[-1])
        low = sum((piece == j) * cuts[i][j][0] for j in range(len(cuts[i])))
        value = holder * MOST + block - low
        picks = jnp.sum(jnp.where(rank[:, :, None] == order, value[:, :, None], 0), axis=1).astype(jnp.int32)
        bounds = [jnp.sum(piece < j, axis=-1) for j in range(len(cuts[i]) + 1)]
        return picks, [
            jnp.stack([bounds[j], bounds[j + 1]], axis=1).astype(jnp.int32) for j in range(len(cuts[i]))
        ]

    gates = jax.nn.sigmoid(gate_logit[0])
    gathered, worked, latest, held = [], [], None, []

    def memory_of(i, hint):
        return pack(mem_keys[0], mem_values[0], hint, seq, own, group, dim, i, cuts[i])

    def queries_of(i):
        return prepare(grad_out[0], queries[0], mem_out[0], row_total[0], gates, at, kv_heads, dim, scale, own, i)

    def exchanged(packed, *first):
        sent = [after(value, *first) if first else value for value in packed]
        return [packed[0]] + [swapped(sent[x], x) for x in range(1, group)]

    memories = memory_of(0, at[None])
    asked = [queries_of(0)]
    for i in range(1, own):
        memories += memory_of(i, after(at[None], asked[-1][0]))
        asked.append(queries_of(i))
    coming = exchanged(asked[0], *memories[len(cuts[0]):], *[value[0] for value in asked[1:]])
    for i in range(own):
        packed = coming
        pieces = []
        for _ in cuts[i]:
            piece = memories.pop(0)
            piece = piece if latest is None else after(piece, latest, *held)
            latest = lax.all_to_all(piece, "seq", split_axis=0, concat_axis=0, tiled=True)
            pieces.append(latest)
            held = packed
        picks, starts = listed(i)
        run = functools.partial(attend, picks=picks, heads=heads, dim=dim, scale=scale)
        acc = None
        for j in range(len(pieces) - 1):
            acc = run(packed, pieces[j], acc, starts=after(starts[j], *worked), last=False)
            worked = [acc]
        if i < own - 1:
            coming = exchanged(asked[i + 1], latest)
            done = run(packed, pieces[-1], acc, starts=after(starts[-1], *worked), last=True)
            worked = done[:1]
            gathered += [delivered(done[x], x) for x in range(group)]
            continue
        results, half = [None] * group, group // 2
        for low, high in ((half, group), (0, half)):
            bounds = after(starts[-1], *worked, *(gathered if low else []))
            done = run(packed[low:high], pieces[-1], acc, starts=bounds, last=True, first=low)
            worked = done[:1]
            for x in range(low, high):
                result = done[x - low]
                result = result if low else after(result, results[x + half])
                results[x] = delivered(result, x)
    return assemble(gathered + results, at, own, group)[None]


def solution(mesh):
    return jax.shard_map(
        shards,
        mesh=mesh,
        in_specs=(
            P("section", "seq", None),
            P("section", "seq", None),
            P("section", "seq", None),
            P("section", "seq", None),
            P("section", None),
            P("section", "seq", None),
            P("section", "seq", None),
            P("section", None, None, None),
        ),
        out_specs=P("section", "seq", None),
        check_vma=False,
    )
```

```python
import functools
import math

import jax
import jax.numpy as jnp
from jax import lax
from jax.experimental import pallas as pl
from jax.experimental.pallas import tpu as pltpu
from jax.sharding import PartitionSpec as P

BLOCK = 128
PARTS = 3
STEPS = (8, 4)
MOST = 1 << 10
HINT = 16
VMEM_LIMIT = 48 * 1024 * 1024
VMEM_MOST = 60 * 1024 * 1024

NT = (((1,), (1,)), ((), ()))


def split_parts(value):
    terms = []
    for _ in range(PARTS):
        term = value.astype(jnp.bfloat16)
        terms.append(term.astype(jnp.float32))
        value = value - terms[-1]
    return terms


def pack_kernel(own, group, index, spans, at_ref, keys_ref, values_ref, *outs):
    dim = outs[0].shape[3]
    block = pl.program_id(0)
    for (low, high), out in zip(spans, outs):

        @pl.when((block >= low) & (block < high))
        def _(out=out):
            for device in range(out.shape[0]):
                head = device % group * own + index
                for half, source in enumerate((keys_ref, values_ref)):
                    out[device, half] = source[:, head * dim:(head + 1) * dim]


def pack(mem_keys, mem_values, at, seq, own, group, dim, index, spans):
    mem_dev, width = mem_keys.shape
    rows = pl.BlockSpec((BLOCK, width), lambda i, _: (i, 0))

    def place(low, high):
        return pl.BlockSpec((seq, 2, BLOCK, dim), lambda i, _: (0, 0, jnp.clip(i - low, 0, high - low - 1), 0))

    outs = pl.pallas_call(
        functools.partial(pack_kernel, own, group, index, spans),
        out_shape=[
            jax.ShapeDtypeStruct((seq, 2, (high - low) * BLOCK, dim), mem_keys.dtype) for low, high in spans
        ],
        grid_spec=pltpu.PrefetchScalarGridSpec(
            num_scalar_prefetch=1,
            grid=(mem_dev // BLOCK,),
            in_specs=[rows, rows],
            out_specs=[place(low, high) for low, high in spans],
        ),
        compiler_params=pltpu.CompilerParams(vmem_limit_bytes=VMEM_MOST),
        cost_estimate=pl.CostEstimate(flops=0, bytes_accessed=8 * mem_dev * width // own, transcendentals=0),
    )(at, mem_keys, mem_values)
    return [out.reshape(seq, -1, dim) for out in outs]


def prepare_kernel(heads, dim, scale, own, index, gate_ref, at_ref, grad_ref, query_ref, out_ref, total_ref, *packed_refs):
    rows = grad_ref.shape[0]
    count = total_ref.shape[1]
    logs = split_parts(jnp.log2(total_ref[...].astype(jnp.float32)) - math.log2(scale))
    target = lax.broadcasted_iota(jnp.int32, (count, dim), 1)
    lane = lax.broadcasted_iota(jnp.int32, (rows, dim), 1)
    for x, packed_ref in enumerate(packed_refs):
        head = (at_ref[0] ^ x) * own + index
        source = lax.broadcasted_iota(jnp.int32, (count, dim), 0) - head * heads
        mine = (source >= 0) & (source < heads)
        stats = jnp.zeros((rows, dim), jnp.float32)
        for part, term in enumerate(logs):
            chosen = jnp.where(mine & (target == source + (2 * part + 1) * heads), 1.0, 0.0).astype(jnp.bfloat16)
            stats += jnp.dot(term.astype(jnp.bfloat16), chosen, preferred_element_type=jnp.float32)
        for h in range(heads):
            columns = pl.ds(pl.multiple_of((head * heads + h) * dim, dim), dim)
            gated = (gate_ref[head * heads + h] * grad_ref[:, columns].astype(jnp.float32)).astype(jnp.bfloat16)
            packed_ref[h * rows:(h + 1) * rows, :] = query_ref[:, columns]
            packed_ref[(heads + h) * rows:(heads + h + 1) * rows, :] = gated
            product = gated.astype(jnp.float32) * out_ref[:, columns].astype(jnp.float32)
            delta = jnp.sum(product, axis=1, keepdims=True)
            for part, term in enumerate(split_parts(delta)):
                stats = jnp.where(lane == 2 * part * heads + h, term, stats)
        packed_ref[2 * heads * rows:, :] = stats.astype(jnp.bfloat16)


def prepare(grad_out, queries, mem_out, row_total, gates, at, kv_heads, dim, scale, own, index):
    rows, width = grad_out.shape
    heads = width // dim // kv_heads
    group = kv_heads // own
    span = 2 * heads * rows + rows
    wide = pl.BlockSpec((rows, width), lambda i, *_: (0, 0))
    return pl.pallas_call(
        functools.partial(prepare_kernel, heads, dim, scale, own, index),
        out_shape=[jax.ShapeDtypeStruct((span, dim), jnp.bfloat16)] * group,
        grid_spec=pltpu.PrefetchScalarGridSpec(
            num_scalar_prefetch=2,
            grid=(1,),
            in_specs=[wide, wide, wide, pl.BlockSpec(row_total.shape, lambda i, *_: (0, 0))],
            out_specs=[pl.BlockSpec((span, dim), lambda i, *_: (0, 0))] * group,
        ),
        compiler_params=pltpu.CompilerParams(vmem_limit_bytes=VMEM_LIMIT),
        cost_estimate=pl.CostEstimate(flops=rows * width * 4, bytes_accessed=rows * width * 12 // own, transcendentals=0),
    )(gates, at[None], grad_out, queries, mem_out, row_total)


def attend_kernel(heads, dim, rows, scale, first, tiles, fresh, last, picks_ref, starts_ref, *refs):
    packed_refs, memory_ref = refs[:tiles], refs[tiles]
    acc_in = None if fresh else refs[tiles + 1]
    out_refs, (query_ref, log_ref, delta_ref, total) = refs[tiles + (1 if fresh else 2):-4], refs[-4:]
    step = pl.program_id(0)
    tile = first + step
    blocks = memory_ref.shape[1] // 2
    count = heads * rows

    if fresh:
        total[...] = jnp.zeros_like(total)
    else:
        total[...] = acc_in[0]

    for x, packed in enumerate(packed_refs):

        @pl.when(step == x)
        def _(packed=packed):
            query_ref[...] = packed[...]

    terms = query_ref[2 * count:, :].astype(jnp.float32)
    stats = terms
    for part in range(1, PARTS):
        stats = stats + pltpu.roll(terms, dim - 2 * part * heads, 1)
    for h in range(heads):
        for target, lane in ((delta_ref, h), (log_ref, heads + h)):
            target[h * rows:(h + 1) * rows, :] = jnp.broadcast_to(stats[:, lane:lane + 1], (rows, dim))

    low = starts_ref[tile, 0]
    high = starts_ref[tile, 1]
    exponent = scale * math.log2(math.e)

    def add(here, number, checked):
        sides = []
        for two in range(0, number, 2):
            keys, values = [], []
            for j in (two, two + 1):
                valid = here + j < high
                pick = picks_ref[tile, jnp.where(valid, here + j, here) if checked else here + j]
                holder = pick // MOST
                block = pick % MOST
                key = memory_ref[holder, block]
                keys.append(jnp.where(valid, key, jnp.zeros_like(key)) if checked and j else key)
                values.append(memory_ref[holder, blocks + block])
            sides.append((jnp.concatenate(keys, axis=0), jnp.concatenate(values, axis=0)))

        def products(side):
            keys, values = side
            scores = lax.dot_general(query_ref[:count, :], keys, NT, preferred_element_type=jnp.float32)
            grad_probs = lax.dot_general(query_ref[count:2 * count, :], values, NT, preferred_element_type=jnp.float32)
            return scores, grad_probs

        ahead = products(sides[0])
        gained = None
        for at, (keys, _) in enumerate(sides):
            scores, grad_probs = ahead
            if at + 1 < len(sides):
                ahead = products(sides[at + 1])
            log_wide = jnp.concatenate([log_ref[...]] * 2, axis=1)
            delta_wide = jnp.concatenate([delta_ref[...]] * 2, axis=1)
            probs = jnp.exp2(scores * exponent - log_wide)
            grad_scores = (probs * (grad_probs - delta_wide)).astype(jnp.bfloat16)
            part = jnp.dot(grad_scores, keys, preferred_element_type=jnp.float32)
            gained = part if gained is None else gained + part
        total[...] += gained

    for number in STEPS:
        full = (high - low) // number

        def many(turn, carry, low=low, number=number):
            add(low + number * turn, number, False)
            return carry

        lax.fori_loop(0, full, many, 0)
        low = low + number * full

    def few(turn, carry):
        add(low + 2 * turn, 2, True)
        return carry

    lax.fori_loop(0, (high - low + 1) // 2, few, 0)

    if not last:
        out_refs[0][0] = total[...]
        return
    for x, out_ref in enumerate(out_refs):

        @pl.when(step == x)
        def _(out_ref=out_ref):
            for h in range(heads):
                out_ref[:, h * dim:(h + 1) * dim] = total[h * rows:(h + 1) * rows, :].astype(jnp.bfloat16)


def attend(packed, memory, acc, picks, starts, heads, dim, scale, last, first=0):
    tiles = len(packed)
    span = packed[0].shape[0]
    rows = span // (2 * heads + 1)
    fresh = acc is None
    width = heads * rows
    holders = memory.shape[0]
    memory = memory.reshape(holders, -1, BLOCK, dim)
    acc_spec = pl.BlockSpec((1, width, dim), lambda t, *_: (first + t, 0, 0))
    if last:
        out_shape = [jax.ShapeDtypeStruct((rows, heads * dim), jnp.bfloat16)] * tiles
        out_spec = [pl.BlockSpec((rows, heads * dim), lambda t, *_: (0, 0))] * tiles
    else:
        out_shape = jax.ShapeDtypeStruct((tiles, width, dim), jnp.float32)
        out_spec = acc_spec
    flops = tiles * holders * memory.shape[1] * (BLOCK // 4) * width * dim * 6
    return pl.pallas_call(
        functools.partial(attend_kernel, heads, dim, rows, scale, first, tiles, fresh, last),
        out_shape=out_shape,
        grid_spec=pltpu.PrefetchScalarGridSpec(
            num_scalar_prefetch=2,
            grid=(tiles,),
            in_specs=[pl.BlockSpec((span, dim), lambda t, *_: (0, 0))] * tiles
            + [pl.BlockSpec(memory.shape, lambda t, *_: (0, 0, 0, 0))]
            + ([] if fresh else [acc_spec]),
            out_specs=out_spec,
            scratch_shapes=[pltpu.VMEM((span, dim), jnp.bfloat16)] + [pltpu.VMEM((width, dim), jnp.float32)] * 3,
        ),
        compiler_params=pltpu.CompilerParams(vmem_limit_bytes=VMEM_MOST),
        cost_estimate=pl.CostEstimate(flops=flops * 4, bytes_accessed=0, transcendentals=0),
    )(picks, starts, *packed, memory, *([] if fresh else [acc]))


def assemble_kernel(own, group, at_ref, *refs):
    pieces, out_ref = refs[:-1], refs[-1]
    span = pieces[0].shape[1]
    for index in range(own):
        for x in range(group):
            column = pl.multiple_of(((at_ref[0] ^ x) * own + index) * span, span)
            out_ref[:, pl.ds(column, span)] = pieces[index * group + x][...]


def assemble(pieces, at, own, group):
    rows, span = pieces[0].shape
    width = own * group * span
    return pl.pallas_call(
        functools.partial(assemble_kernel, own, group),
        out_shape=jax.ShapeDtypeStruct((rows, width), pieces[0].dtype),
        grid_spec=pltpu.PrefetchScalarGridSpec(
            num_scalar_prefetch=1,
            grid=(1,),
            in_specs=[pl.BlockSpec((rows, span), lambda i, _: (0, 0))] * len(pieces),
            out_specs=pl.BlockSpec((rows, width), lambda i, _: (0, 0)),
        ),
        compiler_params=pltpu.CompilerParams(vmem_limit_bytes=VMEM_LIMIT),
        cost_estimate=pl.CostEstimate(flops=0, bytes_accessed=4 * rows * width, transcendentals=0),
    )(at[None], *pieces)


def after(value, *others):
    anywhere = pl.BlockSpec(memory_space=pl.ANY)
    corners = [
        pl.BlockSpec((1,) * (other.ndim - 2) + (HINT, 128), lambda i, count=other.ndim: (0,) * count) for other in others
    ]
    return pl.pallas_call(
        lambda *refs: None,
        out_shape=jax.ShapeDtypeStruct(value.shape, value.dtype),
        grid=(1,),
        in_specs=[anywhere] + corners,
        out_specs=anywhere,
        input_output_aliases={0: 0},
        cost_estimate=pl.CostEstimate(flops=0, bytes_accessed=0, transcendentals=0),
    )(value, *others)


def shards(grad_out, queries, mem_out, row_total, gate_logit, mem_keys, mem_values, retrieved):
    seq = lax.axis_size("seq")
    sections = lax.axis_size("section")
    position = lax.axis_index("seq")
    rows, width = grad_out.shape[1:]
    head_count = gate_logit.shape[1]
    dim = width // head_count
    kv_heads = mem_keys.shape[2] // dim
    heads = head_count // kv_heads
    mem_dev = mem_keys.shape[1]
    blocks = mem_dev // BLOCK
    group = min(kv_heads, seq // 2)
    own = kv_heads // group
    at = position % group
    home = position // group
    scale = dim ** (-0.5)

    def swapped(value, step):
        return lax.ppermute(value, "seq", [(p, p ^ step) for p in range(seq)])

    def delivered(value, step):
        pairs = [(s * seq + p, ((s - 1) % sections) * seq + (p ^ step)) for s in range(sections) for p in range(seq)]
        return lax.ppermute(value, ("section", "seq"), pairs)

    cut = (5 * blocks + 7) // 8
    cuts = [[(0, blocks)]] * (own - 1) + [[(0, cut), (cut, blocks)]]

    moved = own > 1
    chosen = retrieved[0]
    if moved:
        chosen = delivered(chosen, 0)

    def listed(i):
        source = chosen if i == own - 1 else retrieved[0]
        mine = lax.dynamic_index_in_dim(source, at * own + i, 0, keepdims=False)
        mine = jnp.stack(
            [lax.dynamic_index_in_dim(mine, home * group + (at ^ x), 0, keepdims=False) for x in range(group)]
        )
        holder, block = mine // blocks, mine % blocks
        piece = sum((block >= low).astype(jnp.int32) for low, _ in cuts[i][1:]) if len(cuts[i]) > 1 else 0 * block
        key = piece * seq * blocks + mine
        rank = jnp.sum(key[:, None, :] < key[:, :, None], axis=-1)
        order = jnp.arange(mine.shape[-1])
        low = sum((piece == j) * cuts[i][j][0] for j in range(len(cuts[i])))
        value = holder * MOST + block - low
        picks = jnp.sum(jnp.where(rank[:, :, None] == order, value[:, :, None], 0), axis=1).astype(jnp.int32)
        bounds = [jnp.sum(piece < j, axis=-1) for j in range(len(cuts[i]) + 1)]
        return picks, [
            jnp.stack([bounds[j], bounds[j + 1]], axis=1).astype(jnp.int32) for j in range(len(cuts[i]))
        ]

    gates = jax.nn.sigmoid(gate_logit[0])
    gathered, worked, latest, held = [], [], None, []

    def memory_of(i, hint):
        return pack(mem_keys[0], mem_values[0], hint, seq, own, group, dim, i, cuts[i])

    def queries_of(i):
        return prepare(grad_out[0], queries[0], mem_out[0], row_total[0], gates, at, kv_heads, dim, scale, own, i)

    def exchanged(packed, *first):
        sent = [after(value, *first) if first else value for value in packed]
        return [packed[0]] + [swapped(sent[x], x) for x in range(1, group)]

    memories = memory_of(0, at[None])
    asked = [queries_of(0)]
    for i in range(1, own):
        memories += memory_of(i, after(at[None], asked[-1][0]))
        asked.append(queries_of(i))
    coming = exchanged(asked[0], *memories[len(cuts[0]):], *[value[0] for value in asked[1:]])
    if moved:
        memories[-len(cuts[-1]):] = [delivered(value, 0) for value in memories[-len(cuts[-1]):]]
    for i in range(own):
        packed = coming
        pieces = []
        for _ in cuts[i]:
            piece = memories.pop(0)
            piece = piece if latest is None else after(piece, latest, *held)
            latest = lax.all_to_all(piece, "seq", split_axis=0, concat_axis=0, tiled=True)
            pieces.append(latest)
            held = packed
        picks, starts = listed(i)
        run = functools.partial(attend, picks=picks, heads=heads, dim=dim, scale=scale)
        acc = None
        for j in range(len(pieces) - 1):
            acc = run(packed, pieces[j], acc, starts=after(starts[j], *worked), last=False)
            worked = [acc]
        if i < own - 1:
            if i == own - 2:
                coming = [delivered(after(value, latest), x) for x, value in enumerate(asked[i + 1])]
            else:
                coming = exchanged(asked[i + 1], latest)
            done = run(packed, pieces[-1], acc, starts=after(starts[-1], *worked), last=True)
            worked = done[:1]
            gathered += [delivered(done[x], x) for x in range(group)]
            continue
        results, half = [None] * group, group // 2
        for low, high in ((half, group), (0, half)):
            bounds = after(starts[-1], *worked, *(gathered if low else []))
            done = run(packed[low:high], pieces[-1], acc, starts=bounds, last=True, first=low)
            worked = done[:1]
            for x in range(low, high):
                result = done[x - low]
                if not moved:
                    results[x] = delivered(result if low else after(result, results[x + half]), x)
                elif x:
                    results[x] = swapped(result if low else after(result, *results[half:]), x)
                else:
                    results[x] = result
    return assemble(gathered + results, at, own, group)[None]


def solution(mesh):
    return jax.shard_map(
        shards,
        mesh=mesh,
        in_specs=(
            P("section", "seq", None),
            P("section", "seq", None),
            P("section", "seq", None),
            P("section", "seq", None),
            P("section", None),
            P("section", "seq", None),
            P("section", "seq", None),
            P("section", None, None, None),
        ),
        out_specs=P("section", "seq", None),
        check_vma=False,
    )
```

```python
import functools
import math

import jax
import jax.numpy as jnp
from jax import lax
from jax.experimental import pallas as pl
from jax.experimental.pallas import tpu as pltpu
from jax.sharding import PartitionSpec as P

BLOCK = 128
PARTS = 3
STEPS = (8, 4)
MOST = 1 << 10
HINT = 16
VMEM_LIMIT = 48 * 1024 * 1024
VMEM_MOST = 60 * 1024 * 1024

NT = (((1,), (1,)), ((), ()))


def split_parts(value):
    terms = []
    for _ in range(PARTS):
        term = value.astype(jnp.bfloat16)
        terms.append(term.astype(jnp.float32))
        value = value - terms[-1]
    return terms


def narrow_kernel(own, index, at_ref, keys_ref, values_ref, out_ref):
    group, _, dim = out_ref.shape[1:]
    for device in range(group):
        head = device * own + index
        out_ref[0, device] = keys_ref[:, head * dim:(head + 1) * dim]
        out_ref[1, device] = values_ref[:, head * dim:(head + 1) * dim]


def narrow(mem_keys, mem_values, hint, own, group, dim, index):
    mem_dev, width = mem_keys.shape
    rows = pl.BlockSpec((BLOCK, width), lambda i, _: (i, 0))
    return pl.pallas_call(
        functools.partial(narrow_kernel, own, index),
        out_shape=jax.ShapeDtypeStruct((2, group, mem_dev, dim), mem_keys.dtype),
        grid_spec=pltpu.PrefetchScalarGridSpec(
            num_scalar_prefetch=1,
            grid=(mem_dev // BLOCK,),
            in_specs=[rows, rows],
            out_specs=pl.BlockSpec((2, group, BLOCK, dim), lambda i, _: (0, 0, i, 0)),
        ),
        compiler_params=pltpu.CompilerParams(vmem_limit_bytes=VMEM_MOST),
        cost_estimate=pl.CostEstimate(flops=0, bytes_accessed=6 * mem_dev * width // own, transcendentals=0),
    )(hint, mem_keys, mem_values)


def pack_kernel(own, group, index, spans, wide, *refs):
    sources, outs = refs[:2 if wide else 1], refs[2 if wide else 1:]
    dim = outs[0].shape[3]
    block = pl.program_id(0)
    for (low, high), out in zip(spans, outs):

        @pl.when((block >= low) & (block < high))
        def _(out=out):
            for device in range(out.shape[0]):
                head = device % group * own + index
                for half in range(2):
                    if wide:
                        out[device, half] = sources[half][:, head * dim:(head + 1) * dim]
                    else:
                        out[device, half] = sources[0][half, device % group]


def pack(sources, seq, own, group, dim, index, spans):
    wide = len(sources) == 2
    mem_dev = sources[0].shape[0 if wide else 2]
    if wide:
        specs = [pl.BlockSpec((BLOCK, source.shape[1]), lambda i: (i, 0)) for source in sources]
    else:
        specs = [pl.BlockSpec((2, group, BLOCK, dim), lambda i: (0, 0, i, 0))]

    def place(low, high):
        return pl.BlockSpec((seq, 2, BLOCK, dim), lambda i: (0, 0, jnp.clip(i - low, 0, high - low - 1), 0))

    outs = pl.pallas_call(
        functools.partial(pack_kernel, own, group, index, spans, wide),
        out_shape=[
            jax.ShapeDtypeStruct((seq, 2, (high - low) * BLOCK, dim), sources[0].dtype) for low, high in spans
        ],
        grid=(mem_dev // BLOCK,),
        in_specs=specs,
        out_specs=[place(low, high) for low, high in spans],
        compiler_params=pltpu.CompilerParams(vmem_limit_bytes=VMEM_MOST),
        cost_estimate=pl.CostEstimate(flops=0, bytes_accessed=8 * mem_dev * dim * group, transcendentals=0),
    )(*sources)
    return [out.reshape(seq, -1, dim) for out in outs]


def prepare_kernel(heads, dim, scale, own, index, gate_ref, at_ref, grad_ref, query_ref, out_ref, total_ref, *packed_refs):
    rows = grad_ref.shape[0]
    count = total_ref.shape[1]
    logs = split_parts(jnp.log2(total_ref[...].astype(jnp.float32)) - math.log2(scale))
    target = lax.broadcasted_iota(jnp.int32, (count, dim), 1)
    lane = lax.broadcasted_iota(jnp.int32, (rows, dim), 1)
    for x, packed_ref in enumerate(packed_refs):
        head = (at_ref[0] ^ x) * own + index
        source = lax.broadcasted_iota(jnp.int32, (count, dim), 0) - head * heads
        mine = (source >= 0) & (source < heads)
        stats = jnp.zeros((rows, dim), jnp.float32)
        for part, term in enumerate(logs):
            chosen = jnp.where(mine & (target == source + (2 * part + 1) * heads), 1.0, 0.0).astype(jnp.bfloat16)
            stats += jnp.dot(term.astype(jnp.bfloat16), chosen, preferred_element_type=jnp.float32)
        for h in range(heads):
            columns = pl.ds(pl.multiple_of((head * heads + h) * dim, dim), dim)
            gated = (gate_ref[head * heads + h] * grad_ref[:, columns].astype(jnp.float32)).astype(jnp.bfloat16)
            packed_ref[h * rows:(h + 1) * rows, :] = query_ref[:, columns]
            packed_ref[(heads + h) * rows:(heads + h + 1) * rows, :] = gated
            product = gated.astype(jnp.float32) * out_ref[:, columns].astype(jnp.float32)
            delta = jnp.sum(product, axis=1, keepdims=True)
            for part, term in enumerate(split_parts(delta)):
                stats = jnp.where(lane == 2 * part * heads + h, term, stats)
        packed_ref[2 * heads * rows:, :] = stats.astype(jnp.bfloat16)


def prepare(grad_out, queries, mem_out, row_total, gates, at, kv_heads, dim, scale, own, index):
    rows, width = grad_out.shape
    heads = width // dim // kv_heads
    group = kv_heads // own
    span = 2 * heads * rows + rows
    wide = pl.BlockSpec((rows, width), lambda i, *_: (0, 0))
    return pl.pallas_call(
        functools.partial(prepare_kernel, heads, dim, scale, own, index),
        out_shape=[jax.ShapeDtypeStruct((span, dim), jnp.bfloat16)] * group,
        grid_spec=pltpu.PrefetchScalarGridSpec(
            num_scalar_prefetch=2,
            grid=(1,),
            in_specs=[wide, wide, wide, pl.BlockSpec(row_total.shape, lambda i, *_: (0, 0))],
            out_specs=[pl.BlockSpec((span, dim), lambda i, *_: (0, 0))] * group,
        ),
        compiler_params=pltpu.CompilerParams(vmem_limit_bytes=VMEM_LIMIT),
        cost_estimate=pl.CostEstimate(flops=rows * width * 4, bytes_accessed=rows * width * 12 // own, transcendentals=0),
    )(gates, at[None], grad_out, queries, mem_out, row_total)


def attend_kernel(heads, dim, rows, scale, first, tiles, fresh, last, picks_ref, starts_ref, *refs):
    packed_refs, memory_ref = refs[:tiles], refs[tiles]
    acc_in = None if fresh else refs[tiles + 1]
    out_refs, (query_ref, log_ref, delta_ref, total) = refs[tiles + (1 if fresh else 2):-4], refs[-4:]
    step = pl.program_id(0)
    tile = first + step
    blocks = memory_ref.shape[1] // 2
    count = heads * rows

    if fresh:
        total[...] = jnp.zeros_like(total)
    else:
        total[...] = acc_in[0]

    for x, packed in enumerate(packed_refs):

        @pl.when(step == x)
        def _(packed=packed):
            query_ref[...] = packed[...]

    terms = query_ref[2 * count:, :].astype(jnp.float32)
    stats = terms
    for part in range(1, PARTS):
        stats = stats + pltpu.roll(terms, dim - 2 * part * heads, 1)
    for h in range(heads):
        for target, lane in ((delta_ref, h), (log_ref, heads + h)):
            target[h * rows:(h + 1) * rows, :] = jnp.broadcast_to(stats[:, lane:lane + 1], (rows, dim))

    low = starts_ref[tile, 0]
    high = starts_ref[tile, 1]
    exponent = scale * math.log2(math.e)

    def add(here, number, checked):
        sides = []
        for two in range(0, number, 2):
            keys, values = [], []
            for j in (two, two + 1):
                valid = here + j < high
                pick = picks_ref[tile, jnp.where(valid, here + j, here) if checked else here + j]
                holder = pick // MOST
                block = pick % MOST
                key = memory_ref[holder, block]
                keys.append(jnp.where(valid, key, jnp.zeros_like(key)) if checked and j else key)
                values.append(memory_ref[holder, blocks + block])
            sides.append((jnp.concatenate(keys, axis=0), jnp.concatenate(values, axis=0)))

        def products(side):
            keys, values = side
            scores = lax.dot_general(query_ref[:count, :], keys, NT, preferred_element_type=jnp.float32)
            grad_probs = lax.dot_general(query_ref[count:2 * count, :], values, NT, preferred_element_type=jnp.float32)
            return scores, grad_probs

        ahead = products(sides[0])
        gained = None
        for at, (keys, _) in enumerate(sides):
            scores, grad_probs = ahead
            if at + 1 < len(sides):
                ahead = products(sides[at + 1])
            log_wide = jnp.concatenate([log_ref[...]] * 2, axis=1)
            delta_wide = jnp.concatenate([delta_ref[...]] * 2, axis=1)
            probs = jnp.exp2(scores * exponent - log_wide)
            grad_scores = (probs * (grad_probs - delta_wide)).astype(jnp.bfloat16)
            part = jnp.dot(grad_scores, keys, preferred_element_type=jnp.float32)
            gained = part if gained is None else gained + part
        total[...] += gained

    for number in STEPS:
        full = (high - low) // number

        def many(turn, carry, low=low, number=number):
            add(low + number * turn, number, False)
            return carry

        lax.fori_loop(0, full, many, 0)
        low = low + number * full

    def few(turn, carry):
        add(low + 2 * turn, 2, True)
        return carry

    lax.fori_loop(0, (high - low + 1) // 2, few, 0)

    if not last:
        out_refs[0][0] = total[...]
        return
    for x, out_ref in enumerate(out_refs):

        @pl.when(step == x)
        def _(out_ref=out_ref):
            for h in range(heads):
                out_ref[:, h * dim:(h + 1) * dim] = total[h * rows:(h + 1) * rows, :].astype(jnp.bfloat16)


def attend(packed, memory, acc, picks, starts, heads, dim, scale, last, first=0):
    tiles = len(packed)
    span = packed[0].shape[0]
    rows = span // (2 * heads + 1)
    fresh = acc is None
    width = heads * rows
    holders = memory.shape[0]
    memory = memory.reshape(holders, -1, BLOCK, dim)
    acc_spec = pl.BlockSpec((1, width, dim), lambda t, *_: (first + t, 0, 0))
    if last:
        out_shape = [jax.ShapeDtypeStruct((rows, heads * dim), jnp.bfloat16)] * tiles
        out_spec = [pl.BlockSpec((rows, heads * dim), lambda t, *_: (0, 0))] * tiles
    else:
        out_shape = jax.ShapeDtypeStruct((tiles, width, dim), jnp.float32)
        out_spec = acc_spec
    flops = tiles * holders * memory.shape[1] * (BLOCK // 4) * width * dim * 6
    return pl.pallas_call(
        functools.partial(attend_kernel, heads, dim, rows, scale, first, tiles, fresh, last),
        out_shape=out_shape,
        grid_spec=pltpu.PrefetchScalarGridSpec(
            num_scalar_prefetch=2,
            grid=(tiles,),
            in_specs=[pl.BlockSpec((span, dim), lambda t, *_: (0, 0))] * tiles
            + [pl.BlockSpec(memory.shape, lambda t, *_: (0, 0, 0, 0))]
            + ([] if fresh else [acc_spec]),
            out_specs=out_spec,
            scratch_shapes=[pltpu.VMEM((span, dim), jnp.bfloat16)] + [pltpu.VMEM((width, dim), jnp.float32)] * 3,
        ),
        compiler_params=pltpu.CompilerParams(vmem_limit_bytes=VMEM_MOST),
        cost_estimate=pl.CostEstimate(flops=flops * 4, bytes_accessed=0, transcendentals=0),
    )(picks, starts, *packed, memory, *([] if fresh else [acc]))


def assemble_kernel(own, group, at_ref, *refs):
    pieces, out_ref = refs[:-1], refs[-1]
    span = pieces[0].shape[1]
    for index in range(own):
        for x in range(group):
            column = pl.multiple_of(((at_ref[0] ^ x) * own + index) * span, span)
            out_ref[:, pl.ds(column, span)] = pieces[index * group + x][...]


def assemble(pieces, at, own, group):
    rows, span = pieces[0].shape
    width = own * group * span
    return pl.pallas_call(
        functools.partial(assemble_kernel, own, group),
        out_shape=jax.ShapeDtypeStruct((rows, width), pieces[0].dtype),
        grid_spec=pltpu.PrefetchScalarGridSpec(
            num_scalar_prefetch=1,
            grid=(1,),
            in_specs=[pl.BlockSpec((rows, span), lambda i, _: (0, 0))] * len(pieces),
            out_specs=pl.BlockSpec((rows, width), lambda i, _: (0, 0)),
        ),
        compiler_params=pltpu.CompilerParams(vmem_limit_bytes=VMEM_LIMIT),
        cost_estimate=pl.CostEstimate(flops=0, bytes_accessed=4 * rows * width, transcendentals=0),
    )(at[None], *pieces)


def after(value, *others):
    anywhere = pl.BlockSpec(memory_space=pl.ANY)
    corners = [
        pl.BlockSpec((1,) * (other.ndim - 2) + (HINT, 128), lambda i, count=other.ndim: (0,) * count) for other in others
    ]
    return pl.pallas_call(
        lambda *refs: None,
        out_shape=jax.ShapeDtypeStruct(value.shape, value.dtype),
        grid=(1,),
        in_specs=[anywhere] + corners,
        out_specs=anywhere,
        input_output_aliases={0: 0},
        cost_estimate=pl.CostEstimate(flops=0, bytes_accessed=0, transcendentals=0),
    )(value, *others)


def shards(grad_out, queries, mem_out, row_total, gate_logit, mem_keys, mem_values, retrieved):
    seq = lax.axis_size("seq")
    sections = lax.axis_size("section")
    position = lax.axis_index("seq")
    rows, width = grad_out.shape[1:]
    head_count = gate_logit.shape[1]
    dim = width // head_count
    kv_heads = mem_keys.shape[2] // dim
    heads = head_count // kv_heads
    mem_dev = mem_keys.shape[1]
    blocks = mem_dev // BLOCK
    group = min(kv_heads, seq // 2)
    own = kv_heads // group
    at = position % group
    home = position // group
    scale = dim ** (-0.5)

    def swapped(value, step):
        return lax.ppermute(value, "seq", [(p, p ^ step) for p in range(seq)])

    def delivered(value, step):
        pairs = [(s * seq + p, ((s - 1) % sections) * seq + (p ^ step)) for s in range(sections) for p in range(seq)]
        return lax.ppermute(value, ("section", "seq"), pairs)

    cut = (5 * blocks + 7) // 8
    cuts = [[(0, blocks)]] * (own - 1) + [[(0, cut), (cut, blocks)]]

    moved = own > 1
    chosen = retrieved[0]
    if moved:
        chosen = delivered(chosen, 0)

    def listed(i):
        source = chosen if i == own - 1 else retrieved[0]
        mine = lax.dynamic_index_in_dim(source, at * own + i, 0, keepdims=False)
        mine = jnp.stack(
            [lax.dynamic_index_in_dim(mine, home * group + (at ^ x), 0, keepdims=False) for x in range(group)]
        )
        holder, block = mine // blocks, mine % blocks
        piece = sum((block >= low).astype(jnp.int32) for low, _ in cuts[i][1:]) if len(cuts[i]) > 1 else 0 * block
        key = piece * seq * blocks + mine
        rank = jnp.sum(key[:, None, :] < key[:, :, None], axis=-1)
        order = jnp.arange(mine.shape[-1])
        low = sum((piece == j) * cuts[i][j][0] for j in range(len(cuts[i])))
        value = holder * MOST + block - low
        picks = jnp.sum(jnp.where(rank[:, :, None] == order, value[:, :, None], 0), axis=1).astype(jnp.int32)
        bounds = [jnp.sum(piece < j, axis=-1) for j in range(len(cuts[i]) + 1)]
        return picks, [
            jnp.stack([bounds[j], bounds[j + 1]], axis=1).astype(jnp.int32) for j in range(len(cuts[i]))
        ]

    gates = jax.nn.sigmoid(gate_logit[0])
    gathered, worked, latest, held = [], [], None, []

    def memory_of(i, sources):
        return pack(sources, seq, own, group, dim, i, cuts[i])

    def queries_of(i):
        return prepare(grad_out[0], queries[0], mem_out[0], row_total[0], gates, at, kv_heads, dim, scale, own, i)

    def exchanged(packed, *first):
        sent = [after(value, *first) if first else value for value in packed]
        return [packed[0]] + [swapped(sent[x], x) for x in range(1, group)]

    memories = memory_of(0, [mem_keys[0], mem_values[0]])
    asked = [queries_of(0)]
    ready = []
    for i in range(1, own):
        rows_of = narrow(mem_keys[0], mem_values[0], after(at[None], asked[-1][0]), own, group, dim, i)
        asked.append(queries_of(i))
        ready += [rows_of, asked[i][0]]
        memories += memory_of(i, [delivered(rows_of, 0) if i == own - 1 else rows_of])
    coming = exchanged(asked[0], *ready)
    for i in range(own):
        packed = coming
        pieces = []
        for _ in cuts[i]:
            piece = memories.pop(0)
            piece = piece if latest is None else after(piece, latest, *held)
            latest = lax.all_to_all(piece, "seq", split_axis=0, concat_axis=0, tiled=True)
            pieces.append(latest)
            held = packed
        picks, starts = listed(i)
        run = functools.partial(attend, picks=picks, heads=heads, dim=dim, scale=scale)
        acc = None
        for j in range(len(pieces) - 1):
            acc = run(packed, pieces[j], acc, starts=after(starts[j], *worked), last=False)
            worked = [acc]
        if i < own - 1:
            if i == own - 2:
                coming = [delivered(after(value, latest), x) for x, value in enumerate(asked[i + 1])]
            else:
                coming = exchanged(asked[i + 1], latest)
            done = run(packed, pieces[-1], acc, starts=after(starts[-1], *worked, memories[0]), last=True)
            worked = done[:1]
            gathered += [delivered(done[x], x) for x in range(group)]
            continue
        results, half = [None] * group, group // 2
        for low, high in ((half, group), (0, half)):
            bounds = after(starts[-1], *worked, *(gathered if low else []))
            done = run(packed[low:high], pieces[-1], acc, starts=bounds, last=True, first=low)
            worked = done[:1]
            for x in range(low, high):
                result = done[x - low]
                if not moved:
                    results[x] = delivered(result if low else after(result, results[x + half]), x)
                elif x:
                    results[x] = swapped(result if low else after(result, *results[half:]), x)
                else:
                    results[x] = result
    return assemble(gathered + results, at, own, group)[None]


def solution(mesh):
    return jax.shard_map(
        shards,
        mesh=mesh,
        in_specs=(
            P("section", "seq", None),
            P("section", "seq", None),
            P("section", "seq", None),
            P("section", "seq", None),
            P("section", None),
            P("section", "seq", None),
            P("section", "seq", None),
            P("section", None, None, None),
        ),
        out_specs=P("section", "seq", None),
        check_vma=False,
    )
```

```python
import functools
import math

import jax
import jax.numpy as jnp
from jax import lax
from jax.experimental import pallas as pl
from jax.experimental.pallas import tpu as pltpu
from jax.sharding import PartitionSpec as P

BLOCK = 128
PARTS = 3
STEPS = (8, 4)
MOST = 1 << 10
HINT = 16
VMEM_LIMIT = 48 * 1024 * 1024
VMEM_MOST = 60 * 1024 * 1024

NT = (((1,), (1,)), ((), ()))


def split_parts(value):
    terms = []
    for _ in range(PARTS):
        term = value.astype(jnp.bfloat16)
        terms.append(term.astype(jnp.float32))
        value = value - terms[-1]
    return terms


def narrow_kernel(own, index, at_ref, keys_ref, values_ref, out_ref):
    group, _, dim = out_ref.shape[1:]
    for device in range(group):
        head = device * own + index
        out_ref[0, device] = keys_ref[:, head * dim:(head + 1) * dim]
        out_ref[1, device] = values_ref[:, head * dim:(head + 1) * dim]


def narrow(mem_keys, mem_values, hint, own, group, dim, index):
    mem_dev, width = mem_keys.shape
    rows = pl.BlockSpec((BLOCK, width), lambda i, _: (i, 0))
    return pl.pallas_call(
        functools.partial(narrow_kernel, own, index),
        out_shape=jax.ShapeDtypeStruct((2, group, mem_dev, dim), mem_keys.dtype),
        grid_spec=pltpu.PrefetchScalarGridSpec(
            num_scalar_prefetch=1,
            grid=(mem_dev // BLOCK,),
            in_specs=[rows, rows],
            out_specs=pl.BlockSpec((2, group, BLOCK, dim), lambda i, _: (0, 0, i, 0)),
        ),
        compiler_params=pltpu.CompilerParams(vmem_limit_bytes=VMEM_MOST),
        cost_estimate=pl.CostEstimate(flops=0, bytes_accessed=6 * mem_dev * width // own, transcendentals=0),
    )(hint, mem_keys, mem_values)


def pack_kernel(own, group, index, spans, wide, *refs):
    sources, outs = refs[:2 if wide else 1], refs[2 if wide else 1:]
    dim = outs[0].shape[3]
    block = pl.program_id(0)
    for (low, high), out in zip(spans, outs):

        @pl.when((block >= low) & (block < high))
        def _(out=out):
            for device in range(out.shape[0]):
                head = device % group * own + index
                for half in range(2):
                    if wide:
                        out[device, half] = sources[half][:, head * dim:(head + 1) * dim]
                    else:
                        out[device, half] = sources[0][half, device % group]


def pack(sources, seq, own, group, dim, index, spans):
    wide = len(sources) == 2
    mem_dev = sources[0].shape[0 if wide else 2]
    if wide:
        specs = [pl.BlockSpec((BLOCK, source.shape[1]), lambda i: (i, 0)) for source in sources]
    else:
        specs = [pl.BlockSpec((2, group, BLOCK, dim), lambda i: (0, 0, i, 0))]

    def place(low, high):
        return pl.BlockSpec((seq, 2, BLOCK, dim), lambda i: (0, 0, jnp.clip(i - low, 0, high - low - 1), 0))

    outs = pl.pallas_call(
        functools.partial(pack_kernel, own, group, index, spans, wide),
        out_shape=[
            jax.ShapeDtypeStruct((seq, 2, (high - low) * BLOCK, dim), sources[0].dtype) for low, high in spans
        ],
        grid=(mem_dev // BLOCK,),
        in_specs=specs,
        out_specs=[place(low, high) for low, high in spans],
        compiler_params=pltpu.CompilerParams(vmem_limit_bytes=VMEM_MOST),
        cost_estimate=pl.CostEstimate(flops=0, bytes_accessed=8 * mem_dev * dim * group, transcendentals=0),
    )(*sources)
    return [out.reshape(seq, -1, dim) for out in outs]


def prepare_kernel(heads, dim, scale, own, index, gate_ref, at_ref, grad_ref, query_ref, out_ref, total_ref, *packed_refs):
    rows = grad_ref.shape[0]
    count = total_ref.shape[1]
    logs = split_parts(jnp.log2(total_ref[...].astype(jnp.float32)) - math.log2(scale))
    target = lax.broadcasted_iota(jnp.int32, (count, dim), 1)
    lane = lax.broadcasted_iota(jnp.int32, (rows, dim), 1)
    for x, packed_ref in enumerate(packed_refs):
        head = (at_ref[0] ^ x) * own + index
        source = lax.broadcasted_iota(jnp.int32, (count, dim), 0) - head * heads
        mine = (source >= 0) & (source < heads)
        stats = jnp.zeros((rows, dim), jnp.float32)
        for part, term in enumerate(logs):
            chosen = jnp.where(mine & (target == source + (2 * part + 1) * heads), 1.0, 0.0).astype(jnp.bfloat16)
            stats += jnp.dot(term.astype(jnp.bfloat16), chosen, preferred_element_type=jnp.float32)
        for h in range(heads):
            columns = pl.ds(pl.multiple_of((head * heads + h) * dim, dim), dim)
            gated = (gate_ref[head * heads + h] * grad_ref[:, columns].astype(jnp.float32)).astype(jnp.bfloat16)
            packed_ref[h * rows:(h + 1) * rows, :] = query_ref[:, columns]
            packed_ref[(heads + h) * rows:(heads + h + 1) * rows, :] = gated
            product = gated.astype(jnp.float32) * out_ref[:, columns].astype(jnp.float32)
            delta = jnp.sum(product, axis=1, keepdims=True)
            for part, term in enumerate(split_parts(delta)):
                stats = jnp.where(lane == 2 * part * heads + h, term, stats)
        packed_ref[2 * heads * rows:, :] = stats.astype(jnp.bfloat16)


def prepare(grad_out, queries, mem_out, row_total, gates, at, kv_heads, dim, scale, own, index):
    rows, width = grad_out.shape
    heads = width // dim // kv_heads
    group = kv_heads // own
    span = 2 * heads * rows + rows
    wide = pl.BlockSpec((rows, width), lambda i, *_: (0, 0))
    return pl.pallas_call(
        functools.partial(prepare_kernel, heads, dim, scale, own, index),
        out_shape=[jax.ShapeDtypeStruct((span, dim), jnp.bfloat16)] * group,
        grid_spec=pltpu.PrefetchScalarGridSpec(
            num_scalar_prefetch=2,
            grid=(1,),
            in_specs=[wide, wide, wide, pl.BlockSpec(row_total.shape, lambda i, *_: (0, 0))],
            out_specs=[pl.BlockSpec((span, dim), lambda i, *_: (0, 0))] * group,
        ),
        compiler_params=pltpu.CompilerParams(vmem_limit_bytes=VMEM_LIMIT),
        cost_estimate=pl.CostEstimate(flops=rows * width * 4, bytes_accessed=rows * width * 12 // own, transcendentals=0),
    )(gates, at[None], grad_out, queries, mem_out, row_total)


def attend_kernel(heads, dim, rows, scale, first, tiles, fresh, last, picks_ref, starts_ref, *refs):
    packed_refs, memory_ref = refs[:tiles], refs[tiles]
    acc_in = None if fresh else refs[tiles + 1]
    out_refs, (query_ref, log_ref, delta_ref, total) = refs[tiles + (1 if fresh else 2):-4], refs[-4:]
    step = pl.program_id(0)
    tile = first + step
    blocks = memory_ref.shape[1] // 2
    count = heads * rows

    if fresh:
        total[...] = jnp.zeros_like(total)
    else:
        total[...] = acc_in[0]

    for x, packed in enumerate(packed_refs):

        @pl.when(step == x)
        def _(packed=packed):
            query_ref[...] = packed[...]

    terms = query_ref[2 * count:, :].astype(jnp.float32)
    stats = terms
    for part in range(1, PARTS):
        stats = stats + pltpu.roll(terms, dim - 2 * part * heads, 1)
    for h in range(heads):
        for target, lane in ((delta_ref, h), (log_ref, heads + h)):
            target[h * rows:(h + 1) * rows, :] = jnp.broadcast_to(stats[:, lane:lane + 1], (rows, dim))

    low = starts_ref[tile, 0]
    high = starts_ref[tile, 1]
    exponent = scale * math.log2(math.e)

    def add(here, number, checked):
        sides = []
        for two in range(0, number, 2):
            keys, values = [], []
            for j in (two, two + 1):
                valid = here + j < high
                pick = picks_ref[tile, jnp.where(valid, here + j, here) if checked else here + j]
                holder = pick // MOST
                block = pick % MOST
                key = memory_ref[holder, block]
                keys.append(jnp.where(valid, key, jnp.zeros_like(key)) if checked and j else key)
                values.append(memory_ref[holder, blocks + block])
            sides.append((jnp.concatenate(keys, axis=0), jnp.concatenate(values, axis=0)))

        def products(side):
            keys, values = side
            scores = lax.dot_general(query_ref[:count, :], keys, NT, preferred_element_type=jnp.float32)
            grad_probs = lax.dot_general(query_ref[count:2 * count, :], values, NT, preferred_element_type=jnp.float32)
            return scores, grad_probs

        ahead = products(sides[0])
        gained = None
        for at, (keys, _) in enumerate(sides):
            scores, grad_probs = ahead
            if at + 1 < len(sides):
                ahead = products(sides[at + 1])
            log_wide = jnp.concatenate([log_ref[...]] * 2, axis=1)
            delta_wide = jnp.concatenate([delta_ref[...]] * 2, axis=1)
            probs = jnp.exp2(scores * exponent - log_wide)
            grad_scores = (probs * (grad_probs - delta_wide)).astype(jnp.bfloat16)
            part = jnp.dot(grad_scores, keys, preferred_element_type=jnp.float32)
            gained = part if gained is None else gained + part
        total[...] += gained

    for number in STEPS:
        full = (high - low) // number

        def many(turn, carry, low=low, number=number):
            add(low + number * turn, number, False)
            return carry

        lax.fori_loop(0, full, many, 0)
        low = low + number * full

    def few(turn, carry):
        add(low + 2 * turn, 2, True)
        return carry

    lax.fori_loop(0, (high - low + 1) // 2, few, 0)

    if not last:
        out_refs[0][0] = total[...]
        return
    for x, out_ref in enumerate(out_refs):

        @pl.when(step == x)
        def _(out_ref=out_ref):
            for h in range(heads):
                out_ref[:, h * dim:(h + 1) * dim] = total[h * rows:(h + 1) * rows, :].astype(jnp.bfloat16)


def attend(packed, memory, acc, picks, starts, heads, dim, scale, last, first=0):
    tiles = len(packed)
    span = packed[0].shape[0]
    rows = span // (2 * heads + 1)
    fresh = acc is None
    width = heads * rows
    holders = memory.shape[0]
    memory = memory.reshape(holders, -1, BLOCK, dim)
    acc_spec = pl.BlockSpec((1, width, dim), lambda t, *_: (first + t, 0, 0))
    if last:
        out_shape = [jax.ShapeDtypeStruct((rows, heads * dim), jnp.bfloat16)] * tiles
        out_spec = [pl.BlockSpec((rows, heads * dim), lambda t, *_: (0, 0))] * tiles
    else:
        out_shape = jax.ShapeDtypeStruct((tiles, width, dim), jnp.float32)
        out_spec = acc_spec
    flops = tiles * holders * memory.shape[1] * (BLOCK // 4) * width * dim * 6
    return pl.pallas_call(
        functools.partial(attend_kernel, heads, dim, rows, scale, first, tiles, fresh, last),
        out_shape=out_shape,
        grid_spec=pltpu.PrefetchScalarGridSpec(
            num_scalar_prefetch=2,
            grid=(tiles,),
            in_specs=[pl.BlockSpec((span, dim), lambda t, *_: (0, 0))] * tiles
            + [pl.BlockSpec(memory.shape, lambda t, *_: (0, 0, 0, 0))]
            + ([] if fresh else [acc_spec]),
            out_specs=out_spec,
            scratch_shapes=[pltpu.VMEM((span, dim), jnp.bfloat16)] + [pltpu.VMEM((width, dim), jnp.float32)] * 3,
        ),
        compiler_params=pltpu.CompilerParams(vmem_limit_bytes=VMEM_MOST),
        cost_estimate=pl.CostEstimate(flops=flops * 4, bytes_accessed=0, transcendentals=0),
    )(picks, starts, *packed, memory, *([] if fresh else [acc]))


def assemble_kernel(own, group, at_ref, *refs):
    pieces, out_ref = refs[:-1], refs[-1]
    span = pieces[0].shape[1]
    for index in range(own):
        for x in range(group):
            column = pl.multiple_of(((at_ref[0] ^ x) * own + index) * span, span)
            out_ref[:, pl.ds(column, span)] = pieces[index * group + x][...]


def assemble(pieces, at, own, group):
    rows, span = pieces[0].shape
    width = own * group * span
    part = rows // 4
    return pl.pallas_call(
        functools.partial(assemble_kernel, own, group),
        out_shape=jax.ShapeDtypeStruct((rows, width), pieces[0].dtype),
        grid_spec=pltpu.PrefetchScalarGridSpec(
            num_scalar_prefetch=1,
            grid=(rows // part,),
            in_specs=[pl.BlockSpec((part, span), lambda i, _: (i, 0))] * len(pieces),
            out_specs=pl.BlockSpec((part, width), lambda i, _: (i, 0)),
        ),
        compiler_params=pltpu.CompilerParams(vmem_limit_bytes=VMEM_MOST),
        cost_estimate=pl.CostEstimate(flops=0, bytes_accessed=4 * rows * width, transcendentals=0),
    )(at[None], *pieces)


def after(value, *others):
    anywhere = pl.BlockSpec(memory_space=pl.ANY)
    corners = [
        pl.BlockSpec((1,) * (other.ndim - 2) + (HINT, 128), lambda i, count=other.ndim: (0,) * count) for other in others
    ]
    return pl.pallas_call(
        lambda *refs: None,
        out_shape=jax.ShapeDtypeStruct(value.shape, value.dtype),
        grid=(1,),
        in_specs=[anywhere] + corners,
        out_specs=anywhere,
        input_output_aliases={0: 0},
        cost_estimate=pl.CostEstimate(flops=0, bytes_accessed=0, transcendentals=0),
    )(value, *others)


def shards(grad_out, queries, mem_out, row_total, gate_logit, mem_keys, mem_values, retrieved):
    seq = lax.axis_size("seq")
    sections = lax.axis_size("section")
    position = lax.axis_index("seq")
    rows, width = grad_out.shape[1:]
    head_count = gate_logit.shape[1]
    dim = width // head_count
    kv_heads = mem_keys.shape[2] // dim
    heads = head_count // kv_heads
    mem_dev = mem_keys.shape[1]
    blocks = mem_dev // BLOCK
    group = min(kv_heads, seq // 2)
    own = kv_heads // group
    at = position % group
    home = position // group
    scale = dim ** (-0.5)

    def swapped(value, step):
        return lax.ppermute(value, "seq", [(p, p ^ step) for p in range(seq)])

    def delivered(value, step):
        pairs = [(s * seq + p, ((s - 1) % sections) * seq + (p ^ step)) for s in range(sections) for p in range(seq)]
        return lax.ppermute(value, ("section", "seq"), pairs)

    cut = (5 * blocks + 7) // 8
    cuts = [[(0, blocks)]] * (own - 1) + [[(0, cut), (cut, blocks)]]

    moved = own > 1
    chosen = retrieved[0]
    if moved:
        chosen = delivered(chosen, 0)

    def listed(i):
        source = chosen if i == own - 1 else retrieved[0]
        mine = lax.dynamic_index_in_dim(source, at * own + i, 0, keepdims=False)
        mine = jnp.stack(
            [lax.dynamic_index_in_dim(mine, home * group + (at ^ x), 0, keepdims=False) for x in range(group)]
        )
        holder, block = mine // blocks, mine % blocks
        piece = sum((block >= low).astype(jnp.int32) for low, _ in cuts[i][1:]) if len(cuts[i]) > 1 else 0 * block
        key = piece * seq * blocks + mine
        rank = jnp.sum(key[:, None, :] < key[:, :, None], axis=-1)
        order = jnp.arange(mine.shape[-1])
        low = sum((piece == j) * cuts[i][j][0] for j in range(len(cuts[i])))
        value = holder * MOST + block - low
        picks = jnp.sum(jnp.where(rank[:, :, None] == order, value[:, :, None], 0), axis=1).astype(jnp.int32)
        bounds = [jnp.sum(piece < j, axis=-1) for j in range(len(cuts[i]) + 1)]
        return picks, [
            jnp.stack([bounds[j], bounds[j + 1]], axis=1).astype(jnp.int32) for j in range(len(cuts[i]))
        ]

    gates = jax.nn.sigmoid(gate_logit[0])
    gathered, worked, latest, held = [], [], None, []

    def memory_of(i, sources):
        return pack(sources, seq, own, group, dim, i, cuts[i])

    def queries_of(i):
        return prepare(grad_out[0], queries[0], mem_out[0], row_total[0], gates, at, kv_heads, dim, scale, own, i)

    def exchanged(packed):
        return [packed[0]] + [swapped(packed[x], x) for x in range(1, group)]

    memories = memory_of(0, [mem_keys[0], mem_values[0]])
    asked = [queries_of(i) for i in range(own)]
    for i in range(1, own):
        rows_of = narrow(mem_keys[0], mem_values[0], after(at[None], asked[i][0]), own, group, dim, i)
        memories += memory_of(i, [delivered(rows_of, 0) if i == own - 1 else rows_of])
    coming = exchanged(asked[0])
    for i in range(own):
        packed = coming
        pieces = []
        for _ in cuts[i]:
            piece = memories.pop(0)
            piece = piece if latest is None else after(piece, latest, *held)
            latest = lax.all_to_all(piece, "seq", split_axis=0, concat_axis=0, tiled=True)
            pieces.append(latest)
            held = packed
        picks, starts = listed(i)
        run = functools.partial(attend, picks=picks, heads=heads, dim=dim, scale=scale)
        acc = None
        for j in range(len(pieces) - 1):
            acc = run(packed, pieces[j], acc, starts=after(starts[j], *worked), last=False)
            worked = [acc]
        if i < own - 1:
            if i == own - 2:
                coming = [delivered(value, x) for x, value in enumerate(asked[i + 1])]
            else:
                coming = exchanged(asked[i + 1])
            done = run(packed, pieces[-1], acc, starts=after(starts[-1], *worked, memories[0]), last=True)
            worked = done[:1]
            gathered += [delivered(done[x], x) for x in range(group)]
            continue
        results, half = [None] * group, group // 2
        for low, high in ((half, group), (0, half)):
            bounds = after(starts[-1], *worked, *(gathered if low else []))
            done = run(packed[low:high], pieces[-1], acc, starts=bounds, last=True, first=low)
            worked = done[:1]
            for x in range(low, high):
                result = done[x - low]
                if not moved:
                    results[x] = delivered(result if low else after(result, results[x + half]), x)
                elif x:
                    results[x] = swapped(result if low else after(result, *results[half:]), x)
                else:
                    results[x] = result
    return assemble(gathered + results, at, own, group)[None]


def solution(mesh):
    return jax.shard_map(
        shards,
        mesh=mesh,
        in_specs=(
            P("section", "seq", None),
            P("section", "seq", None),
            P("section", "seq", None),
            P("section", "seq", None),
            P("section", None),
            P("section", "seq", None),
            P("section", "seq", None),
            P("section", None, None, None),
        ),
        out_specs=P("section", "seq", None),
        check_vma=False,
    )
```

```python
import functools
import math

import jax
import jax.numpy as jnp
from jax import lax
from jax.experimental import pallas as pl
from jax.experimental.pallas import tpu as pltpu
from jax.sharding import PartitionSpec as P

BLOCK = 128
PARTS = 3
STEPS = (8, 4)
MOST = 1 << 10
HINT = 16
VMEM_LIMIT = 48 * 1024 * 1024
VMEM_MOST = 60 * 1024 * 1024

NT = (((1,), (1,)), ((), ()))


def split_parts(value):
    terms = []
    for _ in range(PARTS):
        term = value.astype(jnp.bfloat16)
        terms.append(term.astype(jnp.float32))
        value = value - terms[-1]
    return terms


def narrow_kernel(own, index, at_ref, keys_ref, values_ref, out_ref):
    group, _, dim = out_ref.shape[1:]
    for device in range(group):
        head = device * own + index
        out_ref[0, device] = keys_ref[:, head * dim:(head + 1) * dim]
        out_ref[1, device] = values_ref[:, head * dim:(head + 1) * dim]


def narrow(mem_keys, mem_values, hint, own, group, dim, index):
    mem_dev, width = mem_keys.shape
    rows = pl.BlockSpec((BLOCK, width), lambda i, _: (i, 0))
    return pl.pallas_call(
        functools.partial(narrow_kernel, own, index),
        out_shape=jax.ShapeDtypeStruct((2, group, mem_dev, dim), mem_keys.dtype),
        grid_spec=pltpu.PrefetchScalarGridSpec(
            num_scalar_prefetch=1,
            grid=(mem_dev // BLOCK,),
            in_specs=[rows, rows],
            out_specs=pl.BlockSpec((2, group, BLOCK, dim), lambda i, _: (0, 0, i, 0)),
        ),
        compiler_params=pltpu.CompilerParams(vmem_limit_bytes=VMEM_MOST),
        cost_estimate=pl.CostEstimate(flops=0, bytes_accessed=6 * mem_dev * width // own, transcendentals=0),
    )(hint, mem_keys, mem_values)


def pack_kernel(own, group, index, spans, wide, *refs):
    sources, outs = refs[:2 if wide else 1], refs[2 if wide else 1:]
    dim = outs[0].shape[3]
    block = pl.program_id(0)
    for (low, high), out in zip(spans, outs):

        @pl.when((block >= low) & (block < high))
        def _(out=out):
            for device in range(out.shape[0]):
                head = device % group * own + index
                for half in range(2):
                    if wide:
                        out[device, half] = sources[half][:, head * dim:(head + 1) * dim]
                    else:
                        out[device, half] = sources[0][half, device % group]


def pack(sources, seq, own, group, dim, index, spans):
    wide = len(sources) == 2
    mem_dev = sources[0].shape[0 if wide else 2]
    if wide:
        specs = [pl.BlockSpec((BLOCK, source.shape[1]), lambda i: (i, 0)) for source in sources]
    else:
        specs = [pl.BlockSpec((2, group, BLOCK, dim), lambda i: (0, 0, i, 0))]

    def place(low, high):
        return pl.BlockSpec((seq, 2, BLOCK, dim), lambda i: (0, 0, jnp.clip(i - low, 0, high - low - 1), 0))

    outs = pl.pallas_call(
        functools.partial(pack_kernel, own, group, index, spans, wide),
        out_shape=[
            jax.ShapeDtypeStruct((seq, 2, (high - low) * BLOCK, dim), sources[0].dtype) for low, high in spans
        ],
        grid=(mem_dev // BLOCK,),
        in_specs=specs,
        out_specs=[place(low, high) for low, high in spans],
        compiler_params=pltpu.CompilerParams(vmem_limit_bytes=VMEM_MOST),
        cost_estimate=pl.CostEstimate(flops=0, bytes_accessed=8 * mem_dev * dim * group, transcendentals=0),
    )(*sources)
    return [out.reshape(seq, -1, dim) for out in outs]


def prepare_kernel(heads, dim, scale, own, index, gate_ref, at_ref, grad_ref, query_ref, out_ref, total_ref, *packed_refs):
    rows = grad_ref.shape[0]
    count = total_ref.shape[1]
    logs = split_parts(jnp.log2(total_ref[...].astype(jnp.float32)) - math.log2(scale))
    target = lax.broadcasted_iota(jnp.int32, (count, dim), 1)
    lane = lax.broadcasted_iota(jnp.int32, (rows, dim), 1)
    for x, packed_ref in enumerate(packed_refs):
        head = (at_ref[0] ^ x) * own + index
        source = lax.broadcasted_iota(jnp.int32, (count, dim), 0) - head * heads
        mine = (source >= 0) & (source < heads)
        stats = jnp.zeros((rows, dim), jnp.float32)
        for part, term in enumerate(logs):
            chosen = jnp.where(mine & (target == source + (2 * part + 1) * heads), 1.0, 0.0).astype(jnp.bfloat16)
            stats += jnp.dot(term.astype(jnp.bfloat16), chosen, preferred_element_type=jnp.float32)
        for h in range(heads):
            columns = pl.ds(pl.multiple_of((head * heads + h) * dim, dim), dim)
            gated = (gate_ref[head * heads + h] * grad_ref[:, columns].astype(jnp.float32)).astype(jnp.bfloat16)
            packed_ref[h * rows:(h + 1) * rows, :] = query_ref[:, columns]
            packed_ref[(heads + h) * rows:(heads + h + 1) * rows, :] = gated
            product = gated.astype(jnp.float32) * out_ref[:, columns].astype(jnp.float32)
            delta = jnp.sum(product, axis=1, keepdims=True)
            for part, term in enumerate(split_parts(delta)):
                stats = jnp.where(lane == 2 * part * heads + h, term, stats)
        packed_ref[2 * heads * rows:, :] = stats.astype(jnp.bfloat16)


def prepare(grad_out, queries, mem_out, row_total, gates, at, kv_heads, dim, scale, own, index):
    rows, width = grad_out.shape
    heads = width // dim // kv_heads
    group = kv_heads // own
    span = 2 * heads * rows + rows
    wide = pl.BlockSpec((rows, width), lambda i, *_: (0, 0))
    return pl.pallas_call(
        functools.partial(prepare_kernel, heads, dim, scale, own, index),
        out_shape=[jax.ShapeDtypeStruct((span, dim), jnp.bfloat16)] * group,
        grid_spec=pltpu.PrefetchScalarGridSpec(
            num_scalar_prefetch=2,
            grid=(1,),
            in_specs=[wide, wide, wide, pl.BlockSpec(row_total.shape, lambda i, *_: (0, 0))],
            out_specs=[pl.BlockSpec((span, dim), lambda i, *_: (0, 0))] * group,
        ),
        compiler_params=pltpu.CompilerParams(vmem_limit_bytes=VMEM_LIMIT),
        cost_estimate=pl.CostEstimate(flops=rows * width * 4, bytes_accessed=rows * width * 12 // own, transcendentals=0),
    )(gates, at[None], grad_out, queries, mem_out, row_total)


def attend_kernel(heads, dim, rows, scale, first, tiles, fresh, last, picks_ref, starts_ref, *refs):
    packed_refs, memory_ref = refs[:tiles], refs[tiles]
    acc_in = None if fresh else refs[tiles + 1]
    out_refs, (query_ref, log_ref, delta_ref, total) = refs[tiles + (1 if fresh else 2):-4], refs[-4:]
    step = pl.program_id(0)
    tile = first + step
    blocks = memory_ref.shape[1] // 2
    count = heads * rows

    if fresh:
        total[...] = jnp.zeros_like(total)
    else:
        total[...] = acc_in[0]

    for x, packed in enumerate(packed_refs):

        @pl.when(step == x)
        def _(packed=packed):
            query_ref[...] = packed[...]

    terms = query_ref[2 * count:, :].astype(jnp.float32)
    stats = terms
    for part in range(1, PARTS):
        stats = stats + pltpu.roll(terms, dim - 2 * part * heads, 1)
    for h in range(heads):
        for target, lane in ((delta_ref, h), (log_ref, heads + h)):
            target[h * rows:(h + 1) * rows, :] = jnp.broadcast_to(stats[:, lane:lane + 1], (rows, dim))

    low = starts_ref[tile, 0]
    high = starts_ref[tile, 1]
    exponent = scale * math.log2(math.e)

    def add(here, number, checked):
        sides = []
        for two in range(0, number, 2):
            keys, values = [], []
            for j in (two, two + 1):
                valid = here + j < high
                pick = picks_ref[tile, jnp.where(valid, here + j, here) if checked else here + j]
                holder = pick // MOST
                block = pick % MOST
                key = memory_ref[holder, block]
                keys.append(jnp.where(valid, key, jnp.zeros_like(key)) if checked and j else key)
                values.append(memory_ref[holder, blocks + block])
            sides.append((jnp.concatenate(keys, axis=0), jnp.concatenate(values, axis=0)))

        def products(side):
            keys, values = side
            scores = lax.dot_general(query_ref[:count, :], keys, NT, preferred_element_type=jnp.float32)
            grad_probs = lax.dot_general(query_ref[count:2 * count, :], values, NT, preferred_element_type=jnp.float32)
            return scores, grad_probs

        ahead = products(sides[0])
        gained = None
        for at, (keys, _) in enumerate(sides):
            scores, grad_probs = ahead
            if at + 1 < len(sides):
                ahead = products(sides[at + 1])
            log_wide = jnp.concatenate([log_ref[...]] * 2, axis=1)
            delta_wide = jnp.concatenate([delta_ref[...]] * 2, axis=1)
            probs = jnp.exp2(scores * exponent - log_wide)
            grad_scores = (probs * (grad_probs - delta_wide)).astype(jnp.bfloat16)
            part = jnp.dot(grad_scores, keys, preferred_element_type=jnp.float32)
            gained = part if gained is None else gained + part
        total[...] += gained

    for number in STEPS:
        full = (high - low) // number

        def many(turn, carry, low=low, number=number):
            add(low + number * turn, number, False)
            return carry

        lax.fori_loop(0, full, many, 0)
        low = low + number * full

    def few(turn, carry):
        add(low + 2 * turn, 2, True)
        return carry

    lax.fori_loop(0, (high - low + 1) // 2, few, 0)

    if not last:
        out_refs[0][0] = total[...]
        return
    for x, out_ref in enumerate(out_refs):

        @pl.when(step == x)
        def _(out_ref=out_ref):
            for h in range(heads):
                out_ref[:, h * dim:(h + 1) * dim] = total[h * rows:(h + 1) * rows, :].astype(jnp.bfloat16)


def attend(packed, memory, acc, picks, starts, heads, dim, scale, last, first=0):
    tiles = len(packed)
    span = packed[0].shape[0]
    rows = span // (2 * heads + 1)
    fresh = acc is None
    width = heads * rows
    holders = memory.shape[0]
    memory = memory.reshape(holders, -1, BLOCK, dim)
    acc_spec = pl.BlockSpec((1, width, dim), lambda t, *_: (first + t, 0, 0))
    if last:
        out_shape = [jax.ShapeDtypeStruct((rows, heads * dim), jnp.bfloat16)] * tiles
        out_spec = [pl.BlockSpec((rows, heads * dim), lambda t, *_: (0, 0))] * tiles
    else:
        out_shape = jax.ShapeDtypeStruct((tiles, width, dim), jnp.float32)
        out_spec = acc_spec
    flops = tiles * holders * memory.shape[1] * (BLOCK // 4) * width * dim * 6
    return pl.pallas_call(
        functools.partial(attend_kernel, heads, dim, rows, scale, first, tiles, fresh, last),
        out_shape=out_shape,
        grid_spec=pltpu.PrefetchScalarGridSpec(
            num_scalar_prefetch=2,
            grid=(tiles,),
            in_specs=[pl.BlockSpec((span, dim), lambda t, *_: (0, 0))] * tiles
            + [pl.BlockSpec(memory.shape, lambda t, *_: (0, 0, 0, 0))]
            + ([] if fresh else [acc_spec]),
            out_specs=out_spec,
            scratch_shapes=[pltpu.VMEM((span, dim), jnp.bfloat16)] + [pltpu.VMEM((width, dim), jnp.float32)] * 3,
        ),
        compiler_params=pltpu.CompilerParams(vmem_limit_bytes=VMEM_MOST),
        cost_estimate=pl.CostEstimate(flops=flops * 4, bytes_accessed=0, transcendentals=0),
    )(picks, starts, *packed, memory, *([] if fresh else [acc]))


def assemble_kernel(own, group, at_ref, *refs):
    pieces, out_ref = refs[:-1], refs[-1]
    span = pieces[0].shape[1]
    for index in range(own):
        for x in range(group):
            column = pl.multiple_of(((at_ref[0] ^ x) * own + index) * span, span)
            out_ref[:, pl.ds(column, span)] = pieces[index * group + x][...]


def assemble(pieces, at, own, group):
    rows, span = pieces[0].shape
    width = own * group * span
    part = rows // 4
    return pl.pallas_call(
        functools.partial(assemble_kernel, own, group),
        out_shape=jax.ShapeDtypeStruct((rows, width), pieces[0].dtype),
        grid_spec=pltpu.PrefetchScalarGridSpec(
            num_scalar_prefetch=1,
            grid=(rows // part,),
            in_specs=[pl.BlockSpec((part, span), lambda i, _: (i, 0))] * len(pieces),
            out_specs=pl.BlockSpec((part, width), lambda i, _: (i, 0)),
        ),
        compiler_params=pltpu.CompilerParams(vmem_limit_bytes=VMEM_MOST),
        cost_estimate=pl.CostEstimate(flops=0, bytes_accessed=4 * rows * width, transcendentals=0),
    )(at[None], *pieces)


def after(value, *others):
    anywhere = pl.BlockSpec(memory_space=pl.ANY)
    corners = [
        pl.BlockSpec((1,) * (other.ndim - 2) + (HINT, 128), lambda i, count=other.ndim: (0,) * count) for other in others
    ]
    return pl.pallas_call(
        lambda *refs: None,
        out_shape=jax.ShapeDtypeStruct(value.shape, value.dtype),
        grid=(1,),
        in_specs=[anywhere] + corners,
        out_specs=anywhere,
        input_output_aliases={0: 0},
        cost_estimate=pl.CostEstimate(flops=0, bytes_accessed=0, transcendentals=0),
    )(value, *others)


def shards(grad_out, queries, mem_out, row_total, gate_logit, mem_keys, mem_values, retrieved):
    seq = lax.axis_size("seq")
    sections = lax.axis_size("section")
    position = lax.axis_index("seq")
    rows, width = grad_out.shape[1:]
    head_count = gate_logit.shape[1]
    dim = width // head_count
    kv_heads = mem_keys.shape[2] // dim
    heads = head_count // kv_heads
    mem_dev = mem_keys.shape[1]
    blocks = mem_dev // BLOCK
    group = min(kv_heads, seq // 2)
    own = kv_heads // group
    at = position % group
    home = position // group
    scale = dim ** (-0.5)

    def swapped(value, step):
        return lax.ppermute(value, "seq", [(p, p ^ step) for p in range(seq)])

    def delivered(value, step):
        pairs = [(s * seq + p, ((s - 1) % sections) * seq + (p ^ step)) for s in range(sections) for p in range(seq)]
        return lax.ppermute(value, ("section", "seq"), pairs)

    cut = (5 * blocks + 7) // 8
    cuts = [[(0, blocks)]] * (own - 1) + [[(0, cut), (cut, blocks)]]

    moved = own > 1
    chosen = retrieved[0]
    if moved:
        of_all = lax.all_gather(chosen, "section")
        chosen = lax.dynamic_index_in_dim(of_all, (lax.axis_index("section") + 1) % sections, 0, keepdims=False)

    def listed(i):
        source = chosen if i == own - 1 else retrieved[0]
        mine = lax.dynamic_index_in_dim(source, at * own + i, 0, keepdims=False)
        mine = jnp.stack(
            [lax.dynamic_index_in_dim(mine, home * group + (at ^ x), 0, keepdims=False) for x in range(group)]
        )
        holder, block = mine // blocks, mine % blocks
        piece = sum((block >= low).astype(jnp.int32) for low, _ in cuts[i][1:]) if len(cuts[i]) > 1 else 0 * block
        key = piece * seq * blocks + mine
        rank = jnp.sum(key[:, None, :] < key[:, :, None], axis=-1)
        order = jnp.arange(mine.shape[-1])
        low = sum((piece == j) * cuts[i][j][0] for j in range(len(cuts[i])))
        value = holder * MOST + block - low
        picks = jnp.sum(jnp.where(rank[:, :, None] == order, value[:, :, None], 0), axis=1).astype(jnp.int32)
        bounds = [jnp.sum(piece < j, axis=-1) for j in range(len(cuts[i]) + 1)]
        return picks, [
            jnp.stack([bounds[j], bounds[j + 1]], axis=1).astype(jnp.int32) for j in range(len(cuts[i]))
        ]

    gates = jax.nn.sigmoid(gate_logit[0])
    gathered, worked, latest, held = [], [], None, []

    def memory_of(i, sources):
        return pack(sources, seq, own, group, dim, i, cuts[i])

    def queries_of(i):
        return prepare(grad_out[0], queries[0], mem_out[0], row_total[0], gates, at, kv_heads, dim, scale, own, i)

    def exchanged(packed):
        return [packed[0]] + [swapped(packed[x], x) for x in range(1, group)]

    memories = memory_of(0, [mem_keys[0], mem_values[0]])
    asked = [queries_of(i) for i in range(own)]
    for i in range(1, own):
        rows_of = narrow(mem_keys[0], mem_values[0], after(at[None], asked[i][0]), own, group, dim, i)
        memories += memory_of(i, [delivered(rows_of, 0) if i == own - 1 else rows_of])
    coming = exchanged(asked[0])
    for i in range(own):
        packed = coming
        pieces = []
        for _ in cuts[i]:
            piece = memories.pop(0)
            piece = piece if latest is None else after(piece, latest, *held)
            latest = lax.all_to_all(piece, "seq", split_axis=0, concat_axis=0, tiled=True)
            pieces.append(latest)
            held = packed
        picks, starts = listed(i)
        run = functools.partial(attend, picks=picks, heads=heads, dim=dim, scale=scale)
        acc = None
        for j in range(len(pieces) - 1):
            acc = run(packed, pieces[j], acc, starts=after(starts[j], *worked), last=False)
            worked = [acc]
        if i < own - 1:
            if i == own - 2:
                coming = [delivered(value, x) for x, value in enumerate(asked[i + 1])]
            else:
                coming = exchanged(asked[i + 1])
            done = run(packed, pieces[-1], acc, starts=after(starts[-1], *worked, memories[0]), last=True)
            worked = done[:1]
            gathered += [delivered(done[x], x) for x in range(group)]
            continue
        results, half = [None] * group, group // 2
        for low, high in ((half, group), (0, half)):
            bounds = after(starts[-1], *worked, *(gathered if low else []))
            done = run(packed[low:high], pieces[-1], acc, starts=bounds, last=True, first=low)
            worked = done[:1]
            for x in range(low, high):
                result = done[x - low]
                if not moved:
                    results[x] = delivered(result if low else after(result, results[x + half]), x)
                elif x:
                    results[x] = swapped(result if low else after(result, *results[half:]), x)
                else:
                    results[x] = result
    return assemble(gathered + results, at, own, group)[None]


def solution(mesh):
    return jax.shard_map(
        shards,
        mesh=mesh,
        in_specs=(
            P("section", "seq", None),
            P("section", "seq", None),
            P("section", "seq", None),
            P("section", "seq", None),
            P("section", None),
            P("section", "seq", None),
            P("section", "seq", None),
            P("section", None, None, None),
        ),
        out_specs=P("section", "seq", None),
        check_vma=False,
    )
```

```python
import functools
import math

import jax
import jax.numpy as jnp
from jax import lax
from jax.experimental import pallas as pl
from jax.experimental.pallas import tpu as pltpu
from jax.sharding import PartitionSpec as P

BLOCK = 128
PARTS = 3
STEPS = (8, 4)
MOST = 1 << 10
HINT = 16
VMEM_LIMIT = 48 * 1024 * 1024
VMEM_MOST = 60 * 1024 * 1024

NT = (((1,), (1,)), ((), ()))


def split_parts(value):
    terms = []
    for _ in range(PARTS):
        term = value.astype(jnp.bfloat16)
        terms.append(term.astype(jnp.float32))
        value = value - terms[-1]
    return terms


def narrow_kernel(own, index, at_ref, keys_ref, values_ref, out_ref):
    group, _, dim = out_ref.shape[1:]
    for device in range(group):
        head = device * own + index
        out_ref[0, device] = keys_ref[:, head * dim:(head + 1) * dim]
        out_ref[1, device] = values_ref[:, head * dim:(head + 1) * dim]


def narrow(mem_keys, mem_values, hint, own, group, dim, index):
    mem_dev, width = mem_keys.shape
    rows = pl.BlockSpec((BLOCK, width), lambda i, _: (i, 0))
    return pl.pallas_call(
        functools.partial(narrow_kernel, own, index),
        out_shape=jax.ShapeDtypeStruct((2, group, mem_dev, dim), mem_keys.dtype),
        grid_spec=pltpu.PrefetchScalarGridSpec(
            num_scalar_prefetch=1,
            grid=(mem_dev // BLOCK,),
            in_specs=[rows, rows],
            out_specs=pl.BlockSpec((2, group, BLOCK, dim), lambda i, _: (0, 0, i, 0)),
        ),
        compiler_params=pltpu.CompilerParams(vmem_limit_bytes=VMEM_MOST),
        cost_estimate=pl.CostEstimate(flops=0, bytes_accessed=6 * mem_dev * width // own, transcendentals=0),
    )(hint, mem_keys, mem_values)


def pack_kernel(own, group, index, spans, wide, *refs):
    sources, outs = refs[:2 if wide else 1], refs[2 if wide else 1:]
    dim = outs[0].shape[3]
    block = pl.program_id(0)
    for (low, high), out in zip(spans, outs):

        @pl.when((block >= low) & (block < high))
        def _(out=out):
            for device in range(out.shape[0]):
                head = device % group * own + index
                for half in range(2):
                    if wide:
                        out[device, half] = sources[half][:, head * dim:(head + 1) * dim]
                    else:
                        out[device, half] = sources[0][half, device % group]


def pack(sources, seq, own, group, dim, index, spans):
    wide = len(sources) == 2
    mem_dev = sources[0].shape[0 if wide else 2]
    if wide:
        specs = [pl.BlockSpec((BLOCK, source.shape[1]), lambda i: (i, 0)) for source in sources]
    else:
        specs = [pl.BlockSpec((2, group, BLOCK, dim), lambda i: (0, 0, i, 0))]

    def place(low, high):
        return pl.BlockSpec((seq, 2, BLOCK, dim), lambda i: (0, 0, jnp.clip(i - low, 0, high - low - 1), 0))

    outs = pl.pallas_call(
        functools.partial(pack_kernel, own, group, index, spans, wide),
        out_shape=[
            jax.ShapeDtypeStruct((seq, 2, (high - low) * BLOCK, dim), sources[0].dtype) for low, high in spans
        ],
        grid=(mem_dev // BLOCK,),
        in_specs=specs,
        out_specs=[place(low, high) for low, high in spans],
        compiler_params=pltpu.CompilerParams(vmem_limit_bytes=VMEM_MOST),
        cost_estimate=pl.CostEstimate(flops=0, bytes_accessed=8 * mem_dev * dim * group, transcendentals=0),
    )(*sources)
    return [out.reshape(seq, -1, dim) for out in outs]


def prepare_kernel(heads, dim, scale, own, index, gate_ref, at_ref, grad_ref, query_ref, out_ref, total_ref, *packed_refs):
    rows = grad_ref.shape[0]
    count = total_ref.shape[1]
    logs = split_parts(jnp.log2(total_ref[...].astype(jnp.float32)) - math.log2(scale))
    target = lax.broadcasted_iota(jnp.int32, (count, dim), 1)
    lane = lax.broadcasted_iota(jnp.int32, (rows, dim), 1)
    for x, packed_ref in enumerate(packed_refs):
        head = (at_ref[0] ^ x) * own + index
        source = lax.broadcasted_iota(jnp.int32, (count, dim), 0) - head * heads
        mine = (source >= 0) & (source < heads)
        stats = jnp.zeros((rows, dim), jnp.float32)
        for part, term in enumerate(logs):
            chosen = jnp.where(mine & (target == source + (2 * part + 1) * heads), 1.0, 0.0).astype(jnp.bfloat16)
            stats += jnp.dot(term.astype(jnp.bfloat16), chosen, preferred_element_type=jnp.float32)
        for h in range(heads):
            columns = pl.ds(pl.multiple_of((head * heads + h) * dim, dim), dim)
            gated = (gate_ref[head * heads + h] * grad_ref[:, columns].astype(jnp.float32)).astype(jnp.bfloat16)
            packed_ref[h * rows:(h + 1) * rows, :] = query_ref[:, columns]
            packed_ref[(heads + h) * rows:(heads + h + 1) * rows, :] = gated
            product = gated.astype(jnp.float32) * out_ref[:, columns].astype(jnp.float32)
            delta = jnp.sum(product, axis=1, keepdims=True)
            for part, term in enumerate(split_parts(delta)):
                stats = jnp.where(lane == 2 * part * heads + h, term, stats)
        packed_ref[2 * heads * rows:, :] = stats.astype(jnp.bfloat16)


def prepare(grad_out, queries, mem_out, row_total, gates, at, kv_heads, dim, scale, own, index):
    rows, width = grad_out.shape
    heads = width // dim // kv_heads
    group = kv_heads // own
    span = 2 * heads * rows + rows
    wide = pl.BlockSpec((rows, width), lambda i, *_: (0, 0))
    return pl.pallas_call(
        functools.partial(prepare_kernel, heads, dim, scale, own, index),
        out_shape=[jax.ShapeDtypeStruct((span, dim), jnp.bfloat16)] * group,
        grid_spec=pltpu.PrefetchScalarGridSpec(
            num_scalar_prefetch=2,
            grid=(1,),
            in_specs=[wide, wide, wide, pl.BlockSpec(row_total.shape, lambda i, *_: (0, 0))],
            out_specs=[pl.BlockSpec((span, dim), lambda i, *_: (0, 0))] * group,
        ),
        compiler_params=pltpu.CompilerParams(vmem_limit_bytes=VMEM_LIMIT),
        cost_estimate=pl.CostEstimate(flops=rows * width * 4, bytes_accessed=rows * width * 12 // own, transcendentals=0),
    )(gates, at[None], grad_out, queries, mem_out, row_total)


def attend_kernel(heads, dim, rows, scale, first, tiles, fresh, last, picks_ref, starts_ref, *refs):
    packed_refs, memory_ref = refs[:tiles], refs[tiles]
    acc_in = None if fresh else refs[tiles + 1]
    out_refs, (query_ref, log_ref, delta_ref, total) = refs[tiles + (1 if fresh else 2):-4], refs[-4:]
    step = pl.program_id(0)
    tile = first + step
    blocks = memory_ref.shape[1] // 2
    count = heads * rows

    if fresh:
        total[...] = jnp.zeros_like(total)
    else:
        total[...] = acc_in[0]

    for x, packed in enumerate(packed_refs):

        @pl.when(step == x)
        def _(packed=packed):
            query_ref[...] = packed[...]

    terms = query_ref[2 * count:, :].astype(jnp.float32)
    stats = terms
    for part in range(1, PARTS):
        stats = stats + pltpu.roll(terms, dim - 2 * part * heads, 1)
    for h in range(heads):
        for target, lane in ((delta_ref, h), (log_ref, heads + h)):
            target[h * rows:(h + 1) * rows, :] = jnp.broadcast_to(stats[:, lane:lane + 1], (rows, dim))

    low = starts_ref[tile, 0]
    high = starts_ref[tile, 1]
    exponent = scale * math.log2(math.e)

    def add(here, number, checked):
        sides = []
        for two in range(0, number, 2):
            keys, values = [], []
            for j in (two, two + 1):
                valid = here + j < high
                pick = picks_ref[tile, jnp.where(valid, here + j, here) if checked else here + j]
                holder = pick // MOST
                block = pick % MOST
                key = memory_ref[holder, block]
                keys.append(jnp.where(valid, key, jnp.zeros_like(key)) if checked and j else key)
                values.append(memory_ref[holder, blocks + block])
            sides.append((jnp.concatenate(keys, axis=0), jnp.concatenate(values, axis=0)))

        def products(side):
            keys, values = side
            scores = lax.dot_general(query_ref[:count, :], keys, NT, preferred_element_type=jnp.float32)
            grad_probs = lax.dot_general(query_ref[count:2 * count, :], values, NT, preferred_element_type=jnp.float32)
            return scores, grad_probs

        ahead = products(sides[0])
        gained = None
        for at, (keys, _) in enumerate(sides):
            scores, grad_probs = ahead
            if at + 1 < len(sides):
                ahead = products(sides[at + 1])
            log_wide = jnp.concatenate([log_ref[...]] * 2, axis=1)
            delta_wide = jnp.concatenate([delta_ref[...]] * 2, axis=1)
            probs = jnp.exp2(scores * exponent - log_wide)
            grad_scores = (probs * (grad_probs - delta_wide)).astype(jnp.bfloat16)
            part = jnp.dot(grad_scores, keys, preferred_element_type=jnp.float32)
            gained = part if gained is None else gained + part
        total[...] += gained

    for number in STEPS:
        full = (high - low) // number

        def many(turn, carry, low=low, number=number):
            add(low + number * turn, number, False)
            return carry

        lax.fori_loop(0, full, many, 0)
        low = low + number * full

    def few(turn, carry):
        add(low + 2 * turn, 2, True)
        return carry

    lax.fori_loop(0, (high - low + 1) // 2, few, 0)

    if not last:
        out_refs[0][0] = total[...]
        return
    for x, out_ref in enumerate(out_refs):

        @pl.when(step == x)
        def _(out_ref=out_ref):
            for h in range(heads):
                out_ref[:, h * dim:(h + 1) * dim] = total[h * rows:(h + 1) * rows, :].astype(jnp.bfloat16)


def attend(packed, memory, acc, picks, starts, heads, dim, scale, last, first=0):
    tiles = len(packed)
    span = packed[0].shape[0]
    rows = span // (2 * heads + 1)
    fresh = acc is None
    width = heads * rows
    holders = memory.shape[0]
    memory = memory.reshape(holders, -1, BLOCK, dim)
    acc_spec = pl.BlockSpec((1, width, dim), lambda t, *_: (first + t, 0, 0))
    if last:
        out_shape = [jax.ShapeDtypeStruct((rows, heads * dim), jnp.bfloat16)] * tiles
        out_spec = [pl.BlockSpec((rows, heads * dim), lambda t, *_: (0, 0))] * tiles
    else:
        out_shape = jax.ShapeDtypeStruct((tiles, width, dim), jnp.float32)
        out_spec = acc_spec
    flops = tiles * holders * memory.shape[1] * (BLOCK // 4) * width * dim * 6
    return pl.pallas_call(
        functools.partial(attend_kernel, heads, dim, rows, scale, first, tiles, fresh, last),
        out_shape=out_shape,
        grid_spec=pltpu.PrefetchScalarGridSpec(
            num_scalar_prefetch=2,
            grid=(tiles,),
            in_specs=[pl.BlockSpec((span, dim), lambda t, *_: (0, 0))] * tiles
            + [pl.BlockSpec(memory.shape, lambda t, *_: (0, 0, 0, 0))]
            + ([] if fresh else [acc_spec]),
            out_specs=out_spec,
            scratch_shapes=[pltpu.VMEM((span, dim), jnp.bfloat16)] + [pltpu.VMEM((width, dim), jnp.float32)] * 3,
        ),
        compiler_params=pltpu.CompilerParams(vmem_limit_bytes=VMEM_MOST),
        cost_estimate=pl.CostEstimate(flops=flops * 4, bytes_accessed=0, transcendentals=0),
    )(picks, starts, *packed, memory, *([] if fresh else [acc]))


def assemble_kernel(own, group, at_ref, *refs):
    pieces, out_ref = refs[:-1], refs[-1]
    span = pieces[0].shape[1]
    for index in range(own):
        for x in range(group):
            column = pl.multiple_of(((at_ref[0] ^ x) * own + index) * span, span)
            out_ref[:, pl.ds(column, span)] = pieces[index * group + x][...]


def assemble(pieces, at, own, group):
    rows, span = pieces[0].shape
    width = own * group * span
    part = rows // 4
    return pl.pallas_call(
        functools.partial(assemble_kernel, own, group),
        out_shape=jax.ShapeDtypeStruct((rows, width), pieces[0].dtype),
        grid_spec=pltpu.PrefetchScalarGridSpec(
            num_scalar_prefetch=1,
            grid=(rows // part,),
            in_specs=[pl.BlockSpec((part, span), lambda i, _: (i, 0))] * len(pieces),
            out_specs=pl.BlockSpec((part, width), lambda i, _: (i, 0)),
        ),
        compiler_params=pltpu.CompilerParams(vmem_limit_bytes=VMEM_MOST),
        cost_estimate=pl.CostEstimate(flops=0, bytes_accessed=4 * rows * width, transcendentals=0),
    )(at[None], *pieces)


def after(value, *others):
    anywhere = pl.BlockSpec(memory_space=pl.ANY)
    corners = [
        pl.BlockSpec((1,) * (other.ndim - 2) + (HINT, 128), lambda i, count=other.ndim: (0,) * count) for other in others
    ]
    return pl.pallas_call(
        lambda *refs: None,
        out_shape=jax.ShapeDtypeStruct(value.shape, value.dtype),
        grid=(1,),
        in_specs=[anywhere] + corners,
        out_specs=anywhere,
        input_output_aliases={0: 0},
        cost_estimate=pl.CostEstimate(flops=0, bytes_accessed=0, transcendentals=0),
    )(value, *others)


def shards(grad_out, queries, mem_out, row_total, gate_logit, mem_keys, mem_values, retrieved):
    seq = lax.axis_size("seq")
    sections = lax.axis_size("section")
    position = lax.axis_index("seq")
    rows, width = grad_out.shape[1:]
    head_count = gate_logit.shape[1]
    dim = width // head_count
    kv_heads = mem_keys.shape[2] // dim
    heads = head_count // kv_heads
    mem_dev = mem_keys.shape[1]
    blocks = mem_dev // BLOCK
    group = min(kv_heads, seq // 2)
    own = kv_heads // group
    at = position % group
    home = position // group
    scale = dim ** (-0.5)

    def swapped(value, step):
        return lax.ppermute(value, "seq", [(p, p ^ step) for p in range(seq)])

    def delivered(value, step):
        pairs = [(s * seq + p, ((s - 1) % sections) * seq + (p ^ step)) for s in range(sections) for p in range(seq)]
        return lax.ppermute(value, ("section", "seq"), pairs)

    cut = (3 * blocks + 3) // 4
    cuts = [[(0, blocks)]] * (own - 1) + [[(0, cut), (cut, blocks)]]

    moved = own > 1
    chosen = retrieved[0]
    if moved:
        of_all = lax.all_gather(chosen, "section")
        chosen = lax.dynamic_index_in_dim(of_all, (lax.axis_index("section") + 1) % sections, 0, keepdims=False)

    def listed(i):
        source = chosen if i == own - 1 else retrieved[0]
        mine = lax.dynamic_index_in_dim(source, at * own + i, 0, keepdims=False)
        mine = jnp.stack(
            [lax.dynamic_index_in_dim(mine, home * group + (at ^ x), 0, keepdims=False) for x in range(group)]
        )
        holder, block = mine // blocks, mine % blocks
        piece = sum((block >= low).astype(jnp.int32) for low, _ in cuts[i][1:]) if len(cuts[i]) > 1 else 0 * block
        key = piece * seq * blocks + mine
        rank = jnp.sum(key[:, None, :] < key[:, :, None], axis=-1)
        order = jnp.arange(mine.shape[-1])
        low = sum((piece == j) * cuts[i][j][0] for j in range(len(cuts[i])))
        value = holder * MOST + block - low
        picks = jnp.sum(jnp.where(rank[:, :, None] == order, value[:, :, None], 0), axis=1).astype(jnp.int32)
        bounds = [jnp.sum(piece < j, axis=-1) for j in range(len(cuts[i]) + 1)]
        return picks, [
            jnp.stack([bounds[j], bounds[j + 1]], axis=1).astype(jnp.int32) for j in range(len(cuts[i]))
        ]

    gates = jax.nn.sigmoid(gate_logit[0])
    gathered, worked, latest, held = [], [], None, []

    def memory_of(i, sources):
        return pack(sources, seq, own, group, dim, i, cuts[i])

    def queries_of(i):
        return prepare(grad_out[0], queries[0], mem_out[0], row_total[0], gates, at, kv_heads, dim, scale, own, i)

    def exchanged(packed):
        return [packed[0]] + [swapped(packed[x], x) for x in range(1, group)]

    memories = memory_of(0, [mem_keys[0], mem_values[0]])
    asked = [queries_of(i) for i in range(own)]
    for i in range(1, own):
        rows_of = narrow(mem_keys[0], mem_values[0], after(at[None], asked[i][0]), own, group, dim, i)
        memories += memory_of(i, [delivered(rows_of, 0) if i == own - 1 else rows_of])
    coming = exchanged(asked[0])
    for i in range(own):
        packed = coming
        pieces = []
        for _ in cuts[i]:
            piece = memories.pop(0)
            piece = piece if latest is None else after(piece, latest, *held)
            latest = lax.all_to_all(piece, "seq", split_axis=0, concat_axis=0, tiled=True)
            pieces.append(latest)
            held = packed
        picks, starts = listed(i)
        run = functools.partial(attend, picks=picks, heads=heads, dim=dim, scale=scale)
        acc = None
        for j in range(len(pieces) - 1):
            acc = run(packed, pieces[j], acc, starts=after(starts[j], *worked), last=False)
            worked = [acc]
        if i < own - 1:
            if i == own - 2:
                coming = [delivered(value, x) for x, value in enumerate(asked[i + 1])]
            else:
                coming = exchanged(asked[i + 1])
            done = run(packed, pieces[-1], acc, starts=after(starts[-1], *worked, memories[0]), last=True)
            worked = done[:1]
            gathered += [delivered(done[x], x) for x in range(group)]
            continue
        results, half = [None] * group, group // 2
        for low, high in ((half, group), (0, half)):
            bounds = after(starts[-1], *worked, *(gathered if low else []))
            done = run(packed[low:high], pieces[-1], acc, starts=bounds, last=True, first=low)
            worked = done[:1]
            for x in range(low, high):
                result = done[x - low]
                if not moved:
                    results[x] = delivered(result if low else after(result, results[x + half]), x)
                elif x:
                    results[x] = swapped(result if low else after(result, *results[half:]), x)
                else:
                    results[x] = result
    return assemble(gathered + results, at, own, group)[None]


def solution(mesh):
    return jax.shard_map(
        shards,
        mesh=mesh,
        in_specs=(
            P("section", "seq", None),
            P("section", "seq", None),
            P("section", "seq", None),
            P("section", "seq", None),
            P("section", None),
            P("section", "seq", None),
            P("section", "seq", None),
            P("section", None, None, None),
        ),
        out_specs=P("section", "seq", None),
        check_vma=False,
    )
```

```python
import functools
import math

import jax
import jax.numpy as jnp
from jax import lax
from jax.experimental import pallas as pl
from jax.experimental.pallas import tpu as pltpu
from jax.sharding import PartitionSpec as P

BLOCK = 128
PARTS = 3
STEPS = (8, 4)
MOST = 1 << 10
HINT = 16
VMEM_LIMIT = 48 * 1024 * 1024
VMEM_MOST = 60 * 1024 * 1024

NT = (((1,), (1,)), ((), ()))


def split_parts(value):
    terms = []
    for _ in range(PARTS):
        term = value.astype(jnp.bfloat16)
        terms.append(term.astype(jnp.float32))
        value = value - terms[-1]
    return terms


def narrow_kernel(own, index, at_ref, keys_ref, values_ref, out_ref):
    group, _, dim = out_ref.shape[1:]
    for device in range(group):
        head = device * own + index
        out_ref[0, device] = keys_ref[:, head * dim:(head + 1) * dim]
        out_ref[1, device] = values_ref[:, head * dim:(head + 1) * dim]


def narrow(mem_keys, mem_values, hint, own, group, dim, index):
    mem_dev, width = mem_keys.shape
    rows = pl.BlockSpec((BLOCK, width), lambda i, _: (i, 0))
    return pl.pallas_call(
        functools.partial(narrow_kernel, own, index),
        out_shape=jax.ShapeDtypeStruct((2, group, mem_dev, dim), mem_keys.dtype),
        grid_spec=pltpu.PrefetchScalarGridSpec(
            num_scalar_prefetch=1,
            grid=(mem_dev // BLOCK,),
            in_specs=[rows, rows],
            out_specs=pl.BlockSpec((2, group, BLOCK, dim), lambda i, _: (0, 0, i, 0)),
        ),
        compiler_params=pltpu.CompilerParams(vmem_limit_bytes=VMEM_MOST),
        cost_estimate=pl.CostEstimate(flops=0, bytes_accessed=6 * mem_dev * width // own, transcendentals=0),
    )(hint, mem_keys, mem_values)


def pack_kernel(own, group, index, spans, wide, *refs):
    sources, outs = refs[:2 if wide else 1], refs[2 if wide else 1:]
    dim = outs[0].shape[3]
    block = pl.program_id(0)
    for (low, high), out in zip(spans, outs):

        @pl.when((block >= low) & (block < high))
        def _(out=out):
            for device in range(out.shape[0]):
                head = device % group * own + index
                for half in range(2):
                    if wide:
                        out[device, half] = sources[half][:, head * dim:(head + 1) * dim]
                    else:
                        out[device, half] = sources[0][half, device % group]


def pack(sources, seq, own, group, dim, index, spans):
    wide = len(sources) == 2
    mem_dev = sources[0].shape[0 if wide else 2]
    if wide:
        specs = [pl.BlockSpec((BLOCK, source.shape[1]), lambda i: (i, 0)) for source in sources]
    else:
        specs = [pl.BlockSpec((2, group, BLOCK, dim), lambda i: (0, 0, i, 0))]

    def place(low, high):
        return pl.BlockSpec((seq, 2, BLOCK, dim), lambda i: (0, 0, jnp.clip(i - low, 0, high - low - 1), 0))

    outs = pl.pallas_call(
        functools.partial(pack_kernel, own, group, index, spans, wide),
        out_shape=[
            jax.ShapeDtypeStruct((seq, 2, (high - low) * BLOCK, dim), sources[0].dtype) for low, high in spans
        ],
        grid=(mem_dev // BLOCK,),
        in_specs=specs,
        out_specs=[place(low, high) for low, high in spans],
        compiler_params=pltpu.CompilerParams(vmem_limit_bytes=VMEM_MOST),
        cost_estimate=pl.CostEstimate(flops=0, bytes_accessed=8 * mem_dev * dim * group, transcendentals=0),
    )(*sources)
    return [out.reshape(seq, -1, dim) for out in outs]


def prepare_kernel(heads, dim, scale, own, index, gate_ref, at_ref, grad_ref, query_ref, out_ref, total_ref, *packed_refs):
    rows = grad_ref.shape[0]
    count = total_ref.shape[1]
    logs = split_parts(jnp.log2(total_ref[...].astype(jnp.float32)) - math.log2(scale))
    target = lax.broadcasted_iota(jnp.int32, (count, dim), 1)
    lane = lax.broadcasted_iota(jnp.int32, (rows, dim), 1)
    for x, packed_ref in enumerate(packed_refs):
        head = (at_ref[0] ^ x) * own + index
        source = lax.broadcasted_iota(jnp.int32, (count, dim), 0) - head * heads
        mine = (source >= 0) & (source < heads)
        stats = jnp.zeros((rows, dim), jnp.float32)
        for part, term in enumerate(logs):
            chosen = jnp.where(mine & (target == source + (2 * part + 1) * heads), 1.0, 0.0).astype(jnp.bfloat16)
            stats += jnp.dot(term.astype(jnp.bfloat16), chosen, preferred_element_type=jnp.float32)
        for h in range(heads):
            columns = pl.ds(pl.multiple_of((head * heads + h) * dim, dim), dim)
            gated = (gate_ref[head * heads + h] * grad_ref[:, columns].astype(jnp.float32)).astype(jnp.bfloat16)
            packed_ref[h * rows:(h + 1) * rows, :] = query_ref[:, columns]
            packed_ref[(heads + h) * rows:(heads + h + 1) * rows, :] = gated
            product = gated.astype(jnp.float32) * out_ref[:, columns].astype(jnp.float32)
            delta = jnp.sum(product, axis=1, keepdims=True)
            for part, term in enumerate(split_parts(delta)):
                stats = jnp.where(lane == 2 * part * heads + h, term, stats)
        packed_ref[2 * heads * rows:, :] = stats.astype(jnp.bfloat16)


def prepare(grad_out, queries, mem_out, row_total, gates, at, kv_heads, dim, scale, own, index):
    rows, width = grad_out.shape
    heads = width // dim // kv_heads
    group = kv_heads // own
    span = 2 * heads * rows + rows
    wide = pl.BlockSpec((rows, width), lambda i, *_: (0, 0))
    return pl.pallas_call(
        functools.partial(prepare_kernel, heads, dim, scale, own, index),
        out_shape=[jax.ShapeDtypeStruct((span, dim), jnp.bfloat16)] * group,
        grid_spec=pltpu.PrefetchScalarGridSpec(
            num_scalar_prefetch=2,
            grid=(1,),
            in_specs=[wide, wide, wide, pl.BlockSpec(row_total.shape, lambda i, *_: (0, 0))],
            out_specs=[pl.BlockSpec((span, dim), lambda i, *_: (0, 0))] * group,
        ),
        compiler_params=pltpu.CompilerParams(vmem_limit_bytes=VMEM_LIMIT),
        cost_estimate=pl.CostEstimate(flops=rows * width * 4, bytes_accessed=rows * width * 12 // own, transcendentals=0),
    )(gates, at[None], grad_out, queries, mem_out, row_total)


def attend_kernel(heads, dim, rows, scale, first, tiles, fresh, last, picks_ref, starts_ref, *refs):
    packed_refs, memory_ref = refs[:tiles], refs[tiles]
    acc_in = None if fresh else refs[tiles + 1]
    out_refs, (query_ref, log_ref, delta_ref, total) = refs[tiles + (1 if fresh else 2):-4], refs[-4:]
    step = pl.program_id(0)
    tile = first + step
    blocks = memory_ref.shape[1] // 2
    count = heads * rows

    if fresh:
        total[...] = jnp.zeros_like(total)
    else:
        total[...] = acc_in[0]

    for x, packed in enumerate(packed_refs):

        @pl.when(step == x)
        def _(packed=packed):
            query_ref[...] = packed[...]

    terms = query_ref[2 * count:, :].astype(jnp.float32)
    stats = terms
    for part in range(1, PARTS):
        stats = stats + pltpu.roll(terms, dim - 2 * part * heads, 1)
    for h in range(heads):
        for target, lane in ((delta_ref, h), (log_ref, heads + h)):
            target[h * rows:(h + 1) * rows, :] = jnp.broadcast_to(stats[:, lane:lane + 1], (rows, dim))

    low = starts_ref[tile, 0]
    high = starts_ref[tile, 1]
    exponent = scale * math.log2(math.e)

    def add(here, number, checked):
        sides = []
        for two in range(0, number, 2):
            keys, values = [], []
            for j in (two, two + 1):
                valid = here + j < high
                pick = picks_ref[tile, jnp.where(valid, here + j, here) if checked else here + j]
                holder = pick // MOST
                block = pick % MOST
                key = memory_ref[holder, block]
                keys.append(jnp.where(valid, key, jnp.zeros_like(key)) if checked and j else key)
                values.append(memory_ref[holder, blocks + block])
            sides.append((jnp.concatenate(keys, axis=0), jnp.concatenate(values, axis=0)))

        def products(side):
            keys, values = side
            scores = lax.dot_general(query_ref[:count, :], keys, NT, preferred_element_type=jnp.float32)
            grad_probs = lax.dot_general(query_ref[count:2 * count, :], values, NT, preferred_element_type=jnp.float32)
            return scores, grad_probs

        ahead = products(sides[0])
        gained = None
        for at, (keys, _) in enumerate(sides):
            scores, grad_probs = ahead
            if at + 1 < len(sides):
                ahead = products(sides[at + 1])
            log_wide = jnp.concatenate([log_ref[...]] * 2, axis=1)
            delta_wide = jnp.concatenate([delta_ref[...]] * 2, axis=1)
            probs = jnp.exp2(scores * exponent - log_wide)
            grad_scores = (probs * (grad_probs - delta_wide)).astype(jnp.bfloat16)
            part = jnp.dot(grad_scores, keys, preferred_element_type=jnp.float32)
            gained = part if gained is None else gained + part
        total[...] += gained

    for number in STEPS:
        full = (high - low) // number

        def many(turn, carry, low=low, number=number):
            add(low + number * turn, number, False)
            return carry

        lax.fori_loop(0, full, many, 0)
        low = low + number * full

    def few(turn, carry):
        add(low + 2 * turn, 2, True)
        return carry

    lax.fori_loop(0, (high - low + 1) // 2, few, 0)

    if not last:
        out_refs[0][0] = total[...]
        return
    for x, out_ref in enumerate(out_refs):

        @pl.when(step == x)
        def _(out_ref=out_ref):
            for h in range(heads):
                out_ref[:, h * dim:(h + 1) * dim] = total[h * rows:(h + 1) * rows, :].astype(jnp.bfloat16)


def attend(packed, memory, acc, picks, starts, heads, dim, scale, last, first=0):
    tiles = len(packed)
    span = packed[0].shape[0]
    rows = span // (2 * heads + 1)
    fresh = acc is None
    width = heads * rows
    holders = memory.shape[0]
    memory = memory.reshape(holders, -1, BLOCK, dim)
    acc_spec = pl.BlockSpec((1, width, dim), lambda t, *_: (first + t, 0, 0))
    if last:
        out_shape = [jax.ShapeDtypeStruct((rows, heads * dim), jnp.bfloat16)] * tiles
        out_spec = [pl.BlockSpec((rows, heads * dim), lambda t, *_: (0, 0))] * tiles
    else:
        out_shape = jax.ShapeDtypeStruct((tiles, width, dim), jnp.float32)
        out_spec = acc_spec
    flops = tiles * holders * memory.shape[1] * (BLOCK // 4) * width * dim * 6
    return pl.pallas_call(
        functools.partial(attend_kernel, heads, dim, rows, scale, first, tiles, fresh, last),
        out_shape=out_shape,
        grid_spec=pltpu.PrefetchScalarGridSpec(
            num_scalar_prefetch=2,
            grid=(tiles,),
            in_specs=[pl.BlockSpec((span, dim), lambda t, *_: (0, 0))] * tiles
            + [pl.BlockSpec(memory.shape, lambda t, *_: (0, 0, 0, 0))]
            + ([] if fresh else [acc_spec]),
            out_specs=out_spec,
            scratch_shapes=[pltpu.VMEM((span, dim), jnp.bfloat16)] + [pltpu.VMEM((width, dim), jnp.float32)] * 3,
        ),
        compiler_params=pltpu.CompilerParams(vmem_limit_bytes=VMEM_MOST),
        cost_estimate=pl.CostEstimate(flops=flops * 4, bytes_accessed=0, transcendentals=0),
    )(picks, starts, *packed, memory, *([] if fresh else [acc]))


def assemble_kernel(own, group, at_ref, *refs):
    pieces, out_ref = refs[:-1], refs[-1]
    span = pieces[0].shape[1]
    for index in range(own):
        for x in range(group):
            column = pl.multiple_of(((at_ref[0] ^ x) * own + index) * span, span)
            out_ref[:, pl.ds(column, span)] = pieces[index * group + x][...]


def assemble(pieces, at, own, group):
    rows, span = pieces[0].shape
    width = own * group * span
    part = rows // 4
    return pl.pallas_call(
        functools.partial(assemble_kernel, own, group),
        out_shape=jax.ShapeDtypeStruct((rows, width), pieces[0].dtype),
        grid_spec=pltpu.PrefetchScalarGridSpec(
            num_scalar_prefetch=1,
            grid=(rows // part,),
            in_specs=[pl.BlockSpec((part, span), lambda i, _: (i, 0))] * len(pieces),
            out_specs=pl.BlockSpec((part, width), lambda i, _: (i, 0)),
        ),
        compiler_params=pltpu.CompilerParams(vmem_limit_bytes=VMEM_MOST),
        cost_estimate=pl.CostEstimate(flops=0, bytes_accessed=4 * rows * width, transcendentals=0),
    )(at[None], *pieces)


def after(value, *others):
    anywhere = pl.BlockSpec(memory_space=pl.ANY)
    corners = [
        pl.BlockSpec((1,) * (other.ndim - 2) + (HINT, 128), lambda i, count=other.ndim: (0,) * count) for other in others
    ]
    return pl.pallas_call(
        lambda *refs: None,
        out_shape=jax.ShapeDtypeStruct(value.shape, value.dtype),
        grid=(1,),
        in_specs=[anywhere] + corners,
        out_specs=anywhere,
        input_output_aliases={0: 0},
        cost_estimate=pl.CostEstimate(flops=0, bytes_accessed=0, transcendentals=0),
    )(value, *others)


def shards(grad_out, queries, mem_out, row_total, gate_logit, mem_keys, mem_values, retrieved):
    seq = lax.axis_size("seq")
    sections = lax.axis_size("section")
    position = lax.axis_index("seq")
    rows, width = grad_out.shape[1:]
    head_count = gate_logit.shape[1]
    dim = width // head_count
    kv_heads = mem_keys.shape[2] // dim
    heads = head_count // kv_heads
    mem_dev = mem_keys.shape[1]
    blocks = mem_dev // BLOCK
    group = min(kv_heads, seq // 2)
    own = kv_heads // group
    at = position % group
    home = position // group
    scale = dim ** (-0.5)

    def swapped(value, step):
        return lax.ppermute(value, "seq", [(p, p ^ step) for p in range(seq)])

    def delivered(value, step):
        pairs = [(s * seq + p, ((s - 1) % sections) * seq + (p ^ step)) for s in range(sections) for p in range(seq)]
        return lax.ppermute(value, ("section", "seq"), pairs)

    cut = (5 * blocks + 7) // 8
    cuts = [[(0, blocks)]] * (own - 1) + [[(0, cut), (cut, blocks)]]

    moved = own > 1
    def listed(i, source):
        mine = lax.dynamic_index_in_dim(source, at * own + i, 0, keepdims=False)
        mine = jnp.stack(
            [lax.dynamic_index_in_dim(mine, home * group + (at ^ x), 0, keepdims=False) for x in range(group)]
        )
        holder, block = mine // blocks, mine % blocks
        piece = sum((block >= low).astype(jnp.int32) for low, _ in cuts[i][1:]) if len(cuts[i]) > 1 else 0 * block
        key = piece * seq * blocks + mine
        rank = jnp.sum(key[:, None, :] < key[:, :, None], axis=-1)
        order = jnp.arange(mine.shape[-1])
        low = sum((piece == j) * cuts[i][j][0] for j in range(len(cuts[i])))
        value = holder * MOST + block - low
        picks = jnp.sum(jnp.where(rank[:, :, None] == order, value[:, :, None], 0), axis=1).astype(jnp.int32)
        bounds = [jnp.sum(piece < j, axis=-1) for j in range(len(cuts[i]) + 1)]
        return picks, [
            jnp.stack([bounds[j], bounds[j + 1]], axis=1).astype(jnp.int32) for j in range(len(cuts[i]))
        ]

    gates = jax.nn.sigmoid(gate_logit[0])
    gathered, worked, latest, held = [], [], None, []

    def memory_of(i, sources):
        return pack(sources, seq, own, group, dim, i, cuts[i])

    def queries_of(i):
        return prepare(grad_out[0], queries[0], mem_out[0], row_total[0], gates, at, kv_heads, dim, scale, own, i)

    def exchanged(packed):
        return [packed[0]] + [swapped(packed[x], x) for x in range(1, group)]

    memories = memory_of(0, [mem_keys[0], mem_values[0]])
    asked = [queries_of(i) for i in range(own)]
    for i in range(1, own):
        rows_of = narrow(mem_keys[0], mem_values[0], after(at[None], asked[i][0]), own, group, dim, i)
        memories += memory_of(i, [delivered(rows_of, 0) if i == own - 1 else rows_of])
    coming = exchanged(asked[0])
    for i in range(own):
        packed = coming
        pieces = []
        for _ in cuts[i]:
            piece = memories.pop(0)
            piece = piece if latest is None else after(piece, latest, *held)
            latest = lax.all_to_all(piece, "seq", split_axis=0, concat_axis=0, tiled=True)
            pieces.append(latest)
            held = packed
        if i == own - 1 and moved:
            chosen = delivered(after(retrieved[0], *opened), 0)
        else:
            chosen, opened = retrieved[0], [latest, *packed[1:]]
        picks, starts = listed(i, chosen)
        run = functools.partial(attend, picks=picks, heads=heads, dim=dim, scale=scale)
        acc = None
        for j in range(len(pieces) - 1):
            acc = run(packed, pieces[j], acc, starts=after(starts[j], *worked), last=False)
            worked = [acc]
        if i < own - 1:
            if i == own - 2:
                coming = [delivered(value, x) for x, value in enumerate(asked[i + 1])]
            else:
                coming = exchanged(asked[i + 1])
            done = run(packed, pieces[-1], acc, starts=after(starts[-1], *worked, memories[0]), last=True)
            worked = done[:1]
            gathered += [delivered(done[x], x) for x in range(group)]
            continue
        results, half = [None] * group, group // 2
        for low, high in ((half, group), (0, half)):
            bounds = after(starts[-1], *worked, *(gathered if low else []))
            done = run(packed[low:high], pieces[-1], acc, starts=bounds, last=True, first=low)
            worked = done[:1]
            for x in range(low, high):
                result = done[x - low]
                if not moved:
                    results[x] = delivered(result if low else after(result, results[x + half]), x)
                elif x:
                    results[x] = swapped(result if low else after(result, *results[half:]), x)
                else:
                    results[x] = result
    return assemble(gathered + results, at, own, group)[None]


def solution(mesh):
    return jax.shard_map(
        shards,
        mesh=mesh,
        in_specs=(
            P("section", "seq", None),
            P("section", "seq", None),
            P("section", "seq", None),
            P("section", "seq", None),
            P("section", None),
            P("section", "seq", None),
            P("section", "seq", None),
            P("section", None, None, None),
        ),
        out_specs=P("section", "seq", None),
        check_vma=False,
    )
```

```python
import functools
import math

import jax
import jax.numpy as jnp
from jax import lax
from jax.experimental import pallas as pl
from jax.experimental.pallas import tpu as pltpu
from jax.sharding import PartitionSpec as P

BLOCK = 128
PARTS = 3
STEPS = (8, 4)
MOST = 1 << 10
HINT = 16
VMEM_LIMIT = 48 * 1024 * 1024
VMEM_MOST = 60 * 1024 * 1024

NT = (((1,), (1,)), ((), ()))


def split_parts(value):
    terms = []
    for _ in range(PARTS):
        term = value.astype(jnp.bfloat16)
        terms.append(term.astype(jnp.float32))
        value = value - terms[-1]
    return terms


def narrow_kernel(own, index, at_ref, keys_ref, values_ref, out_ref):
    group, _, dim = out_ref.shape[1:]
    for device in range(group):
        head = device * own + index
        out_ref[0, device] = keys_ref[:, head * dim:(head + 1) * dim]
        out_ref[1, device] = values_ref[:, head * dim:(head + 1) * dim]


def narrow(mem_keys, mem_values, hint, own, group, dim, index):
    mem_dev, width = mem_keys.shape
    rows = pl.BlockSpec((BLOCK, width), lambda i, _: (i, 0))
    return pl.pallas_call(
        functools.partial(narrow_kernel, own, index),
        out_shape=jax.ShapeDtypeStruct((2, group, mem_dev, dim), mem_keys.dtype),
        grid_spec=pltpu.PrefetchScalarGridSpec(
            num_scalar_prefetch=1,
            grid=(mem_dev // BLOCK,),
            in_specs=[rows, rows],
            out_specs=pl.BlockSpec((2, group, BLOCK, dim), lambda i, _: (0, 0, i, 0)),
        ),
        compiler_params=pltpu.CompilerParams(vmem_limit_bytes=VMEM_MOST),
        cost_estimate=pl.CostEstimate(flops=0, bytes_accessed=6 * mem_dev * width // own, transcendentals=0),
    )(hint, mem_keys, mem_values)


def pack_kernel(own, group, index, spans, wide, *refs):
    sources, outs = refs[:2 if wide else 1], refs[2 if wide else 1:]
    dim = outs[0].shape[3]
    block = pl.program_id(0)
    for (low, high), out in zip(spans, outs):

        @pl.when((block >= low) & (block < high))
        def _(out=out):
            for device in range(out.shape[0]):
                head = device % group * own + index
                for half in range(2):
                    if wide:
                        out[device, half] = sources[half][:, head * dim:(head + 1) * dim]
                    else:
                        out[device, half] = sources[0][half, device % group]


def pack(sources, seq, own, group, dim, index, spans):
    wide = len(sources) == 2
    mem_dev = sources[0].shape[0 if wide else 2]
    if wide:
        specs = [pl.BlockSpec((BLOCK, source.shape[1]), lambda i: (i, 0)) for source in sources]
    else:
        specs = [pl.BlockSpec((2, group, BLOCK, dim), lambda i: (0, 0, i, 0))]

    def place(low, high):
        return pl.BlockSpec((seq, 2, BLOCK, dim), lambda i: (0, 0, jnp.clip(i - low, 0, high - low - 1), 0))

    outs = pl.pallas_call(
        functools.partial(pack_kernel, own, group, index, spans, wide),
        out_shape=[
            jax.ShapeDtypeStruct((seq, 2, (high - low) * BLOCK, dim), sources[0].dtype) for low, high in spans
        ],
        grid=(mem_dev // BLOCK,),
        in_specs=specs,
        out_specs=[place(low, high) for low, high in spans],
        compiler_params=pltpu.CompilerParams(vmem_limit_bytes=VMEM_MOST),
        cost_estimate=pl.CostEstimate(flops=0, bytes_accessed=8 * mem_dev * dim * group, transcendentals=0),
    )(*sources)
    return [out.reshape(seq, -1, dim) for out in outs]


def prepare_kernel(heads, dim, scale, own, index, gate_ref, at_ref, grad_ref, query_ref, out_ref, total_ref, *packed_refs):
    rows = grad_ref.shape[0]
    count = total_ref.shape[1]
    logs = split_parts(jnp.log2(total_ref[...].astype(jnp.float32)) - math.log2(scale))
    target = lax.broadcasted_iota(jnp.int32, (count, dim), 1)
    lane = lax.broadcasted_iota(jnp.int32, (rows, dim), 1)
    for x, packed_ref in enumerate(packed_refs):
        head = (at_ref[0] ^ x) * own + index
        source = lax.broadcasted_iota(jnp.int32, (count, dim), 0) - head * heads
        mine = (source >= 0) & (source < heads)
        stats = jnp.zeros((rows, dim), jnp.float32)
        for part, term in enumerate(logs):
            chosen = jnp.where(mine & (target == source + (2 * part + 1) * heads), 1.0, 0.0).astype(jnp.bfloat16)
            stats += jnp.dot(term.astype(jnp.bfloat16), chosen, preferred_element_type=jnp.float32)
        for h in range(heads):
            columns = pl.ds(pl.multiple_of((head * heads + h) * dim, dim), dim)
            gated = (gate_ref[head * heads + h] * grad_ref[:, columns].astype(jnp.float32)).astype(jnp.bfloat16)
            packed_ref[h * rows:(h + 1) * rows, :] = query_ref[:, columns]
            packed_ref[(heads + h) * rows:(heads + h + 1) * rows, :] = gated
            product = gated.astype(jnp.float32) * out_ref[:, columns].astype(jnp.float32)
            delta = jnp.sum(product, axis=1, keepdims=True)
            for part, term in enumerate(split_parts(delta)):
                stats = jnp.where(lane == 2 * part * heads + h, term, stats)
        packed_ref[2 * heads * rows:, :] = stats.T[:2 * PARTS * heads].astype(jnp.bfloat16)


def prepare(grad_out, queries, mem_out, row_total, gates, at, kv_heads, dim, scale, own, index):
    rows, width = grad_out.shape
    heads = width // dim // kv_heads
    group = kv_heads // own
    span = 2 * heads * (rows + PARTS)
    wide = pl.BlockSpec((rows, width), lambda i, *_: (0, 0))
    return pl.pallas_call(
        functools.partial(prepare_kernel, heads, dim, scale, own, index),
        out_shape=[jax.ShapeDtypeStruct((span, dim), jnp.bfloat16)] * group,
        grid_spec=pltpu.PrefetchScalarGridSpec(
            num_scalar_prefetch=2,
            grid=(1,),
            in_specs=[wide, wide, wide, pl.BlockSpec(row_total.shape, lambda i, *_: (0, 0))],
            out_specs=[pl.BlockSpec((span, dim), lambda i, *_: (0, 0))] * group,
        ),
        compiler_params=pltpu.CompilerParams(vmem_limit_bytes=VMEM_LIMIT),
        cost_estimate=pl.CostEstimate(flops=rows * width * 4, bytes_accessed=rows * width * 12 // own, transcendentals=0),
    )(gates, at[None], grad_out, queries, mem_out, row_total)


def attend_kernel(heads, dim, rows, scale, first, tiles, fresh, last, picks_ref, starts_ref, *refs):
    packed_refs, memory_ref = refs[:tiles], refs[tiles]
    acc_in = None if fresh else refs[tiles + 1]
    out_refs, (query_ref, log_ref, delta_ref, total) = refs[tiles + (1 if fresh else 2):-4], refs[-4:]
    step = pl.program_id(0)
    tile = first + step
    blocks = memory_ref.shape[1] // 2
    count = heads * rows

    if fresh:
        total[...] = jnp.zeros_like(total)
    else:
        total[...] = acc_in[0]

    for x, packed in enumerate(packed_refs):

        @pl.when(step == x)
        def _(packed=packed):
            query_ref[...] = packed[...]

    terms = query_ref[2 * count:, :].astype(jnp.float32)
    terms = jnp.concatenate([terms, jnp.zeros((dim - terms.shape[0], rows), jnp.float32)], axis=0).T
    stats = terms
    for part in range(1, PARTS):
        stats = stats + pltpu.roll(terms, dim - 2 * part * heads, 1)
    for h in range(heads):
        for target, lane in ((delta_ref, h), (log_ref, heads + h)):
            target[h * rows:(h + 1) * rows, :] = jnp.broadcast_to(stats[:, lane:lane + 1], (rows, dim))

    low = starts_ref[tile, 0]
    high = starts_ref[tile, 1]
    exponent = scale * math.log2(math.e)

    def add(here, number, checked):
        sides = []
        for two in range(0, number, 2):
            keys, values = [], []
            for j in (two, two + 1):
                valid = here + j < high
                pick = picks_ref[tile, jnp.where(valid, here + j, here) if checked else here + j]
                holder = pick // MOST
                block = pick % MOST
                key = memory_ref[holder, block]
                keys.append(jnp.where(valid, key, jnp.zeros_like(key)) if checked and j else key)
                values.append(memory_ref[holder, blocks + block])
            sides.append((jnp.concatenate(keys, axis=0), jnp.concatenate(values, axis=0)))

        def products(side):
            keys, values = side
            scores = lax.dot_general(query_ref[:count, :], keys, NT, preferred_element_type=jnp.float32)
            grad_probs = lax.dot_general(query_ref[count:2 * count, :], values, NT, preferred_element_type=jnp.float32)
            return scores, grad_probs

        ahead = products(sides[0])
        gained = None
        for at, (keys, _) in enumerate(sides):
            scores, grad_probs = ahead
            if at + 1 < len(sides):
                ahead = products(sides[at + 1])
            log_wide = jnp.concatenate([log_ref[...]] * 2, axis=1)
            delta_wide = jnp.concatenate([delta_ref[...]] * 2, axis=1)
            probs = jnp.exp2(scores * exponent - log_wide)
            grad_scores = (probs * (grad_probs - delta_wide)).astype(jnp.bfloat16)
            part = jnp.dot(grad_scores, keys, preferred_element_type=jnp.float32)
            gained = part if gained is None else gained + part
        total[...] += gained

    for number in STEPS:
        full = (high - low) // number

        def many(turn, carry, low=low, number=number):
            add(low + number * turn, number, False)
            return carry

        lax.fori_loop(0, full, many, 0)
        low = low + number * full

    def few(turn, carry):
        add(low + 2 * turn, 2, True)
        return carry

    lax.fori_loop(0, (high - low + 1) // 2, few, 0)

    if not last:
        out_refs[0][0] = total[...]
        return
    for x, out_ref in enumerate(out_refs):

        @pl.when(step == x)
        def _(out_ref=out_ref):
            for h in range(heads):
                out_ref[:, h * dim:(h + 1) * dim] = total[h * rows:(h + 1) * rows, :].astype(jnp.bfloat16)


def attend(packed, memory, acc, picks, starts, heads, dim, scale, last, first=0):
    tiles = len(packed)
    span = packed[0].shape[0]
    rows = span // (2 * heads) - PARTS
    fresh = acc is None
    width = heads * rows
    holders = memory.shape[0]
    memory = memory.reshape(holders, -1, BLOCK, dim)
    acc_spec = pl.BlockSpec((1, width, dim), lambda t, *_: (first + t, 0, 0))
    if last:
        out_shape = [jax.ShapeDtypeStruct((rows, heads * dim), jnp.bfloat16)] * tiles
        out_spec = [pl.BlockSpec((rows, heads * dim), lambda t, *_: (0, 0))] * tiles
    else:
        out_shape = jax.ShapeDtypeStruct((tiles, width, dim), jnp.float32)
        out_spec = acc_spec
    flops = tiles * holders * memory.shape[1] * (BLOCK // 4) * width * dim * 6
    return pl.pallas_call(
        functools.partial(attend_kernel, heads, dim, rows, scale, first, tiles, fresh, last),
        out_shape=out_shape,
        grid_spec=pltpu.PrefetchScalarGridSpec(
            num_scalar_prefetch=2,
            grid=(tiles,),
            in_specs=[pl.BlockSpec((span, dim), lambda t, *_: (0, 0))] * tiles
            + [pl.BlockSpec(memory.shape, lambda t, *_: (0, 0, 0, 0))]
            + ([] if fresh else [acc_spec]),
            out_specs=out_spec,
            scratch_shapes=[pltpu.VMEM((span, dim), jnp.bfloat16)] + [pltpu.VMEM((width, dim), jnp.float32)] * 3,
        ),
        compiler_params=pltpu.CompilerParams(vmem_limit_bytes=VMEM_MOST),
        cost_estimate=pl.CostEstimate(flops=flops * 4, bytes_accessed=0, transcendentals=0),
    )(picks, starts, *packed, memory, *([] if fresh else [acc]))


def assemble_kernel(own, group, at_ref, *refs):
    pieces, out_ref = refs[:-1], refs[-1]
    span = pieces[0].shape[1]
    for index in range(own):
        for x in range(group):
            column = pl.multiple_of(((at_ref[0] ^ x) * own + index) * span, span)
            out_ref[:, pl.ds(column, span)] = pieces[index * group + x][...]


def assemble(pieces, at, own, group):
    rows, span = pieces[0].shape
    width = own * group * span
    part = rows // 4
    return pl.pallas_call(
        functools.partial(assemble_kernel, own, group),
        out_shape=jax.ShapeDtypeStruct((rows, width), pieces[0].dtype),
        grid_spec=pltpu.PrefetchScalarGridSpec(
            num_scalar_prefetch=1,
            grid=(rows // part,),
            in_specs=[pl.BlockSpec((part, span), lambda i, _: (i, 0))] * len(pieces),
            out_specs=pl.BlockSpec((part, width), lambda i, _: (i, 0)),
        ),
        compiler_params=pltpu.CompilerParams(vmem_limit_bytes=VMEM_MOST),
        cost_estimate=pl.CostEstimate(flops=0, bytes_accessed=4 * rows * width, transcendentals=0),
    )(at[None], *pieces)


def after(value, *others):
    anywhere = pl.BlockSpec(memory_space=pl.ANY)
    corners = [
        pl.BlockSpec((1,) * (other.ndim - 2) + (HINT, 128), lambda i, count=other.ndim: (0,) * count) for other in others
    ]
    return pl.pallas_call(
        lambda *refs: None,
        out_shape=jax.ShapeDtypeStruct(value.shape, value.dtype),
        grid=(1,),
        in_specs=[anywhere] + corners,
        out_specs=anywhere,
        input_output_aliases={0: 0},
        cost_estimate=pl.CostEstimate(flops=0, bytes_accessed=0, transcendentals=0),
    )(value, *others)


def shards(grad_out, queries, mem_out, row_total, gate_logit, mem_keys, mem_values, retrieved):
    seq = lax.axis_size("seq")
    sections = lax.axis_size("section")
    position = lax.axis_index("seq")
    rows, width = grad_out.shape[1:]
    head_count = gate_logit.shape[1]
    dim = width // head_count
    kv_heads = mem_keys.shape[2] // dim
    heads = head_count // kv_heads
    mem_dev = mem_keys.shape[1]
    blocks = mem_dev // BLOCK
    group = min(kv_heads, seq // 2)
    own = kv_heads // group
    at = position % group
    home = position // group
    scale = dim ** (-0.5)

    def swapped(value, step):
        return lax.ppermute(value, "seq", [(p, p ^ step) for p in range(seq)])

    def delivered(value, step):
        pairs = [(s * seq + p, ((s - 1) % sections) * seq + (p ^ step)) for s in range(sections) for p in range(seq)]
        return lax.ppermute(value, ("section", "seq"), pairs)

    cut = (5 * blocks + 7) // 8
    cuts = [[(0, blocks)]] * (own - 1) + [[(0, cut), (cut, blocks)]]

    moved = own > 1
    chosen = retrieved[0]
    if moved:
        of_all = lax.all_gather(chosen, "section")
        chosen = lax.dynamic_index_in_dim(of_all, (lax.axis_index("section") + 1) % sections, 0, keepdims=False)

    def listed(i):
        source = chosen if i == own - 1 else retrieved[0]
        mine = lax.dynamic_index_in_dim(source, at * own + i, 0, keepdims=False)
        mine = jnp.stack(
            [lax.dynamic_index_in_dim(mine, home * group + (at ^ x), 0, keepdims=False) for x in range(group)]
        )
        holder, block = mine // blocks, mine % blocks
        piece = sum((block >= low).astype(jnp.int32) for low, _ in cuts[i][1:]) if len(cuts[i]) > 1 else 0 * block
        key = piece * seq * blocks + mine
        rank = jnp.sum(key[:, None, :] < key[:, :, None], axis=-1)
        order = jnp.arange(mine.shape[-1])
        low = sum((piece == j) * cuts[i][j][0] for j in range(len(cuts[i])))
        value = holder * MOST + block - low
        picks = jnp.sum(jnp.where(rank[:, :, None] == order, value[:, :, None], 0), axis=1).astype(jnp.int32)
        bounds = [jnp.sum(piece < j, axis=-1) for j in range(len(cuts[i]) + 1)]
        return picks, [
            jnp.stack([bounds[j], bounds[j + 1]], axis=1).astype(jnp.int32) for j in range(len(cuts[i]))
        ]

    gates = jax.nn.sigmoid(gate_logit[0])
    gathered, worked, latest, held = [], [], None, []

    def memory_of(i, sources):
        return pack(sources, seq, own, group, dim, i, cuts[i])

    def queries_of(i):
        return prepare(grad_out[0], queries[0], mem_out[0], row_total[0], gates, at, kv_heads, dim, scale, own, i)

    def exchanged(packed):
        return [packed[0]] + [swapped(packed[x], x) for x in range(1, group)]

    memories = memory_of(0, [mem_keys[0], mem_values[0]])
    asked = [queries_of(i) for i in range(own)]
    for i in range(1, own):
        rows_of = narrow(mem_keys[0], mem_values[0], after(at[None], asked[i][0]), own, group, dim, i)
        memories += memory_of(i, [delivered(rows_of, 0) if i == own - 1 else rows_of])
    coming = exchanged(asked[0])
    for i in range(own):
        packed = coming
        pieces = []
        for _ in cuts[i]:
            piece = memories.pop(0)
            piece = piece if latest is None else after(piece, latest, *held)
            latest = lax.all_to_all(piece, "seq", split_axis=0, concat_axis=0, tiled=True)
            pieces.append(latest)
            held = packed
        picks, starts = listed(i)
        run = functools.partial(attend, picks=picks, heads=heads, dim=dim, scale=scale)
        acc = None
        for j in range(len(pieces) - 1):
            acc = run(packed, pieces[j], acc, starts=after(starts[j], *worked), last=False)
            worked = [acc]
        if i < own - 1:
            if i == own - 2:
                coming = [delivered(value, x) for x, value in enumerate(asked[i + 1])]
            else:
                coming = exchanged(asked[i + 1])
            done = run(packed, pieces[-1], acc, starts=after(starts[-1], *worked, memories[0]), last=True)
            worked = done[:1]
            gathered += [delivered(done[x], x) for x in range(group)]
            continue
        results, half = [None] * group, group // 2
        for low, high in ((half, group), (0, half)):
            bounds = after(starts[-1], *worked, *(gathered if low else []))
            done = run(packed[low:high], pieces[-1], acc, starts=bounds, last=True, first=low)
            worked = done[:1]
            for x in range(low, high):
                result = done[x - low]
                if not moved:
                    results[x] = delivered(result if low else after(result, results[x + half]), x)
                elif x:
                    results[x] = swapped(result if low else after(result, *results[half:]), x)
                else:
                    results[x] = result
    return assemble(gathered + results, at, own, group)[None]


def solution(mesh):
    return jax.shard_map(
        shards,
        mesh=mesh,
        in_specs=(
            P("section", "seq", None),
            P("section", "seq", None),
            P("section", "seq", None),
            P("section", "seq", None),
            P("section", None),
            P("section", "seq", None),
            P("section", "seq", None),
            P("section", None, None, None),
        ),
        out_specs=P("section", "seq", None),
        check_vma=False,
    )
```
